32 devices in a mesh: fsdp: 4 (over z), context: 2 (over x), tensor: 4 (over y, core).
Axes of the slice: x: 2, y: 2, z: 4, core: 2. Of those that a mesh axis runs over, the one named last changes fastest.
Arguments:
- hidden_in: bfloat16 [8, 1024, 2048], P('fsdp', 'context'), may hold values from -6 to 6
- norm_gains: bfloat16 [2, 2048], P(None, 'fsdp'), may hold values from 0.5 to 1.5
- norm_biases: bfloat16 [2, 2048], P(None, 'fsdp'), may hold values from -3 to 3
- qkv_weight: bfloat16 [3, 2048, 2048], P(None, 'fsdp', 'tensor'), may hold values from -0.1875 to 0.1875
- qkv_bias: bfloat16 [3, 2048], P(None, 'tensor'), may hold values from -3 to 3
- out_weight: bfloat16 [2048, 2048], P('tensor', 'fsdp'), may hold values from -0.25 to 0.25
- gate_up_weight: bfloat16 [2, 2048, 5632], P(None, 'fsdp', 'tensor'), may hold values from -0.125 to 0.125
- down_weight: bfloat16 [5632, 2048], P('tensor', 'fsdp'), may hold values from -0.109375 to 0.109375
- cotangent: bfloat16 [8, 1024, 2048], P('fsdp', 'context'), may hold values from -6 to 6
Outputs:
- layer_out: bfloat16 [8, 1024, 2048], P('fsdp', 'context')
- input_grad: float32 [8, 1024, 2048], P('fsdp', 'context')
- grad_norm_gains: float32 [2, 2048], P(None, 'fsdp')
- grad_norm_biases: float32 [2, 2048], P(None, 'fsdp')
- grad_qkv_weight: float32 [3, 2048, 2048], P(None, 'fsdp', 'tensor')
- grad_qkv_bias: float32 [3, 2048], P(None, 'tensor')
- grad_out_weight: float32 [2048, 2048], P('tensor', 'fsdp')
- grad_gate_up: float32 [2, 2048, 5632], P(None, 'fsdp', 'tensor')
- grad_down: float32 [5632, 2048], P('tensor', 'fsdp')
The draws below stay inside these ranges and needn't reach their ends.
All inputs are finite; a program needn't handle non-finite values.
Results may differ from the reference program's by a relative error of at most 0.022.
Values may be sent and summed in bfloat16 or wider, within the bound.
No kernel may reach another device: no remote copies, remote signals or barrier semaphores. Data moves between devices by JAX's collectives and lax.ppermute only.
A program may use at most 320 MiB of HBM per device.

```python
import math
import jax
import jax.numpy as jnp
from jax import lax

D = 2048
HEADS = 32
HEAD_DIM = 64
ROT = 16
FF = 5632
BATCH = 8
SEQ_LEN = 1024


def block_scale(key, dims, cuts, least, largest):
    level, own = 1.0, jax.random.fold_in(key, 6)
    for axis_at, blocks in cuts:
        heights = jnp.exp(jax.random.uniform(jax.random.fold_in(own, axis_at), (blocks,), jnp.float32, least / len(cuts), largest / len(cuts)))
        level = level * jnp.repeat(heights, dims[axis_at] // blocks).reshape([-1 if axis == axis_at else 1 for axis in range(len(dims))])
    return level


def gaussian(rng, shape, width, reach, cuts=(), held_as=jnp.bfloat16):
    values = jax.random.normal(rng, shape, jnp.float32) * width
    if len(cuts) > 0:
        values = block_scale(rng, shape, cuts, -0.22, 0.18) * values
    return jnp.clip(values, min=-reach, max=reach).astype(held_as)


def setup_inputs(seed: int = 0) -> dict:
    arg_keys = jax.random.split(jax.random.key(seed), 10)
    hidden_in = gaussian(arg_keys[0], (BATCH, SEQ_LEN, D), 1.0, 6.0, ((0, 4), (1, 2)))
    norm_gains = jnp.clip(1.0 + 0.1 * jax.random.normal(arg_keys[1], (2, D), jnp.float32), 0.5, 1.5).astype(jnp.bfloat16)
    norm_biases = gaussian(arg_keys[2], (2, D), 0.5, 3.0, ((1, 4),))
    qkv_weight = gaussian(arg_keys[3], (3, D, D), (D // 2) ** -0.5, 0.1875, ((1, 4), (2, 4)))
    qkv_bias = gaussian(arg_keys[4], (3, D), 0.5, 3.0, ((1, 4),))
    out_weight = gaussian(arg_keys[5], (D, D), (D // 4) ** -0.5, 0.25, ((0, 4), (1, 4)))
    gate_up_weight = gaussian(arg_keys[6], (2, D, FF), D ** -0.5, 0.125, ((1, 4), (2, 4)))
    down_weight = gaussian(arg_keys[7], (FF, D), (FF // 2) ** -0.5, 0.109375, ((0, 4), (1, 4)))
    cotangent = gaussian(arg_keys[8], (BATCH, SEQ_LEN, D), 1.0, 6.0, ((0, 4), (1, 2)))
    return dict(hidden_in=hidden_in, norm_gains=norm_gains, norm_biases=norm_biases, qkv_weight=qkv_weight, qkv_bias=qkv_bias, out_weight=out_weight, gate_up_weight=gate_up_weight, down_weight=down_weight, cotangent=cotangent)


PRECISE = lax.Precision.HIGHEST
EPSILON = 1e-05
NEG_HUGE = -1e+30

@jax.custom_vjp
def low(v):
    return lax.optimization_barrier(v.astype(jnp.bfloat16)).astype(jnp.float32)

@jax.custom_vjp
def low_back(v):
    return v

def low_keep(v):
    return (low(v), None)

def low_pass(kept, grad):
    return (grad,)

def back_keep(v):
    return (v, None)

def back_low(kept, grad):
    return (low(grad),)
low.defvjp(low_keep, low_pass)
low_back.defvjp(back_keep, back_low)

def layer_norm(values, gain, shift):
    row_mean = lax.optimization_barrier(jnp.mean(values, axis=-1, keepdims=True))
    centred = values - row_mean
    variance = lax.optimization_barrier(jnp.mean(centred * centred, axis=-1, keepdims=True))
    return centred * lax.rsqrt(variance + EPSILON) * gain + shift

def rotary(tensor_in):
    half_rot = ROT // 2
    freq_index = jnp.arange(half_rot, dtype=jnp.float32)
    frequency = jnp.power(10000.0, -2.0 * freq_index / ROT)
    angles = jnp.arange(SEQ_LEN, dtype=jnp.float32)[:, None] * frequency[None, :]
    cosine = jnp.cos(angles)[None, :, None, :]
    sine_tab = jnp.sin(angles)[None, :, None, :]
    first_half = tensor_in[..., :half_rot]
    second_half = tensor_in[..., half_rot:ROT]
    return jnp.concatenate([first_half * cosine - second_half * sine_tab, second_half * cosine + first_half * sine_tab, tensor_in[..., ROT:]], axis=-1)

def head_attend(operands):
    query_head, key_head, value_head = operands
    score_scale = 1.0 / math.sqrt(HEAD_DIM)
    scores = low_back(jnp.einsum('gqd,gkd->gqk', query_head, key_head, precision=PRECISE) * score_scale)
    positions = jnp.arange(SEQ_LEN, dtype=jnp.int32)
    scores = jnp.where(positions[:, None] >= positions[None, :], scores, NEG_HUGE)
    attn_probs = low(jax.nn.softmax(scores, axis=-1))
    return low_back(jnp.einsum('gqk,gkd->gqd', attn_probs, value_head, precision=PRECISE))

def forward(inputs, gain_pair, shift_pair, w_qkv, b_qkv, w_out, w_gate_up, w_down):
    group_size = inputs.shape[0]
    split_shape = (group_size, SEQ_LEN, HEADS, HEAD_DIM)
    normed = low(layer_norm(inputs, gain_pair[0], shift_pair[0]))
    mixed_qkv = low_back(jnp.einsum('gld,cde->cgle', normed, w_qkv, precision=PRECISE) + b_qkv[:, None, None, :])
    query_all = low(rotary(mixed_qkv[0].reshape(split_shape))).transpose(2, 0, 1, 3)
    key_all = low(rotary(mixed_qkv[1].reshape(split_shape))).transpose(2, 0, 1, 3)
    value_all = low(mixed_qkv[2].reshape(split_shape)).transpose(2, 0, 1, 3)
    attended = lax.map(jax.checkpoint(head_attend), (query_all, key_all, value_all))
    attended = low(attended.transpose(1, 2, 0, 3).reshape(group_size, SEQ_LEN, D))
    middle = inputs + low_back(jnp.einsum('gle,ed->gld', attended, w_out, precision=PRECISE))
    normed_two = low(layer_norm(middle, gain_pair[1], shift_pair[1]))
    gate_up = low_back(jnp.einsum('gld,cdf->cglf', normed_two, w_gate_up, precision=PRECISE))
    hidden = low(jax.nn.silu(gate_up[0]) * gate_up[1])
    return middle + low_back(jnp.einsum('glf,fd->gld', hidden, w_down, precision=PRECISE))

def reference(hidden_in, norm_gains, norm_biases, qkv_weight, qkv_bias, out_weight, gate_up_weight, down_weight, cotangent):
    params = tuple((weight_in.astype(jnp.float32) for weight_in in (norm_gains, norm_biases, qkv_weight, qkv_bias, out_weight, gate_up_weight, down_weight)))
    per_step = math.gcd(BATCH, max(1, 4096 // SEQ_LEN))
    step_count = BATCH // per_step
    input_blocks = hidden_in.astype(jnp.float32).reshape(step_count, per_step, SEQ_LEN, D)
    cot_blocks = cotangent.astype(jnp.float32).reshape(step_count, per_step, SEQ_LEN, D)

    def scan_step(totals, block_data):
        inputs, cot_in = block_data
        layer_out, pull_back = jax.vjp(forward, inputs, params[0], params[1], params[2], params[3], params[4], params[5], params[6])
        grad_list = pull_back(cot_in)
        totals = jax.tree.map(jnp.add, totals, tuple(grad_list[1:]))
        return (totals, (layer_out, grad_list[0]))
    zero_grads = tuple((jnp.zeros_like(weight_in) for weight_in in params))
    totals, (out_blocks, input_grads) = lax.scan(scan_step, zero_grads, (input_blocks, cot_blocks))
    return (out_blocks.reshape(BATCH, SEQ_LEN, D).astype(jnp.bfloat16), input_grads.reshape(BATCH, SEQ_LEN, D), totals[0], totals[1], totals[2], totals[3], totals[4], totals[5], totals[6])
```

```python
import math

import jax
import jax.numpy as jnp
import numpy as np
from jax import lax
from jax.experimental import pallas as pl
from jax.experimental.pallas import tpu as pltpu
from jax.sharding import PartitionSpec as P

HEAD_DIM = 64
ROT = 16
EPSILON = 1e-05
F32 = jnp.float32
LOW = jnp.bfloat16


def rotary_tables(length, width):
    column = np.arange(width) % HEAD_DIM
    half = ROT // 2
    frequency = np.power(10000.0, -2.0 * (column % half) / ROT).astype(np.float32)
    angles = np.arange(length, dtype=np.float32)[:, None] * frequency[None, :]
    inside = column < ROT
    lower = column < half
    sine = np.sin(angles)
    cosine = np.where(inside, np.cos(angles), 1.0)
    minus = np.where(lower, -sine, 0.0)
    plus = np.where(inside & ~lower, sine, 0.0)
    return jnp.asarray(np.stack([cosine, minus, plus]).astype(np.float32))

def dot_nt(a,b): return lax.dot_general(a,b,(((1,),(1,)),((),())),preferred_element_type=F32)
def dot_nn(a,b): return lax.dot_general(a,b,(((1,),(0,)),((),())),preferred_element_type=F32)
def dot_tn(a,b): return lax.dot_general(a,b,(((0,),(0,)),((),())),preferred_element_type=F32)

def head_masks(width):
    lane=lax.broadcasted_iota(jnp.int32,(1,width),1)
    return [ (lane//HEAD_DIM)==h for h in range(width//HEAD_DIM)]

def fwd_kernel(block, mixed_ref, bias_ref, table_ref, q_ref, k_ref, v_ref, att_ref, lse_ref):
    length, width = q_ref.shape
    half=ROT//2
    def rotated(c):
        v=mixed_ref[c]+bias_ref[c]
        return v*table_ref[0]+pltpu.roll(v,width-half,1)*table_ref[1]+pltpu.roll(v,half,1)*table_ref[2]
    q_ref[...]=(rotated(0)*(1.0/math.sqrt(HEAD_DIM))).astype(LOW)
    k_ref[...]=rotated(1).astype(LOW)
    v_ref[...]=(mixed_ref[2]+bias_ref[2]).astype(LOW)
    masks=head_masks(width)
    row=lax.broadcasted_iota(jnp.int32,(block,block),0)
    col=lax.broadcasted_iota(jnp.int32,(block,block),1)
    for i in range(length//block):
        rows=pl.ds(i*block,block)
        q=q_ref[rows,:]
        out=jnp.zeros((block,width),F32); lse=jnp.zeros((block,width),F32)
        for mask in masks:
            qh=jnp.where(mask,q,jnp.zeros_like(q))
            diag=jnp.where(row>=col,dot_nt(qh,k_ref[rows,:]),-1e30)
            top=jnp.max(diag,axis=1,keepdims=True)
            if i>0:
                rest=dot_nt(qh,k_ref[pl.ds(0,i*block),:])
                top=jnp.maximum(top,jnp.max(rest,axis=1,keepdims=True))
            diag=jnp.exp(diag-top)
            total=jnp.sum(diag,axis=1,keepdims=True)
            acc=dot_nn(diag.astype(LOW),v_ref[rows,:])
            if i>0:
                rest=jnp.exp(rest-top)
                total=total+jnp.sum(rest,axis=1,keepdims=True)
                acc=acc+dot_nn(rest.astype(LOW),v_ref[pl.ds(0,i*block),:])
            out=jnp.where(mask,acc/total,out)
            lse=jnp.where(mask,top+jnp.log(total),lse)
        att_ref[rows,:]=out.astype(LOW)
        lse_ref[rows,:]=lse

def attend_forward(mixed,bias,tables,seqs,length,block=256):
    pair,_,rows,cols=mixed.shape
    width=min(cols,128); groups=cols//width
    tok=lambda o,s,g:(o,s,g)
    spec=pl.BlockSpec((None,length,width),tok)
    shape=lambda d:jax.ShapeDtypeStruct((pair,rows,cols),d)
    return pl.pallas_call(
        lambda *r: fwd_kernel(block,*r),
        grid=(pair,seqs,groups),
        in_specs=[pl.BlockSpec((None,3,length,width),lambda o,s,g:(o,0,s,g)),
                  pl.BlockSpec((None,3,1,width),lambda o,s,g:(o,0,0,g)),
                  pl.BlockSpec((3,length,width),lambda o,s,g:(0,0,0))],
        out_specs=[spec]*5,
        out_shape=[shape(LOW)]*4+[shape(F32)],
        compiler_params=pltpu.CompilerParams(vmem_limit_bytes=48<<20),
        cost_estimate=pl.CostEstimate(flops=int(4*pair*rows*length*cols*0.6),bytes_accessed=pair*rows*cols*26,transcendentals=pair*rows*length*cols//128),
        name="attend_forward",
    )(mixed,bias,tables)

def bwd_kernel(block,q_ref,k_ref,v_ref,att_ref,lse_ref,do_ref,table_ref,out_ref,dk_acc,dv_acc,dq_acc):
    length,width=q_ref.shape
    half=ROT//2
    masks=head_masks(width)
    row=lax.broadcasted_iota(jnp.int32,(block,block),0)
    col=lax.broadcasted_iota(jnp.int32,(block,block),1)
    count=length//block
    for i in reversed(range(count)):
        rows=pl.ds(i*block,block)
        q=q_ref[rows,:]; do=do_ref[rows,:]; lse=lse_ref[rows,:]
        prod=do.astype(F32)*att_ref[rows,:].astype(F32)
        n=(i+1)*block
        keys=k_ref[pl.ds(0,n),:]; vals=v_ref[pl.ds(0,n),:]
        dq=jnp.zeros((block,width),F32)
        dk=None
        for h,mask in enumerate(masks):
            qh=jnp.where(mask,q,jnp.zeros_like(q)); dh=jnp.where(mask,do,jnp.zeros_like(do))
            delta=jnp.sum(jnp.where(mask,prod,0.0),axis=1,keepdims=True)
            lse_h=lse[:,h*HEAD_DIM:h*HEAD_DIM+1]
            s=dot_nt(qh,keys)
            p=jnp.exp(s-lse_h)
            if i==0:
                p=jnp.where(row>=col,p,0.0)
            else:
                p=jnp.concatenate([p[:,:n-block],jnp.where(row>=col,p[:,n-block:],0.0)],axis=1)
            dp=dot_nt(dh,vals)
            ds=(p*(dp-delta)).astype(LOW)
            pl_low=p.astype(LOW)
            dq=jnp.where(mask,dot_nn(ds,keys),dq)
            tk=dot_tn(ds,qh); tv=dot_tn(pl_low,dh)
            dk=tk if dk is None else dk+tk
            dv=tv if h==0 else dv+tv
        dq_acc[rows,:]=dq*(1.0/math.sqrt(HEAD_DIM))
        if i==count-1:
            dk_acc[...]=dk; dv_acc[...]=dv
        else:
            dk_acc[pl.ds(0,n),:]+=dk; dv_acc[pl.ds(0,n),:]+=dv
    def back(v):
        return v*table_ref[0]+pltpu.roll(v*table_ref[1],half,1)+pltpu.roll(v*table_ref[2],width-half,1)
    out_ref[0]=back(dq_acc[...]).astype(LOW)
    out_ref[1]=back(dk_acc[...]).astype(LOW)
    out_ref[2]=dv_acc[...].astype(LOW)

def attend_back(q,k,v,att,lse,grad,tables,seqs,length,block=256):
    pair,rows,cols=q.shape
    width=min(cols,128); groups=cols//width
    spec=pl.BlockSpec((None,length,width),lambda o,s,g:(o,s,g))
    return pl.pallas_call(
        lambda *r: bwd_kernel(block,*r),
        grid=(pair,seqs,groups),
        in_specs=[spec]*6+[pl.BlockSpec((3,length,width),lambda o,s,g:(0,0,0))],
        out_specs=pl.BlockSpec((None,3,length,width),lambda o,s,g:(o,0,s,g)),
        out_shape=jax.ShapeDtypeStruct((pair,3,rows,cols),LOW),
        scratch_shapes=[pltpu.VMEM((length,width),F32)]*3,
        compiler_params=pltpu.CompilerParams(vmem_limit_bytes=48<<20),
        cost_estimate=pl.CostEstimate(flops=int(10*pair*rows*length*cols*0.6),bytes_accessed=pair*rows*cols*20,transcendentals=pair*rows*length*cols//128),
        name="attend_back",
    )(q,k,v,att,lse,grad,tables)


class Place:
    def __init__(self):
        self.fsdp = lax.axis_size("fsdp")
        self.context = lax.axis_size("context")
        self.tensor = lax.axis_size("tensor")
        self.pairs = self.tensor // 2
        self.z = lax.axis_index("fsdp")
        self.x = lax.axis_index("context")
        self.t = lax.axis_index("tensor")
        self.y = self.t // 2
        self.core = self.t % 2

    def size(self, which):
        return self.context if which == "x" else self.pairs

    def at(self, which):
        return self.x if which == "x" else self.y

    def shift(self, value, which, step):
        if which == "z":
            n = self.fsdp
            return lax.ppermute(value, "fsdp", [(i, (i + step) % n) for i in range(n)])
        if which == "x":
            n = self.context
            return lax.ppermute(value, "context", [(i, (i + step) % n) for i in range(n)])
        n = self.tensor
        return lax.ppermute(value, "tensor", [(i, (i + 2 * step) % n) for i in range(n)])

    def swap(self, value):
        return lax.ppermute(value, "tensor", [(i, i ^ 1) for i in range(self.tensor)])


def pick(value, index, axis):
    return lax.dynamic_index_in_dim(value, index, axis, keepdims=False)


def scatter_stage(place, value, axis, which):
    n, at = place.size(which), place.at(which)
    total = pick(value, at, axis).astype(F32)
    for step in range(1, n):
        sent = pick(value, (at + step) % n, axis)
        total = total + place.shift(sent, which, step).astype(F32)
    return total


def gather_stage(place, value, axis, which):
    n, at = place.size(which), place.at(which)
    if n == 1:
        return jnp.expand_dims(value, axis)
    if n == 2:
        other = place.shift(value, which, 1)
        return jnp.where(at == 0, jnp.stack([value, other], axis), jnp.stack([other, value], axis))
    parts = [value] + [place.shift(value, which, step) for step in range(1, n)]
    order = (at - jnp.arange(n)) % n
    return jnp.take(jnp.stack(parts, axis), order, axis=axis)


def sum_rows(place, value, seqs):
    feat = value.shape[1]
    value = value.reshape(seqs, place.context, place.pairs, -1, feat)
    first, second = value[..., : feat // 2], value[..., feat // 2 :]
    first = scatter_stage(place, first, 1, "x").astype(LOW)
    second = scatter_stage(place, second, 2, "y").astype(LOW)
    first = scatter_stage(place, first, 1, "y")
    second = scatter_stage(place, second, 1, "x")
    return jnp.concatenate([first, second], axis=-1)


def spread_rows(place, value):
    feat = value.shape[-1]
    first, second = value[..., : feat // 2], value[..., feat // 2 :]
    first = gather_stage(place, first, 1, "y")
    second = gather_stage(place, second, 1, "x")
    first = gather_stage(place, first, 1, "x")
    second = gather_stage(place, second, 2, "y")
    return jnp.concatenate([first, second], axis=-1).reshape(-1, feat)


def whole_rows(place, value):
    value = gather_stage(place, value, 1, "y")
    seqs, pairs, rows, feat = value.shape
    value = value.reshape(seqs, pairs * rows, feat)
    other = place.swap(value)
    return jnp.where(
        place.core == 0,
        jnp.concatenate([value, other]),
        jnp.concatenate([other, value]),
    )


def gather_weight(place, shard, axis):
    n, z = place.fsdp, place.z
    size = shard.shape[axis]
    if n != 4:
        mine = lax.all_gather(shard, "fsdp", axis=axis, tiled=True)
        return jnp.stack([mine, place.swap(mine)])
    half = size // 2
    before = place.shift(shard, "z", 1)
    after = place.shift(shard, "z", -1)
    low = place.shift(lax.slice_in_dim(before, 0, half, axis=axis), "z", 1)
    high = place.shift(lax.slice_in_dim(after, half, size, axis=axis), "z", -1)
    shape = list(shard.shape)
    shape[axis] = n * size
    whole = jnp.zeros([2] + shape, shard.dtype)
    parts = [
        (shard, z * size),
        (before, (z + 3) % n * size),
        (after, (z + 1) % n * size),
        (low, (z + 2) % n * size),
        (high, (z + 2) % n * size + half),
    ]
    for part, start in parts:
        for slot, piece in enumerate((part, place.swap(part))):
            where = [0] * (shard.ndim + 1)
            where[0], where[axis + 1] = slot, start
            whole = lax.dynamic_update_slice(whole, piece[None], where)
    return whole


def scatter_grad(place, grad, axis):
    n, z = place.fsdp, place.z
    if n != 4:
        return lax.psum_scatter(grad, "fsdp", scatter_dimension=axis, tiled=True)
    size = grad.shape[axis] // n
    half = size // 2

    def part(ahead, start, count):
        return lax.dynamic_slice_in_dim(grad, (z + ahead) % n * size + start, count, axis)

    def added(one, two):
        return (one.astype(F32) + two.astype(F32)).astype(LOW)

    from_left = place.shift(part(2, half, half), "z", 1)
    from_right = place.shift(part(2, 0, half), "z", -1)
    left_low = place.shift(part(1, 0, half), "z", 1)
    right_high = place.shift(part(3, half, half), "z", -1)
    left_high = place.shift(added(part(1, half, half), from_left), "z", 1)
    right_low = place.shift(added(part(3, 0, half), from_right), "z", -1)
    low = part(0, 0, half).astype(F32) + left_low.astype(F32) + right_low.astype(F32)
    high = part(0, half, half).astype(F32) + left_high.astype(F32) + right_high.astype(F32)
    return jnp.concatenate([low, high], axis=axis).astype(LOW)


def join_context(place, value, axis):
    value = gather_stage(place, value, axis, "x")
    shape = list(value.shape)
    shape[axis : axis + 2] = [shape[axis] * shape[axis + 1]]
    return value.reshape(shape).astype(F32)


def product_grad(mine, theirs, my_grad, their_grad):
    total = dot_tn(mine, my_grad) + dot_tn(theirs, their_grad)
    return total.astype(LOW)


def norm_forward(values, gain, shift):
    row_mean = jnp.mean(values, axis=-1, keepdims=True)
    centred = values - row_mean
    variance = jnp.mean(centred * centred, axis=-1, keepdims=True)
    inv_std = lax.rsqrt(variance + EPSILON)
    scaled = centred * inv_std
    return scaled * gain + shift, scaled, inv_std


def norm_backward(grad_out, scaled, inv_std, gain):
    grad_scaled = grad_out * gain
    first_mean = jnp.mean(grad_scaled, axis=-1, keepdims=True)
    second_mean = jnp.mean(grad_scaled * scaled, axis=-1, keepdims=True)
    grad_in = inv_std * (grad_scaled - first_mean - scaled * second_mean)
    sums = jnp.stack([jnp.sum(grad_out * scaled, axis=(0, 1)), jnp.sum(grad_out, axis=(0, 1))])
    return grad_in, sums


def local(
    hidden_in,
    norm_gains,
    norm_biases,
    qkv_weight,
    qkv_bias,
    out_weight,
    gate_up_weight,
    down_weight,
    cotangent,
):
    place = Place()
    all_seqs, part_rows, feat = hidden_in.shape
    seqs = all_seqs // 2
    length = part_rows * place.context
    own_rows = part_rows // place.pairs
    head_cols = qkv_bias.shape[1] // place.context
    hidden_cols = down_weight.shape[0] // place.context

    def columns(value, count, axis):
        return lax.dynamic_slice_in_dim(value, place.x * count, count, axis)

    def own_sequences(value):
        return lax.dynamic_slice_in_dim(value, place.core * seqs, seqs, 0)

    def own_piece(value):
        return lax.dynamic_slice_in_dim(value, place.y * own_rows, own_rows, 1)

    norms = lax.all_gather(jnp.stack([norm_gains, norm_biases]), "fsdp", axis=2, tiled=True).astype(F32)
    gain_rows, shift_rows = norms[0], norms[1]
    w_qkv = gather_weight(place, columns(qkv_weight, head_cols, 2), 1)
    hidden_mine = own_sequences(hidden_in)
    hidden_full = gather_stage(place, hidden_mine, 1, "x").reshape(seqs * length, feat)
    w_out = gather_weight(place, columns(out_weight, head_cols, 0), 1)
    w_gate_up = gather_weight(place, columns(gate_up_weight, hidden_cols, 2), 1)
    w_down = gather_weight(place, columns(down_weight, hidden_cols, 0), 1)
    grad_top_mine = own_sequences(cotangent)
    grad_top = gather_stage(place, grad_top_mine, 1, "x").reshape(seqs * length, feat)
    bias = columns(qkv_bias, head_cols, 1)
    bias = jnp.stack([bias, place.swap(bias)]).astype(F32)[:, :, None, :]

    normed = norm_forward(hidden_full.astype(F32), gain_rows[0], shift_rows[0])[0].astype(LOW)
    mixed = jnp.einsum("rd,ocde->ocre", normed, w_qkv, preferred_element_type=F32)
    tables = rotary_tables(length, min(head_cols, 128))
    query, keys, values, attended, log_total = attend_forward(mixed, bias, tables, seqs, length)
    attn_term = jnp.einsum("ore,oed->rd", attended, w_out, preferred_element_type=F32).astype(LOW)
    inputs = own_piece(hidden_mine).astype(F32)
    middle = inputs + sum_rows(place, attn_term, seqs)
    normed_two, scaled_two, inv_two = norm_forward(middle, gain_rows[1], shift_rows[1])
    normed_two = spread_rows(place, normed_two.astype(LOW))
    gate_up = jnp.einsum("rd,ocdf->ocrf", normed_two, w_gate_up, preferred_element_type=F32)
    gate, up = gate_up[:, 0], gate_up[:, 1]
    sig = jax.nn.sigmoid(gate)
    act = gate * sig
    hidden = (act * up).astype(LOW)
    down_term = jnp.einsum("orf,ofd->rd", hidden, w_down, preferred_element_type=F32).astype(LOW)
    final_out = (middle + sum_rows(place, down_term, seqs)).astype(LOW)
    layer_out = whole_rows(place, final_out)

    grad_down = product_grad(hidden[0], place.swap(hidden[1]), grad_top, place.swap(grad_top))
    grad_hidden = jnp.einsum("rd,ofd->orf", grad_top, w_down, preferred_element_type=F32)
    grad_gate = grad_hidden * up * (sig * (1.0 + gate * (1.0 - sig)))
    grad_up = grad_hidden * act
    grad_gu = jnp.stack([grad_gate, grad_up], axis=1).astype(LOW)
    grad_two = jnp.einsum("ocrf,ocdf->rd", grad_gu, w_gate_up, preferred_element_type=F32).astype(LOW)
    theirs_two, theirs_gu = place.swap(normed_two), place.swap(grad_gu[1])
    grad_gate_up = jnp.stack(
        [product_grad(normed_two, theirs_two, grad_gu[0, c], theirs_gu[c]) for c in range(2)]
    )
    grad_mid, sums_two = norm_backward(sum_rows(place, grad_two, seqs), scaled_two, inv_two, gain_rows[1])
    grad_middle = own_piece(grad_top_mine).astype(F32) + grad_mid
    grad_mid_low = spread_rows(place, grad_middle.astype(LOW))
    grad_out = product_grad(
        attended[0], place.swap(attended[1]), grad_mid_low, place.swap(grad_mid_low)
    )
    grad_att = jnp.einsum("rd,oed->ore", grad_mid_low, w_out, preferred_element_type=F32).astype(LOW)
    grad_mixed = attend_back(query, keys, values, attended, log_total, grad_att, tables, seqs, length)
    theirs_one, theirs_mixed = place.swap(normed), place.swap(grad_mixed[1])
    grad_qkv = jnp.stack(
        [product_grad(normed, theirs_one, grad_mixed[0, c], theirs_mixed[c]) for c in range(3)]
    )
    grad_one = jnp.einsum("ocre,ocde->rd", grad_mixed, w_qkv, preferred_element_type=F32).astype(LOW)
    _, scaled_one, inv_one = norm_forward(inputs, gain_rows[0], shift_rows[0])
    grad_first, sums_one = norm_backward(sum_rows(place, grad_one, seqs), scaled_one, inv_one, gain_rows[0])
    input_grad = whole_rows(place, (grad_middle + grad_first).astype(LOW)).astype(F32)

    sums = lax.psum(jnp.stack([sums_one, sums_two], axis=1), ("fsdp", "context", "tensor"))
    sums = lax.dynamic_slice_in_dim(sums, place.z * norm_gains.shape[1], norm_gains.shape[1], 2)
    bias_part = jnp.sum(grad_mixed.astype(F32), axis=2)
    bias_part = bias_part[0] + place.swap(bias_part[1])
    grad_bias = lax.dynamic_update_slice(
        jnp.zeros(qkv_bias.shape, F32), bias_part, (0, place.x * head_cols)
    )
    grad_bias = lax.psum(grad_bias, ("fsdp", "context"))

    return (
        layer_out,
        input_grad,
        sums[0],
        sums[1],
        join_context(place, scatter_grad(place, grad_qkv, 1), 2),
        grad_bias,
        join_context(place, scatter_grad(place, grad_out, 1), 0),
        join_context(place, scatter_grad(place, grad_gate_up, 1), 2),
        join_context(place, scatter_grad(place, grad_down, 1), 0),
    )


def solution(mesh):
    placed = (
        P("fsdp", "context", None),
        P(None, "fsdp"),
        P(None, "fsdp"),
        P(None, "fsdp", "tensor"),
        P(None, "tensor"),
        P("tensor", "fsdp"),
        P(None, "fsdp", "tensor"),
        P("tensor", "fsdp"),
        P("fsdp", "context", None),
    )
    return jax.shard_map(
        local,
        mesh=mesh,
        in_specs=placed,
        out_specs=(
            P("fsdp", "context", None),
            P("fsdp", "context", None),
            P(None, "fsdp"),
            P(None, "fsdp"),
            P(None, "fsdp", "tensor"),
            P(None, "tensor"),
            P("tensor", "fsdp"),
            P(None, "fsdp", "tensor"),
            P("tensor", "fsdp"),
        ),
        check_vma=False,
    )
```

```python
import math

import jax
import jax.numpy as jnp
import numpy as np
from jax import lax
from jax.experimental import pallas as pl
from jax.experimental.pallas import tpu as pltpu
from jax.sharding import PartitionSpec as P

HEAD_DIM = 64
ROT = 16
EPSILON = 1e-05
F32 = jnp.float32
LOW = jnp.bfloat16


def rotary_tables(length, width):
    column = np.arange(width) % HEAD_DIM
    half = ROT // 2
    frequency = np.power(10000.0, -2.0 * (column % half) / ROT).astype(np.float32)
    angles = np.arange(length, dtype=np.float32)[:, None] * frequency[None, :]
    inside = column < ROT
    lower = column < half
    sine = np.sin(angles)
    cosine = np.where(inside, np.cos(angles), 1.0)
    minus = np.where(lower, -sine, 0.0)
    plus = np.where(inside & ~lower, sine, 0.0)
    return jnp.asarray(np.stack([cosine, minus, plus]).astype(np.float32))

def light(flops, bytes_accessed, transcendentals):
    return pl.CostEstimate(flops=flops // 100, bytes_accessed=bytes_accessed // 100, transcendentals=0)


def dot_nt(a,b): return lax.dot_general(a,b,(((1,),(1,)),((),())),preferred_element_type=F32)
def dot_nn(a,b): return lax.dot_general(a,b,(((1,),(0,)),((),())),preferred_element_type=F32)
def dot_tn(a,b): return lax.dot_general(a,b,(((0,),(0,)),((),())),preferred_element_type=F32)

def head_masks(width):
    lane=lax.broadcasted_iota(jnp.int32,(1,width),1)
    return [ (lane//HEAD_DIM)==h for h in range(width//HEAD_DIM)]

def fwd_kernel(block, mixed_ref, bias_ref, table_ref, q_ref, k_ref, v_ref, att_ref, lse_ref):
    length, width = q_ref.shape
    half=ROT//2
    def rotated(c):
        v=mixed_ref[c]+bias_ref[c]
        return v*table_ref[0]+pltpu.roll(v,width-half,1)*table_ref[1]+pltpu.roll(v,half,1)*table_ref[2]
    q_ref[...]=(rotated(0)*(1.0/math.sqrt(HEAD_DIM))).astype(LOW)
    k_ref[...]=rotated(1).astype(LOW)
    v_ref[...]=(mixed_ref[2]+bias_ref[2]).astype(LOW)
    masks=head_masks(width)
    row=lax.broadcasted_iota(jnp.int32,(block,block),0)
    col=lax.broadcasted_iota(jnp.int32,(block,block),1)
    for i in range(length//block):
        rows=pl.ds(i*block,block)
        q=q_ref[rows,:]
        out=jnp.zeros((block,width),F32); lse=jnp.zeros((block,width),F32)
        for mask in masks:
            qh=jnp.where(mask,q,jnp.zeros_like(q))
            diag=jnp.where(row>=col,dot_nt(qh,k_ref[rows,:]),-1e30)
            top=jnp.max(diag,axis=1,keepdims=True)
            if i>0:
                rest=dot_nt(qh,k_ref[pl.ds(0,i*block),:])
                top=jnp.maximum(top,jnp.max(rest,axis=1,keepdims=True))
            diag=jnp.exp(diag-top)
            total=jnp.sum(diag,axis=1,keepdims=True)
            acc=dot_nn(diag.astype(LOW),v_ref[rows,:])
            if i>0:
                rest=jnp.exp(rest-top)
                total=total+jnp.sum(rest,axis=1,keepdims=True)
                acc=acc+dot_nn(rest.astype(LOW),v_ref[pl.ds(0,i*block),:])
            out=jnp.where(mask,acc/total,out)
            lse=jnp.where(mask,top+jnp.log(total),lse)
        att_ref[rows,:]=out.astype(LOW)
        lse_ref[rows,:]=lse

def attend_forward(mixed,bias,tables,seqs,length,block=256):
    pair,_,rows,cols=mixed.shape
    width=min(cols,128); groups=cols//width
    tok=lambda o,s,g:(o,s,g)
    spec=pl.BlockSpec((None,length,width),tok)
    shape=lambda d:jax.ShapeDtypeStruct((pair,rows,cols),d)
    return pl.pallas_call(
        lambda *r: fwd_kernel(block,*r),
        grid=(pair,seqs,groups),
        in_specs=[pl.BlockSpec((None,3,length,width),lambda o,s,g:(o,0,s,g)),
                  pl.BlockSpec((None,3,1,width),lambda o,s,g:(o,0,0,g)),
                  pl.BlockSpec((3,length,width),lambda o,s,g:(0,0,0))],
        out_specs=[spec]*5,
        out_shape=[shape(LOW)]*4+[shape(F32)],
        compiler_params=pltpu.CompilerParams(vmem_limit_bytes=48<<20),
        cost_estimate=light(flops=int(4*pair*rows*length*cols*0.6),bytes_accessed=pair*rows*cols*26,transcendentals=pair*rows*length*cols//128),
        name="attend_forward",
    )(mixed,bias,tables)

def bwd_kernel(block,q_ref,k_ref,v_ref,att_ref,lse_ref,do_ref,table_ref,out_ref,dk_acc,dv_acc,dq_acc):
    length,width=q_ref.shape
    half=ROT//2
    masks=head_masks(width)
    row=lax.broadcasted_iota(jnp.int32,(block,block),0)
    col=lax.broadcasted_iota(jnp.int32,(block,block),1)
    count=length//block
    for i in reversed(range(count)):
        rows=pl.ds(i*block,block)
        q=q_ref[rows,:]; do=do_ref[rows,:]; lse=lse_ref[rows,:]
        prod=do.astype(F32)*att_ref[rows,:].astype(F32)
        n=(i+1)*block
        keys=k_ref[pl.ds(0,n),:]; vals=v_ref[pl.ds(0,n),:]
        dq=jnp.zeros((block,width),F32)
        dk=None
        for h,mask in enumerate(masks):
            qh=jnp.where(mask,q,jnp.zeros_like(q)); dh=jnp.where(mask,do,jnp.zeros_like(do))
            delta=jnp.sum(jnp.where(mask,prod,0.0),axis=1,keepdims=True)
            lse_h=lse[:,h*HEAD_DIM:h*HEAD_DIM+1]
            s=dot_nt(qh,keys)
            p=jnp.exp(s-lse_h)
            if i==0:
                p=jnp.where(row>=col,p,0.0)
            else:
                p=jnp.concatenate([p[:,:n-block],jnp.where(row>=col,p[:,n-block:],0.0)],axis=1)
            dp=dot_nt(dh,vals)
            ds=(p*(dp-delta)).astype(LOW)
            pl_low=p.astype(LOW)
            dq=jnp.where(mask,dot_nn(ds,keys),dq)
            tk=dot_tn(ds,qh); tv=dot_tn(pl_low,dh)
            dk=tk if dk is None else dk+tk
            dv=tv if h==0 else dv+tv
        dq_acc[rows,:]=dq*(1.0/math.sqrt(HEAD_DIM))
        if i==count-1:
            dk_acc[...]=dk; dv_acc[...]=dv
        else:
            dk_acc[pl.ds(0,n),:]+=dk; dv_acc[pl.ds(0,n),:]+=dv
    def back(v):
        return v*table_ref[0]+pltpu.roll(v*table_ref[1],half,1)+pltpu.roll(v*table_ref[2],width-half,1)
    out_ref[0]=back(dq_acc[...]).astype(LOW)
    out_ref[1]=back(dk_acc[...]).astype(LOW)
    out_ref[2]=dv_acc[...].astype(LOW)

def attend_back(q,k,v,att,lse,grad,tables,seqs,length,block=256):
    pair,rows,cols=q.shape
    width=min(cols,128); groups=cols//width
    spec=pl.BlockSpec((None,length,width),lambda o,s,g:(o,s,g))
    return pl.pallas_call(
        lambda *r: bwd_kernel(block,*r),
        grid=(pair,seqs,groups),
        in_specs=[spec]*6+[pl.BlockSpec((3,length,width),lambda o,s,g:(0,0,0))],
        out_specs=pl.BlockSpec((None,3,length,width),lambda o,s,g:(o,0,s,g)),
        out_shape=jax.ShapeDtypeStruct((pair,3,rows,cols),LOW),
        scratch_shapes=[pltpu.VMEM((length,width),F32)]*3,
        compiler_params=pltpu.CompilerParams(vmem_limit_bytes=48<<20),
        cost_estimate=light(flops=int(10*pair*rows*length*cols*0.6),bytes_accessed=pair*rows*cols*20,transcendentals=pair*rows*length*cols//128),
        name="attend_back",
    )(q,k,v,att,lse,grad,tables)


VMEM_BYTES = 56 << 20
FORMS = {"nn": dot_nn, "nt": dot_nt, "tn": dot_tn}
ANYWHERE = pl.BlockSpec(memory_space=pl.ANY)


def tiles(size, most):
    while size > most and size % 2 == 0:
        size //= 2
    return size


def lead_spec(lead, block, where):
    return pl.BlockSpec((None,) * len(lead) + block, lambda *at: lead + where(*at))


def products(kind, terms, row_tile, col_tile, name, count=None, dtype=LOW, behind=()):
    one, _, two, _ = terms[0]
    deep = one.shape[-2] if kind == "tn" else one.shape[-1]
    rows = one.shape[-1] if kind == "tn" else one.shape[-2]
    cols = two.shape[-2] if kind == "nt" else two.shape[-1]
    tm, tn = tiles(rows, row_tile), tiles(cols, col_tile)
    one_block = ((deep, tm), lambda c, i, j: (0, i)) if kind == "tn" else ((tm, deep), lambda c, i, j: (i, 0))
    two_block = ((tn, deep), lambda c, i, j: (j, 0)) if kind == "nt" else ((deep, tn), lambda c, i, j: (0, j))
    number = len(terms)

    def kernel(*refs):
        total = sum(FORMS[kind](a[...], b[...]) for a, b in zip(refs[:number], refs[number : 2 * number]))
        refs[-1][...] = total.astype(dtype)

    if count is None:
        ones = [lead_spec(t[1], *one_block) for t in terms]
        out_spec = pl.BlockSpec((tm, tn), lambda c, i, j: (i, j))
        out_shape = (rows, cols)
    else:
        ones = [pl.BlockSpec((None,) + one_block[0], lambda c, i, j: (c,) + one_block[1](c, i, j)) for t in terms]
        out_spec = pl.BlockSpec((None, tm, tn), lambda c, i, j: (c, i, j))
        out_shape = (count, rows, cols)
    many = count or 1
    return pl.pallas_call(
        kernel,
        grid=(many, rows // tm, cols // tn),
        in_specs=ones + [lead_spec(t[3], *two_block) for t in terms] + [ANYWHERE] * len(behind),
        out_specs=out_spec,
        out_shape=jax.ShapeDtypeStruct(out_shape, dtype),
        compiler_params=pltpu.CompilerParams(vmem_limit_bytes=VMEM_BYTES),
        cost_estimate=light(
            flops=2 * rows * deep * cols * number * many,
            bytes_accessed=2 * (many * number * (rows * deep + deep * cols) + many * rows * cols),
            transcendentals=0,
        ),
        name=name,
    )(*[t[0] for t in terms], *[t[2] for t in terms], *behind)


def products_apart(place, kind, terms, col_tile, name, behind=()):
    one, _, two, _ = terms[0]
    deep = one.shape[-2] if kind == "tn" else one.shape[-1]
    rows = one.shape[-1] if kind == "tn" else one.shape[-2]
    cols = two.shape[-2] if kind == "nt" else two.shape[-1]
    tn = tiles(cols // 2, col_tile)
    half = cols // 2 // tn
    piece = rows // 4
    one_block = ((deep, rows), lambda j, at: (0, 0)) if kind == "tn" else ((rows, deep), lambda j, at: (0, 0))
    two_block = ((tn, deep), lambda j, at: (j, 0)) if kind == "nt" else ((deep, tn), lambda j, at: (0, j))
    number = len(terms)

    def kernel(at_ref, *refs):
        total = sum(FORMS[kind](a[...], b[...]) for a, b in zip(refs[:number], refs[number : 2 * number]))
        keep_first, send_first, keep_second, send_second, held = refs[-5:]
        held[...] = total.astype(LOW).reshape(held.shape)
        x, y = at_ref[0], at_ref[1]

        @pl.when(pl.program_id(0) < half)
        def _():
            for other in range(2):
                across = y if other == 0 else 1 - y
                keep_first[other] = held[2 * x + across]
                send_first[other] = held[2 * (1 - x) + across]

        @pl.when(pl.program_id(0) >= half)
        def _():
            for other in range(2):
                along = x if other == 0 else 1 - x
                keep_second[other] = held[2 * along + y]
                send_second[other] = held[2 * along + 1 - y]

    first = pl.BlockSpec((2, piece, tn), lambda j, at: (0, 0, jnp.minimum(j, half - 1)))
    second = pl.BlockSpec((2, piece, tn), lambda j, at: (0, 0, jnp.maximum(j - half, 0)))
    return pl.pallas_call(
        kernel,
        grid_spec=pltpu.PrefetchScalarGridSpec(
            num_scalar_prefetch=1,
            grid=(2 * half,),
            in_specs=[lead_spec(t[1], *one_block) for t in terms]
            + [lead_spec(t[3], *two_block) for t in terms]
            + [ANYWHERE] * len(behind),
            out_specs=[first, first, second, second],
            scratch_shapes=[pltpu.VMEM((4, piece, tn), LOW)],
        ),
        out_shape=[jax.ShapeDtypeStruct((2, piece, cols // 2), LOW)] * 4,
        compiler_params=pltpu.CompilerParams(vmem_limit_bytes=VMEM_BYTES),
        cost_estimate=light(
            flops=2 * rows * deep * cols * number,
            bytes_accessed=2 * (number * (rows * deep + deep * cols) + rows * cols),
            transcendentals=0,
        ),
        name=name,
    )(jnp.stack([place.x, place.y]).astype(jnp.int32), *[t[0] for t in terms], *[t[2] for t in terms], *behind)


def gate_kernel(weight_ref, rows_ref, turned_ref, slope_ref, hidden_ref):
    rows = rows_ref[...]
    gate = dot_nt(weight_ref[0], rows)
    up = dot_nt(weight_ref[1], rows)
    sig = 1.0 / (1.0 + jnp.exp(-gate))
    act = gate * sig
    hidden = (act * up).astype(LOW)
    turned_ref[...] = hidden
    hidden_ref[...] = hidden.T
    slope_ref[0] = (up * sig * (1.0 + gate * (1.0 - sig))).astype(LOW)
    slope_ref[1] = act.astype(LOW)


def gate_up(values, weight):
    rows, feat = values.shape
    units = weight.shape[1]
    tm = tiles(rows, 512)
    return pl.pallas_call(
        gate_kernel,
        grid=(rows // tm,),
        in_specs=[
            pl.BlockSpec((2, units, feat), lambda i: (0, 0, 0)),
            pl.BlockSpec((tm, feat), lambda i: (i, 0)),
        ],
        out_specs=[
            pl.BlockSpec((units, tm), lambda i: (0, i)),
            pl.BlockSpec((2, units, tm), lambda i: (0, 0, i)),
            pl.BlockSpec((tm, units), lambda i: (i, 0)),
        ],
        out_shape=[
            jax.ShapeDtypeStruct((units, rows), LOW),
            jax.ShapeDtypeStruct((2, units, rows), LOW),
            jax.ShapeDtypeStruct((rows, units), LOW),
        ],
        compiler_params=pltpu.CompilerParams(vmem_limit_bytes=VMEM_BYTES),
        cost_estimate=light(
            flops=4 * rows * feat * units,
            bytes_accessed=2 * (rows * feat + 2 * feat * units + 4 * rows * units),
            transcendentals=rows * units,
        ),
        name="gate_up",
    )(weight, values)


def hidden_back_kernel(weight_ref, grad_ref, slope_ref, *refs):
    turned_ref, out_ref = refs[-2:]
    grad = dot_nt(weight_ref[...], grad_ref[...])
    for c in range(2):
        part = (grad * slope_ref[c].astype(F32)).astype(LOW)
        turned_ref[c] = part
        out_ref[c] = part.T


def hidden_back(grad, weight, slope, behind=()):
    rows, feat = grad.shape
    units = weight.shape[0]
    tm = tiles(rows, 512)
    return pl.pallas_call(
        hidden_back_kernel,
        grid=(rows // tm,),
        in_specs=[
            pl.BlockSpec((units, feat), lambda i: (0, 0)),
            pl.BlockSpec((tm, feat), lambda i: (i, 0)),
            pl.BlockSpec((2, units, tm), lambda i: (0, 0, i)),
        ]
        + [ANYWHERE] * len(behind),
        out_specs=[
            pl.BlockSpec((2, units, tm), lambda i: (0, 0, i)),
            pl.BlockSpec((2, tm, units), lambda i: (0, i, 0)),
        ],
        out_shape=[
            jax.ShapeDtypeStruct((2, units, rows), LOW),
            jax.ShapeDtypeStruct((2, rows, units), LOW),
        ],
        compiler_params=pltpu.CompilerParams(vmem_limit_bytes=VMEM_BYTES),
        cost_estimate=light(
            flops=2 * rows * feat * units,
            bytes_accessed=2 * (rows * feat + feat * units + 6 * rows * units),
            transcendentals=0,
        ),
        name="hidden_back",
    )(weight, grad, slope, *behind)


def pieces_of(places, rows, feat, dtype, body, name, operands, behind=()):
    def kernel(at_ref, *refs):
        for step in range(len(places)):
            pl.when(pl.program_id(0) == step)(lambda step=step: body(step, refs, refs[-1]))

    specs = [pl.BlockSpec(v.shape, lambda i, at, n=v.ndim: (0,) * n) for v in operands]
    return pl.pallas_call(
        kernel,
        grid_spec=pltpu.PrefetchScalarGridSpec(
            num_scalar_prefetch=1,
            grid=(len(places),),
            in_specs=specs + [ANYWHERE] * len(behind),
            out_specs=pl.BlockSpec((None, rows, feat), lambda i, at: (at[i], 0, 0)),
        ),
        out_shape=jax.ShapeDtypeStruct((len(places), rows, feat), dtype),
        compiler_params=pltpu.CompilerParams(vmem_limit_bytes=VMEM_BYTES),
        cost_estimate=light(flops=0, bytes_accessed=4 * len(places) * rows * feat, transcendentals=0),
        name=name,
    )(jnp.stack(places).astype(jnp.int32), *operands, *behind)


def lay_rows(one, two, own, over_one, over_two, far, dtype, behind=()):
    rows, feat = own.shape

    def body(step, refs, out_ref):
        start = 0
        for ref in refs[step : step + 1] if step < 3 else refs[3 : 3 + len(far)]:
            out_ref[:, start : start + ref.shape[1]] = ref[...].astype(dtype)
            start += ref.shape[1]

    places = [2 * one + two, 2 * (1 - one) + two, 2 * one + 1 - two, 2 * (1 - one) + 1 - two]
    return pieces_of(places, rows, feat, dtype, body, "lay_rows", [own, over_one, over_two] + list(far), behind)


def norm_first(places, pieces, gain, shift, behind=()):
    rows, feat = pieces[0].shape

    def body(step, refs, out_ref):
        values = refs[step][...].astype(F32)
        out_ref[...] = (centre(values)[0] * refs[4][...] + refs[5][...]).astype(LOW)

    return pieces_of(places, rows, feat, LOW, body, "norm_first", pieces + [gain, shift], behind).reshape(-1, feat)


def lay_pieces(places, pieces, behind=()):
    rows, feat = pieces[0].shape

    def body(step, refs, out_ref):
        out_ref[...] = refs[step][...]

    return pieces_of(places, rows, feat, LOW, body, "lay_pieces", pieces, behind).reshape(-1, feat)


def join(keep_first, came_first, keep_second, came_second, behind=()):
    _, rows, half = keep_first.shape

    def kernel(one, two, three, four, *refs):
        first_stays, first_goes, second_stays, second_goes = refs[-4:]
        first_stays[...] = one[0].astype(F32) + two[0].astype(F32)
        first_goes[...] = (one[1].astype(F32) + two[1].astype(F32)).astype(LOW)
        second_stays[...] = three[0].astype(F32) + four[0].astype(F32)
        second_goes[...] = (three[1].astype(F32) + four[1].astype(F32)).astype(LOW)

    tm = tiles(rows, 128)
    pair = pl.BlockSpec((2, tm, half), lambda i: (0, i, 0))
    flat = pl.BlockSpec((tm, half), lambda i: (i, 0))
    shape = lambda dtype: jax.ShapeDtypeStruct((rows, half), dtype)
    return pl.pallas_call(
        kernel,
        grid=(rows // tm,),
        in_specs=[pair] * 4 + [ANYWHERE] * len(behind),
        out_specs=[flat] * 4,
        out_shape=[shape(F32), shape(LOW)] * 2,
        cost_estimate=light(flops=4 * rows * half, bytes_accessed=28 * rows * half, transcendentals=0),
        compiler_params=pltpu.CompilerParams(vmem_limit_bytes=VMEM_BYTES),
        name="join",
    )(keep_first, came_first, keep_second, came_second, *behind)


def on_rows(kernel, shares, values, tables, outs, sums, name, behind=()):
    rows, half = shares[0].shape
    feat = 2 * half
    tm = tiles(rows, 128)
    count, tabled = len(values), len(tables)

    def body(*refs):
        total = jnp.concatenate(
            [refs[0][...] + refs[1][...].astype(F32), refs[2][...] + refs[3][...].astype(F32)], axis=1
        )
        rest = refs[4 + count + tabled + len(behind) :]
        kernel(total, refs[4 : 4 + count], refs[4 + count : 4 + count + tabled], rest[: len(outs)], rest[len(outs) :])

    block = lambda cols: pl.BlockSpec((tm, cols), lambda i: (i, 0))
    return pl.pallas_call(
        body,
        grid=(rows // tm,),
        in_specs=[block(half)] * 4
        + [block(feat)] * count
        + [pl.BlockSpec((1, feat), lambda i: (0, 0))] * tabled
        + [ANYWHERE] * len(behind),
        out_specs=[block(feat)] * len(outs) + [pl.BlockSpec((2, feat), lambda i: (0, 0))] * sums,
        out_shape=[jax.ShapeDtypeStruct((rows, feat), dtype) for dtype in outs]
        + [jax.ShapeDtypeStruct((2, feat), F32)] * sums,
        cost_estimate=light(flops=20 * rows * feat, bytes_accessed=20 * rows * feat, transcendentals=0),
        compiler_params=pltpu.CompilerParams(vmem_limit_bytes=VMEM_BYTES),
        name=name,
    )(*shares, *values, *tables, *behind)


def centre(values):
    centred = values - jnp.mean(values, axis=1, keepdims=True)
    inv_std = lax.rsqrt(jnp.mean(centred * centred, axis=1, keepdims=True) + EPSILON)
    return centred * inv_std, inv_std


def add_norm(shares, values, gain, shift, behind=()):
    def kernel(total, value_refs, table_refs, out_refs, _):
        middle = value_refs[0][...].astype(F32) + total
        out_refs[0][...] = middle
        out_refs[1][...] = (centre(middle)[0] * table_refs[0][...] + table_refs[1][...]).astype(LOW)

    return on_rows(kernel, shares, [values], [gain, shift], [F32, LOW], 0, "add_norm", behind)


def add_low(shares, values, behind=()):
    def kernel(total, value_refs, _, out_refs, __):
        out_refs[0][...] = (value_refs[0][...].astype(F32) + total).astype(LOW)

    return on_rows(kernel, shares, [values], [], [LOW], 0, "add_low", behind)[0]


def norm_back(shares, values, gain, grad, outs, behind=()):
    def kernel(total, value_refs, table_refs, out_refs, sum_refs):
        scaled, inv_std = centre(value_refs[0][...].astype(F32))
        part = total * table_refs[0][...]
        first = jnp.mean(part, axis=1, keepdims=True)
        second = jnp.mean(part * scaled, axis=1, keepdims=True)
        result = value_refs[1][...].astype(F32) + inv_std * (part - first - scaled * second)
        for ref in out_refs:
            ref[...] = result.astype(ref.dtype)
        sums = sum_refs[0]

        @pl.when(pl.program_id(0) == 0)
        def _():
            sums[...] = jnp.zeros_like(sums)

        sums[0:1, :] += jnp.sum(total * scaled, axis=0, keepdims=True)
        sums[1:2, :] += jnp.sum(total, axis=0, keepdims=True)

    return on_rows(kernel, shares, [values, grad], [gain], outs, 1, "norm_back", behind)


def qkv_back(mine, theirs, my_grad, their_grad, behind=()):
    rows, feat = mine.shape
    count, _, cols = my_grad.shape
    tm = tiles(feat, 512)

    def kernel(mine_ref, theirs_ref, my_ref, their_ref, *refs):
        one, two = mine_ref[...].T, theirs_ref[...].T
        for c in range(count):
            refs[-1][c] = (dot_nn(one, my_ref[c]) + dot_nn(two, their_ref[c])).astype(LOW)

    tall = pl.BlockSpec((rows, tm), lambda i: (0, i))
    whole = pl.BlockSpec((count, rows, cols), lambda i: (0, 0, 0))
    return pl.pallas_call(
        kernel,
        grid=(feat // tm,),
        in_specs=[tall, tall, whole, whole] + [ANYWHERE] * len(behind),
        out_specs=pl.BlockSpec((count, tm, cols), lambda i: (0, i, 0)),
        out_shape=jax.ShapeDtypeStruct((count, feat, cols), LOW),
        cost_estimate=light(
            flops=4 * count * rows * feat * cols,
            bytes_accessed=4 * rows * feat + 4 * count * rows * cols + 2 * count * feat * cols,
            transcendentals=0,
        ),
        compiler_params=pltpu.CompilerParams(vmem_limit_bytes=VMEM_BYTES),
        name="grad_qkv",
    )(mine, theirs, my_grad, their_grad, *behind)


class Place:
    def __init__(self):
        self.fsdp = lax.axis_size("fsdp")
        self.context = lax.axis_size("context")
        self.tensor = lax.axis_size("tensor")
        self.pairs = self.tensor // 2
        self.z = lax.axis_index("fsdp")
        self.x = lax.axis_index("context")
        self.t = lax.axis_index("tensor")
        self.y = self.t // 2
        self.core = self.t % 2

    def square(self, seqs):
        return self.context == 2 and self.pairs == 2 and seqs == 1

    def size(self, which):
        return self.context if which == "x" else self.pairs

    def at(self, which):
        return self.x if which == "x" else self.y

    def shift(self, value, which, step):
        if which == "z":
            n = self.fsdp
            return lax.ppermute(value, "fsdp", [(i, (i + step) % n) for i in range(n)])
        if which == "x":
            n = self.context
            return lax.ppermute(value, "context", [(i, (i + step) % n) for i in range(n)])
        n = self.tensor
        return lax.ppermute(value, "tensor", [(i, (i + 2 * step) % n) for i in range(n)])

    def swap(self, value):
        return lax.ppermute(value, "tensor", [(i, i ^ 1) for i in range(self.tensor)])


def pick(value, index, axis):
    return lax.dynamic_index_in_dim(value, index, axis, keepdims=False)


def scatter_stage(place, value, axis, which):
    n, at = place.size(which), place.at(which)
    total = pick(value, at, axis).astype(F32)
    for step in range(1, n):
        sent = pick(value, (at + step) % n, axis)
        total = total + place.shift(sent, which, step).astype(F32)
    return total


def gather_stage(place, value, axis, which):
    n, at = place.size(which), place.at(which)
    if n == 1:
        return value
    if n == 2:
        return ordered(at, value, place.shift(value, which, 1), axis)
    parts = [value] + [place.shift(value, which, step) for step in range(1, n)]
    order = (at - jnp.arange(n)) % n
    shape = list(value.shape)
    shape[axis] = n * shape[axis]
    return jnp.take(jnp.stack(parts, axis), order, axis=axis).reshape(shape)


def ordered(at, mine, other, axis):
    first = jnp.where(at == 0, mine, other)
    second = jnp.where(at == 0, other, mine)
    return jnp.concatenate([first, second], axis=axis)


def after(value, *others):
    return lax.optimization_barrier((value,) + others)[0]


class RowSum:
    def __init__(self, place, kind, terms, seqs, name, behind=()):
        self.place = place
        self.square = place.square(seqs)
        if self.square:
            self.keep_first, self.sent, self.keep_second, self.second = products_apart(
                place, kind, terms, 512, name, behind
            )
            return
        value = self.sent = products(kind, terms, 1024, 512, name, behind=behind)
        feat = value.shape[1]
        value = value.reshape(seqs, place.context, place.pairs, -1, feat)
        first, second = value[..., : feat // 2], value[..., feat // 2 :]
        first = scatter_stage(place, first, 1, "x").astype(LOW)
        second = scatter_stage(place, second, 2, "y").astype(LOW)
        first = scatter_stage(place, first, 1, "y").reshape(-1, feat // 2)
        second = scatter_stage(place, second, 1, "x").reshape(-1, feat // 2)
        nothing = jnp.zeros(first.shape, LOW)
        self.shares = [first, nothing, second, nothing]

    def start(self, *others):
        if self.square:
            first, second = after((self.sent, self.second), *others) if others else (self.sent, self.second)
            self.came_first = self.place.shift(first, "x", 1)
            self.came_second = self.place.shift(second, "y", 1)
        return self

    def follow(self, behind=()):
        if not self.square:
            return self.shares[0]
        first, first_goes, second, second_goes = join(
            self.keep_first, self.came_first, self.keep_second, self.came_second, behind
        )
        self.shares = [first, self.place.shift(first_goes, "y", 1), second, self.place.shift(second_goes, "x", 1)]
        return first


def spread_rows(place, value, seqs, behind=()):
    feat = value.shape[-1]
    half = feat // 2
    if place.square(seqs):
        over_x = place.shift(value, "x", 1)
        over_y = place.shift(value, "y", 1)
        far_first = place.shift(over_y[:, :half], "x", 1)
        far_second = place.shift(over_x[:, half:], "y", 1)
        whole = lay_rows(place.x, place.y, value, over_x, over_y, [far_first, far_second], LOW, behind)
        return whole.reshape(-1, feat)
    value = value.reshape(seqs, -1, feat)
    rows = value.shape[1]
    first, second = value[..., :half], value[..., half:]
    first = gather_stage(place, first, 1, "y")
    second = gather_stage(place, second, 1, "x")
    first = gather_stage(place, first, 1, "x")
    second = second.reshape(seqs, place.context, rows, half)
    second = gather_stage(place, second, 2, "y").reshape(first.shape)
    return jnp.concatenate([first, second], axis=-1).reshape(-1, feat)


def whole_rows(place, value, seqs, dtype, behind=()):
    feat = value.shape[-1]
    if place.square(seqs):
        over_y, over_core = place.shift(value, "y", 1), place.swap(value)
        whole = lay_rows(place.core, place.y, value, over_core, over_y, [place.swap(over_y)], dtype, behind)
        return whole.reshape(2, -1, feat)
    value = gather_stage(place, value.reshape(seqs, -1, feat), 1, "y")
    return ordered(place.core, value, place.swap(value), 0).astype(dtype)


def other_rows(place, value):
    rows = value.shape[0] // 2
    straight = place.shift(lax.dynamic_slice_in_dim(value, place.y * rows, rows, 0), "x", 1)
    return [value[:rows], value[rows:], straight, place.shift(straight, "y", 1)]


def other_places(place):
    x, y = place.x, place.y
    return [2 * x, 2 * x + 1, 2 * (1 - x) + y, 2 * (1 - x) + 1 - y]


def empty_kernel(out_ref):
    pass


def empty(shape, dtype):
    return pl.pallas_call(
        empty_kernel,
        out_specs=pl.BlockSpec(memory_space=pl.ANY),
        out_shape=jax.ShapeDtypeStruct(shape, dtype),
        name="empty",
    )()


def gather_pack(place, shard, before, behind, ready):
    n, z = place.fsdp, place.z
    blocks, size, cols = shard.shape
    half = blocks // 2
    low = place.shift(before[:half, :size], "z", 1)
    high = place.shift(behind[half:, :size], "z", -1)
    low = after(low, ready)
    whole = empty((blocks, n * size, cols), shard.dtype)
    for part, block, start in (
        (shard, 0, z),
        (before[:, :size], 0, (z + 3) % n),
        (behind[:, :size], 0, (z + 1) % n),
        (low, 0, (z + 2) % n),
        (high, half, (z + 2) % n),
    ):
        whole = lax.dynamic_update_slice(whole, part, (block, start * size, 0))
    return whole, (low, high)


def reduce_shards(place, grad, axis, half_axis, begin, ready):
    n = place.fsdp
    size = grad.shape[axis] // n
    half = (size if axis == half_axis else grad.shape[half_axis]) // 2

    def part(ahead, side):
        shard = lax.dynamic_slice_in_dim(grad, (place.z + ahead) % n * size, size, axis)
        return lax.slice_in_dim(shard, side * half, (side + 1) * half, axis=half_axis).astype(F32)

    def pair(one, two):
        return after(jnp.stack([one, two]).astype(LOW), begin)

    left = place.shift(pair(part(2, 1), part(1, 0)), "z", 1)
    right = place.shift(pair(part(2, 0), part(3, 1)), "z", -1)
    left, right = after((left, right), ready)
    left_high = place.shift((part(1, 1) + left[0].astype(F32)).astype(LOW), "z", 1)
    right_low = place.shift((part(3, 0) + right[0].astype(F32)).astype(LOW), "z", -1)
    low = part(0, 0) + left[1].astype(F32) + right_low.astype(F32)
    high = part(0, 1) + right[1].astype(F32) + left_high.astype(F32)
    return jnp.concatenate([low.astype(LOW), high.astype(LOW)], axis=half_axis)


def total_over(place, value, which):
    n = {"z": place.fsdp, "x": place.context, "y": place.pairs, "core": 2}[which]
    if n == 1:
        return value
    if which == "core":
        return value + place.swap(value)
    if n == 2:
        return value + place.shift(value, which, 1)
    at = {"z": place.z, "x": place.x, "y": place.y}[which]
    parts = jnp.zeros((n,) + value.shape, value.dtype)
    parts = lax.dynamic_update_index_in_dim(parts, value, at, 0)
    for step in range(1, n):
        sent = place.shift(value, which, step)
        parts = lax.dynamic_update_index_in_dim(parts, sent, (at - step) % n, 0)
    return jnp.sum(parts, axis=0)


def small_totals(place, sums, bias, bias_other):
    n, z = place.fsdp, place.z
    feat = sums.shape[1]
    pad = [(0, 1), (0, 0)]
    sent = place.swap(jnp.concatenate([sums, jnp.pad(bias_other, pad)], axis=1))
    sums, bias = sums + sent[:, :feat], jnp.pad(bias, pad) + sent[:, feat:]
    if place.context == 2:
        sent = place.shift(jnp.concatenate([sums, bias], axis=1), "x", 1)
        sums = sums + sent[:, :feat]
        bias = ordered(place.x, bias, sent[:, feat:], 1)
    else:
        sums = total_over(place, sums, "x")
        bias = gather_stage(place, bias, 1, "x")
    size = feat // n
    parts = jnp.zeros((n,) + (4, size + bias.shape[1]), F32)
    for step in range(n):
        part = lax.dynamic_slice_in_dim(sums, (z + step) % n * size, size, 1)
        part = jnp.concatenate([part, bias], axis=1)
        part = place.shift(part, "z", step) if step else part
        parts = lax.dynamic_update_index_in_dim(parts, part, (z - step) % n, 0)
    total = jnp.sum(parts, axis=0)
    return total[:, :size], total[:3, size:]


def local(
    hidden_in,
    norm_gains,
    norm_biases,
    qkv_weight,
    qkv_bias,
    out_weight,
    gate_up_weight,
    down_weight,
    cotangent,
):
    place = Place()
    all_seqs, part_rows, feat = hidden_in.shape
    seqs = all_seqs // 2
    length = part_rows * place.context
    own_rows = part_rows // place.pairs
    head_cols = qkv_bias.shape[1] // place.context
    hidden_cols = down_weight.shape[0] // place.context

    def columns(value, count, axis):
        return lax.dynamic_slice_in_dim(value, place.x * count, count, axis)

    def own_sequences(value):
        return lax.dynamic_slice_in_dim(value, place.core * seqs, seqs, 0)

    def own_piece(value):
        return lax.dynamic_slice_in_dim(value, place.y * own_rows, own_rows, 1)

    pack = jnp.concatenate(
        [columns(qkv_weight, head_cols, 2), columns(out_weight, head_cols, 0).T[None]]
    )
    norm_part = jnp.concatenate([norm_gains, norm_biases]).reshape(-1, head_cols)
    norm_rows = norm_part.shape[0]
    pad = -norm_rows % 16
    part_feat = pack.shape[1]
    norm_block = jnp.pad(norm_part, [(0, pad), (0, 0)])[None]
    extra = jnp.pad(norm_block, [(0, 3), (0, 0), (0, 0)])
    pack = jnp.concatenate([pack, extra], axis=1)
    pack_before, pack_behind = place.shift(pack, "z", 1), place.shift(pack, "z", -1)
    norm_far = place.shift(norm_block, "z", 2)
    hidden_mine = own_sequences(hidden_in)
    hidden_mine = hidden_mine.reshape(-1, feat)
    norms = jnp.zeros((2, 2, feat), F32)
    for step, piece in (
        (0, norm_block),
        (1, pack_before[:1, part_feat:]),
        (2, norm_far),
        (3, pack_behind[:1, part_feat:]),
    ):
        piece = piece[0, :norm_rows].reshape(2, 2, part_feat).astype(F32)
        norms = lax.dynamic_update_slice(norms, piece, (0, 0, (place.z - step) % place.fsdp * part_feat))
    gains, shifts = norms[0][:, None, :], norms[1][:, None, :]
    bias = columns(qkv_bias, head_cols, 1)
    bias_other = place.swap(bias).astype(F32)[None, :, None, :]
    bias = bias.astype(F32)[None, :, None, :]

    gate_up_part = columns(gate_up_weight, hidden_cols, 2).transpose(0, 2, 1)
    down_part = columns(down_weight, hidden_cols, 0)
    top_mine = own_sequences(cotangent)
    if place.square(seqs):
        pieces = other_rows(place, hidden_mine)
        top_pieces = other_rows(place, top_mine.reshape(-1, feat))
        normed = norm_first(other_places(place), pieces, gains[0], shifts[0], behind=[top_pieces[3]])
        grad_top = lay_pieces(other_places(place), top_pieces)
    else:
        whole = gather_stage(place, hidden_mine.reshape(seqs, -1, feat), 1, "x").reshape(-1, feat)
        normed = (centre(whole.astype(F32))[0] * gains[0] + shifts[0]).astype(LOW)
        grad_top = gather_stage(place, top_mine, 1, "x").reshape(seqs * length, feat)
    w_attn, far = gather_pack(place, pack[:, :part_feat], pack_before, pack_behind, normed)
    gate_up_part, down_part = after((gate_up_part, down_part), *far)
    w_gate_up = lax.all_gather(gate_up_part, "fsdp", axis=2, tiled=True)
    w_down = lax.all_gather(down_part, "fsdp", axis=1, tiled=True)
    tables = rotary_tables(length, min(head_cols, 128))
    w_attn_other = place.swap(w_attn)

    def attend(weight, bias):
        mixed = jnp.einsum("rd,cde->cre", normed, weight[:3], preferred_element_type=F32)
        return attend_forward(mixed[None], bias, tables, seqs, length)

    kept = attend(w_attn, bias)
    kept_other = attend(w_attn_other, bias_other)
    attended, attended_other = kept[3][0], kept_other[3][0]
    theirs_top, theirs_one, theirs_attended = place.swap(grad_top), place.swap(normed), place.swap(attended_other)
    attn_sum = RowSum(
        place,
        "nt",
        [(attended, (), w_attn, (3,)), (attended_other, (), w_attn_other, (3,))],
        seqs,
        "out",
        behind=[theirs_top, theirs_one],
    ).start()
    attn_sum.follow()
    inputs = own_piece(hidden_mine.reshape(seqs, -1, feat)).reshape(-1, feat)
    middle, normed_two = add_norm(attn_sum.shares, inputs, gains[1], shifts[1])
    normed_two = spread_rows(place, normed_two, seqs)

    w_gate_up_other = place.swap(after(w_gate_up, middle))
    turned_other, slope_other, hidden_part = gate_up(normed_two, w_gate_up_other)
    theirs_turned, w_down_other = place.swap(turned_other), place.swap(after(w_down, turned_other))
    turned, slope, hidden = gate_up(normed_two, w_gate_up)
    grad_down = products(
        "nn",
        [(turned, (), grad_top, ()), (theirs_turned, (), theirs_top, ())],
        hidden_cols,
        512,
        "grad_down",
    )
    down_sum = lax.psum_scatter(grad_down, "fsdp", scatter_dimension=1, tiled=True)
    grad_gu_turned_other, grad_gu_other = hidden_back(grad_top, w_down_other, slope_other, [grad_down])
    theirs_gu, theirs_two = place.swap(grad_gu_turned_other), place.swap(normed_two)
    grad_gu_turned, grad_gu = hidden_back(grad_top, w_down, slope, [grad_gu_other])
    two_sum = RowSum(
        place,
        "nn",
        [(grad_gu, (c,), w_gate_up, (c,)) for c in range(2)]
        + [(grad_gu_other, (c,), w_gate_up_other, (c,)) for c in range(2)],
        seqs,
        "grad_two",
        behind=[theirs_two, theirs_attended, theirs_gu],
    ).start()
    grad_gate_up = products(
        "nn",
        [(grad_gu_turned, (), normed_two, ()), (theirs_gu, (), theirs_two, ())],
        hidden_cols,
        512,
        "grad_gate_up",
        count=2,
        behind=[two_sum.sent],
    )
    two_next = two_sum.follow([grad_gate_up, down_sum])
    gate_up_sum = lax.psum_scatter(after(grad_gate_up, two_next), "fsdp", scatter_dimension=2, tiled=True)
    down_sums = RowSum(
        place,
        "nn",
        [(hidden, (), w_down, ()), (hidden_part, (), w_down_other, ())],
        seqs,
        "down",
        behind=[two_next],
    )
    top_rows = own_piece(top_mine).reshape(-1, feat)
    grad_middle, mid_low, sums_two = norm_back(
        two_sum.shares, middle, gains[1], top_rows, [F32, LOW], behind=[down_sums.sent]
    )
    grad_mid_low = spread_rows(place, mid_low, seqs)
    down_sum = gather_stage(place, after(down_sum, grad_mid_low), 0, "x")
    down_sums.start(grad_mid_low)

    def attend_grad(kept, weight, behind):
        grad_att = products("nn", [(grad_mid_low, (), weight, (3,))], 1024, head_cols, "grad_att", behind=behind)
        return attend_back(*kept, grad_att[None], tables, seqs, length)[0]

    theirs_mid = place.swap(grad_mid_low)
    grad_mixed_other = attend_grad(kept_other, w_attn_other, [])
    theirs_mixed = place.swap(grad_mixed_other)
    grad_mixed = attend_grad(kept, w_attn, [grad_mixed_other, theirs_mid])
    down_next = down_sums.follow([grad_mixed])
    gate_up_mine = gate_up_sum
    gate_up_sum = gather_stage(place, after(gate_up_sum, grad_mixed), 1, "x")
    final_out = add_low(down_sums.shares, middle, behind=[grad_mixed])
    grad_qkv = qkv_back(normed, theirs_one, grad_mixed, theirs_mixed, behind=[down_next, gate_up_mine])
    one_sum = RowSum(
        place,
        "nt",
        [(grad_mixed, (c,), w_attn, (c,)) for c in range(3)]
        + [(grad_mixed_other, (c,), w_attn_other, (c,)) for c in range(3)],
        seqs,
        "grad_one",
        behind=[grad_qkv],
    ).start()
    grad_out = products(
        "tn",
        [(grad_mid_low, (), attended, ()), (theirs_mid, (), theirs_attended, ())],
        512,
        head_cols,
        "grad_out",
        behind=[one_sum.sent],
    )
    one_next = one_sum.follow([grad_out])
    qkv_sum = reduce_shards(place, grad_qkv, 1, 1, grad_mixed, one_next)
    input_low, sums_one = norm_back(one_sum.shares, inputs, gains[0], grad_middle, [LOW], behind=[one_next])
    out_sum = reduce_shards(place, grad_out, 0, 0, one_next, input_low)
    sums = total_over(place, jnp.concatenate([sums_one, sums_two]), "y")
    input_grad = whole_rows(place, after(input_low, sums), seqs, F32)
    layer_out = whole_rows(place, after(final_out, input_low, sums), seqs, LOW)
    sums, grad_bias = small_totals(
        place,
        sums,
        jnp.sum(grad_mixed.astype(F32), axis=1),
        jnp.sum(grad_mixed_other.astype(F32), axis=1),
    )

    return (
        layer_out,
        input_grad,
        sums[0::2],
        sums[1::2],
        gather_stage(place, qkv_sum, 2, "x").astype(F32),
        grad_bias,
        gather_stage(place, out_sum, 1, "x").T.astype(F32),
        gate_up_sum.transpose(0, 2, 1).astype(F32),
        down_sum.astype(F32),
    )


def solution(mesh):
    placed = (
        P("fsdp", "context", None),
        P(None, "fsdp"),
        P(None, "fsdp"),
        P(None, "fsdp", "tensor"),
        P(None, "tensor"),
        P("tensor", "fsdp"),
        P(None, "fsdp", "tensor"),
        P("tensor", "fsdp"),
        P("fsdp", "context", None),
    )
    return jax.shard_map(
        local,
        mesh=mesh,
        in_specs=placed,
        out_specs=(
            P("fsdp", "context", None),
            P("fsdp", "context", None),
            P(None, "fsdp"),
            P(None, "fsdp"),
            P(None, "fsdp", "tensor"),
            P(None, "tensor"),
            P("tensor", "fsdp"),
            P(None, "fsdp", "tensor"),
            P("tensor", "fsdp"),
        ),
        check_vma=False,
    )
```

```python
import math

import jax
import jax.numpy as jnp
import numpy as np
from jax import lax
from jax.experimental import pallas as pl
from jax.experimental.pallas import tpu as pltpu
from jax.sharding import PartitionSpec as P

HEAD_DIM = 64
ROT = 16
EPSILON = 1e-05
F32 = jnp.float32
LOW = jnp.bfloat16


def rotary_tables(length, width):
    column = np.arange(width) % HEAD_DIM
    half = ROT // 2
    frequency = np.power(10000.0, -2.0 * (column % half) / ROT).astype(np.float32)
    angles = np.arange(length, dtype=np.float32)[:, None] * frequency[None, :]
    inside = column < ROT
    lower = column < half
    sine = np.sin(angles)
    cosine = np.where(inside, np.cos(angles), 1.0)
    minus = np.where(lower, -sine, 0.0)
    plus = np.where(inside & ~lower, sine, 0.0)
    return jnp.asarray(np.stack([cosine, minus, plus]).astype(np.float32))

def light(flops, bytes_accessed, transcendentals):
    return pl.CostEstimate(flops=flops // 100, bytes_accessed=bytes_accessed // 100, transcendentals=0)


def dot_nt(a,b): return lax.dot_general(a,b,(((1,),(1,)),((),())),preferred_element_type=F32)
def dot_nn(a,b): return lax.dot_general(a,b,(((1,),(0,)),((),())),preferred_element_type=F32)
def dot_tn(a,b): return lax.dot_general(a,b,(((0,),(0,)),((),())),preferred_element_type=F32)

def head_masks(width):
    lane=lax.broadcasted_iota(jnp.int32,(1,width),1)
    return [ (lane//HEAD_DIM)==h for h in range(width//HEAD_DIM)]

def fwd_kernel(block, mixed_ref, bias_ref, table_ref, *refs):
    q_ref, k_ref, v_ref, att_ref, lse_ref = refs[-5:]
    length, width = q_ref.shape
    half=ROT//2
    def rotated(c):
        v=mixed_ref[c]+bias_ref[c]
        return v*table_ref[0]+pltpu.roll(v,width-half,1)*table_ref[1]+pltpu.roll(v,half,1)*table_ref[2]
    q_ref[...]=(rotated(0)*(1.0/math.sqrt(HEAD_DIM))).astype(LOW)
    k_ref[...]=rotated(1).astype(LOW)
    v_ref[...]=(mixed_ref[2]+bias_ref[2]).astype(LOW)
    masks=head_masks(width)
    row=lax.broadcasted_iota(jnp.int32,(block,block),0)
    col=lax.broadcasted_iota(jnp.int32,(block,block),1)
    for i in range(length//block):
        rows=pl.ds(i*block,block)
        q=q_ref[rows,:]
        out=jnp.zeros((block,width),F32); lse=jnp.zeros((block,width),F32)
        for mask in masks:
            qh=jnp.where(mask,q,jnp.zeros_like(q))
            diag=jnp.where(row>=col,dot_nt(qh,k_ref[rows,:]),-1e30)
            top=jnp.max(diag,axis=1,keepdims=True)
            if i>0:
                rest=dot_nt(qh,k_ref[pl.ds(0,i*block),:])
                top=jnp.maximum(top,jnp.max(rest,axis=1,keepdims=True))
            diag=jnp.exp(diag-top)
            total=jnp.sum(diag,axis=1,keepdims=True)
            acc=dot_nn(diag.astype(LOW),v_ref[rows,:])
            if i>0:
                rest=jnp.exp(rest-top)
                total=total+jnp.sum(rest,axis=1,keepdims=True)
                acc=acc+dot_nn(rest.astype(LOW),v_ref[pl.ds(0,i*block),:])
            out=jnp.where(mask,acc/total,out)
            lse=jnp.where(mask,top+jnp.log(total),lse)
        att_ref[rows,:]=out.astype(LOW)
        lse_ref[rows,:]=lse

def attend_forward(mixed,bias,tables,seqs,length,behind=(),block=256):
    pair,_,rows,cols=mixed.shape
    width=min(cols,128); groups=cols//width
    tok=lambda o,s,g:(o,s,g)
    spec=pl.BlockSpec((None,length,width),tok)
    shape=lambda d:jax.ShapeDtypeStruct((pair,rows,cols),d)
    return pl.pallas_call(
        lambda *r: fwd_kernel(block,*r),
        grid=(pair,seqs,groups),
        in_specs=[pl.BlockSpec((None,3,length,width),lambda o,s,g:(o,0,s,g)),
                  pl.BlockSpec((None,3,1,width),lambda o,s,g:(o,0,0,g)),
                  pl.BlockSpec((3,length,width),lambda o,s,g:(0,0,0))]+[pl.BlockSpec(memory_space=pl.ANY)]*len(behind),
        out_specs=[spec]*5,
        out_shape=[shape(LOW)]*4+[shape(F32)],
        compiler_params=pltpu.CompilerParams(vmem_limit_bytes=48<<20),
        cost_estimate=light(flops=int(4*pair*rows*length*cols*0.6),bytes_accessed=pair*rows*cols*26,transcendentals=pair*rows*length*cols//128),
        name="attend_forward",
    )(mixed,bias,tables,*behind)

def bwd_kernel(block,q_ref,k_ref,v_ref,att_ref,lse_ref,do_ref,table_ref,out_ref,dk_acc,dv_acc,dq_acc):
    length,width=q_ref.shape
    half=ROT//2
    masks=head_masks(width)
    row=lax.broadcasted_iota(jnp.int32,(block,block),0)
    col=lax.broadcasted_iota(jnp.int32,(block,block),1)
    count=length//block
    for i in reversed(range(count)):
        rows=pl.ds(i*block,block)
        q=q_ref[rows,:]; do=do_ref[rows,:]; lse=lse_ref[rows,:]
        prod=do.astype(F32)*att_ref[rows,:].astype(F32)
        n=(i+1)*block
        keys=k_ref[pl.ds(0,n),:]; vals=v_ref[pl.ds(0,n),:]
        dq=jnp.zeros((block,width),F32)
        dk=None
        for h,mask in enumerate(masks):
            qh=jnp.where(mask,q,jnp.zeros_like(q)); dh=jnp.where(mask,do,jnp.zeros_like(do))
            delta=jnp.sum(jnp.where(mask,prod,0.0),axis=1,keepdims=True)
            lse_h=lse[:,h*HEAD_DIM:h*HEAD_DIM+1]
            s=dot_nt(qh,keys)
            p=jnp.exp(s-lse_h)
            if i==0:
                p=jnp.where(row>=col,p,0.0)
            else:
                p=jnp.concatenate([p[:,:n-block],jnp.where(row>=col,p[:,n-block:],0.0)],axis=1)
            dp=dot_nt(dh,vals)
            ds=(p*(dp-delta)).astype(LOW)
            pl_low=p.astype(LOW)
            dq=jnp.where(mask,dot_nn(ds,keys),dq)
            tk=dot_tn(ds,qh); tv=dot_tn(pl_low,dh)
            dk=tk if dk is None else dk+tk
            dv=tv if h==0 else dv+tv
        dq_acc[rows,:]=dq*(1.0/math.sqrt(HEAD_DIM))
        if i==count-1:
            dk_acc[...]=dk; dv_acc[...]=dv
        else:
            dk_acc[pl.ds(0,n),:]+=dk; dv_acc[pl.ds(0,n),:]+=dv
    def back(v):
        return v*table_ref[0]+pltpu.roll(v*table_ref[1],half,1)+pltpu.roll(v*table_ref[2],width-half,1)
    out_ref[0]=back(dq_acc[...]).astype(LOW)
    out_ref[1]=back(dk_acc[...]).astype(LOW)
    out_ref[2]=dv_acc[...].astype(LOW)

def attend_back(q,k,v,att,lse,grad,tables,seqs,length,block=256):
    pair,rows,cols=q.shape
    width=min(cols,128); groups=cols//width
    spec=pl.BlockSpec((None,length,width),lambda o,s,g:(o,s,g))
    return pl.pallas_call(
        lambda *r: bwd_kernel(block,*r),
        grid=(pair,seqs,groups),
        in_specs=[spec]*6+[pl.BlockSpec((3,length,width),lambda o,s,g:(0,0,0))],
        out_specs=pl.BlockSpec((None,3,length,width),lambda o,s,g:(o,0,s,g)),
        out_shape=jax.ShapeDtypeStruct((pair,3,rows,cols),LOW),
        scratch_shapes=[pltpu.VMEM((length,width),F32)]*3,
        compiler_params=pltpu.CompilerParams(vmem_limit_bytes=48<<20),
        cost_estimate=light(flops=int(10*pair*rows*length*cols*0.6),bytes_accessed=pair*rows*cols*20,transcendentals=pair*rows*length*cols//128),
        name="attend_back",
    )(q,k,v,att,lse,grad,tables)


VMEM_BYTES = 56 << 20
FORMS = {"nn": dot_nn, "nt": dot_nt, "tn": dot_tn}
ANYWHERE = pl.BlockSpec(memory_space=pl.ANY)


def tiles(size, most):
    while size > most and size % 2 == 0:
        size //= 2
    return size


def lead_spec(lead, block, where):
    return pl.BlockSpec((None,) * len(lead) + block, lambda *at: lead + where(*at))


def products(kind, terms, row_tile, col_tile, name, count=None, dtype=LOW, behind=()):
    one, _, two, _ = terms[0]
    deep = one.shape[-2] if kind == "tn" else one.shape[-1]
    rows = one.shape[-1] if kind == "tn" else one.shape[-2]
    cols = two.shape[-2] if kind == "nt" else two.shape[-1]
    tm, tn = tiles(rows, row_tile), tiles(cols, col_tile)
    one_block = ((deep, tm), lambda c, i, j: (0, i)) if kind == "tn" else ((tm, deep), lambda c, i, j: (i, 0))
    two_block = ((tn, deep), lambda c, i, j: (j, 0)) if kind == "nt" else ((deep, tn), lambda c, i, j: (0, j))
    number = len(terms)

    def kernel(*refs):
        total = sum(FORMS[kind](a[...], b[...]) for a, b in zip(refs[:number], refs[number : 2 * number]))
        refs[-1][...] = total.astype(dtype)

    if count is None:
        ones = [lead_spec(t[1], *one_block) for t in terms]
        out_spec = pl.BlockSpec((tm, tn), lambda c, i, j: (i, j))
        out_shape = (rows, cols)
    else:
        ones = [pl.BlockSpec((None,) + one_block[0], lambda c, i, j: (c,) + one_block[1](c, i, j)) for t in terms]
        out_spec = pl.BlockSpec((None, tm, tn), lambda c, i, j: (c, i, j))
        out_shape = (count, rows, cols)
    many = count or 1
    return pl.pallas_call(
        kernel,
        grid=(many, rows // tm, cols // tn),
        in_specs=ones + [lead_spec(t[3], *two_block) for t in terms] + [ANYWHERE] * len(behind),
        out_specs=out_spec,
        out_shape=jax.ShapeDtypeStruct(out_shape, dtype),
        compiler_params=pltpu.CompilerParams(vmem_limit_bytes=VMEM_BYTES),
        cost_estimate=light(
            flops=2 * rows * deep * cols * number * many,
            bytes_accessed=2 * (many * number * (rows * deep + deep * cols) + many * rows * cols),
            transcendentals=0,
        ),
        name=name,
    )(*[t[0] for t in terms], *[t[2] for t in terms], *behind)


def products_apart(place, kind, terms, col_tile, name, behind=()):
    one, _, two, _ = terms[0]
    deep = one.shape[-2] if kind == "tn" else one.shape[-1]
    rows = one.shape[-1] if kind == "tn" else one.shape[-2]
    cols = two.shape[-2] if kind == "nt" else two.shape[-1]
    tn = tiles(cols // 2, col_tile)
    half = cols // 2 // tn
    piece = rows // 4
    one_block = ((deep, rows), lambda j, at: (0, 0)) if kind == "tn" else ((rows, deep), lambda j, at: (0, 0))
    two_block = ((tn, deep), lambda j, at: (j, 0)) if kind == "nt" else ((deep, tn), lambda j, at: (0, j))
    number = len(terms)

    def kernel(at_ref, *refs):
        total = sum(FORMS[kind](a[...], b[...]) for a, b in zip(refs[:number], refs[number : 2 * number]))
        keep_first, send_first, keep_second, send_second, held = refs[-5:]
        held[...] = total.astype(LOW).reshape(held.shape)
        x, y = at_ref[0], at_ref[1]

        @pl.when(pl.program_id(0) < half)
        def _():
            for other in range(2):
                across = y if other == 0 else 1 - y
                keep_first[other] = held[2 * x + across]
                send_first[other] = held[2 * (1 - x) + across]

        @pl.when(pl.program_id(0) >= half)
        def _():
            for other in range(2):
                along = x if other == 0 else 1 - x
                keep_second[other] = held[2 * along + y]
                send_second[other] = held[2 * along + 1 - y]

    first = pl.BlockSpec((2, piece, tn), lambda j, at: (0, 0, jnp.minimum(j, half - 1)))
    second = pl.BlockSpec((2, piece, tn), lambda j, at: (0, 0, jnp.maximum(j - half, 0)))
    return pl.pallas_call(
        kernel,
        grid_spec=pltpu.PrefetchScalarGridSpec(
            num_scalar_prefetch=1,
            grid=(2 * half,),
            in_specs=[lead_spec(t[1], *one_block) for t in terms]
            + [lead_spec(t[3], *two_block) for t in terms]
            + [ANYWHERE] * len(behind),
            out_specs=[first, first, second, second],
            scratch_shapes=[pltpu.VMEM((4, piece, tn), LOW)],
        ),
        out_shape=[jax.ShapeDtypeStruct((2, piece, cols // 2), LOW)] * 4,
        compiler_params=pltpu.CompilerParams(vmem_limit_bytes=VMEM_BYTES),
        cost_estimate=light(
            flops=2 * rows * deep * cols * number,
            bytes_accessed=2 * (number * (rows * deep + deep * cols) + rows * cols),
            transcendentals=0,
        ),
        name=name,
    )(jnp.stack([place.x, place.y]).astype(jnp.int32), *[t[0] for t in terms], *[t[2] for t in terms], *behind)


def gate_kernel(weight_ref, rows_ref, turned_ref, slope_ref, hidden_ref):
    rows = rows_ref[...]
    gate = dot_nt(weight_ref[0], rows)
    up = dot_nt(weight_ref[1], rows)
    sig = 1.0 / (1.0 + jnp.exp(-gate))
    act = gate * sig
    hidden = (act * up).astype(LOW)
    turned_ref[...] = hidden
    hidden_ref[...] = hidden.T
    slope_ref[0] = (up * sig * (1.0 + gate * (1.0 - sig))).astype(LOW)
    slope_ref[1] = act.astype(LOW)


def gate_up(values, weight):
    rows, feat = values.shape
    units = weight.shape[1]
    tm = tiles(rows, 512)
    return pl.pallas_call(
        gate_kernel,
        grid=(rows // tm,),
        in_specs=[
            pl.BlockSpec((2, units, feat), lambda i: (0, 0, 0)),
            pl.BlockSpec((tm, feat), lambda i: (i, 0)),
        ],
        out_specs=[
            pl.BlockSpec((units, tm), lambda i: (0, i)),
            pl.BlockSpec((2, units, tm), lambda i: (0, 0, i)),
            pl.BlockSpec((tm, units), lambda i: (i, 0)),
        ],
        out_shape=[
            jax.ShapeDtypeStruct((units, rows), LOW),
            jax.ShapeDtypeStruct((2, units, rows), LOW),
            jax.ShapeDtypeStruct((rows, units), LOW),
        ],
        compiler_params=pltpu.CompilerParams(vmem_limit_bytes=VMEM_BYTES),
        cost_estimate=light(
            flops=4 * rows * feat * units,
            bytes_accessed=2 * (rows * feat + 2 * feat * units + 4 * rows * units),
            transcendentals=rows * units,
        ),
        name="gate_up",
    )(weight, values)


def hidden_back_kernel(weight_ref, grad_ref, slope_ref, *refs):
    turned_ref, out_ref = refs[-2:]
    grad = dot_nt(weight_ref[...], grad_ref[...])
    for c in range(2):
        part = (grad * slope_ref[c].astype(F32)).astype(LOW)
        turned_ref[c] = part
        out_ref[c] = part.T


def hidden_back(grad, weight, slope, behind=()):
    rows, feat = grad.shape
    units = weight.shape[0]
    tm = tiles(rows, 512)
    return pl.pallas_call(
        hidden_back_kernel,
        grid=(rows // tm,),
        in_specs=[
            pl.BlockSpec((units, feat), lambda i: (0, 0)),
            pl.BlockSpec((tm, feat), lambda i: (i, 0)),
            pl.BlockSpec((2, units, tm), lambda i: (0, 0, i)),
        ]
        + [ANYWHERE] * len(behind),
        out_specs=[
            pl.BlockSpec((2, units, tm), lambda i: (0, 0, i)),
            pl.BlockSpec((2, tm, units), lambda i: (0, i, 0)),
        ],
        out_shape=[
            jax.ShapeDtypeStruct((2, units, rows), LOW),
            jax.ShapeDtypeStruct((2, rows, units), LOW),
        ],
        compiler_params=pltpu.CompilerParams(vmem_limit_bytes=VMEM_BYTES),
        cost_estimate=light(
            flops=2 * rows * feat * units,
            bytes_accessed=2 * (rows * feat + feat * units + 6 * rows * units),
            transcendentals=0,
        ),
        name="hidden_back",
    )(weight, grad, slope, *behind)


def pieces_of(places, rows, feat, dtype, body, name, operands, behind=()):
    def kernel(at_ref, *refs):
        for step in range(len(places)):
            pl.when(pl.program_id(0) == step)(lambda step=step: body(step, refs, refs[-1]))

    specs = [pl.BlockSpec(v.shape, lambda i, at, n=v.ndim: (0,) * n) for v in operands]
    return pl.pallas_call(
        kernel,
        grid_spec=pltpu.PrefetchScalarGridSpec(
            num_scalar_prefetch=1,
            grid=(len(places),),
            in_specs=specs + [ANYWHERE] * len(behind),
            out_specs=pl.BlockSpec((None, rows, feat), lambda i, at: (at[i], 0, 0)),
        ),
        out_shape=jax.ShapeDtypeStruct((len(places), rows, feat), dtype),
        compiler_params=pltpu.CompilerParams(vmem_limit_bytes=VMEM_BYTES),
        cost_estimate=light(flops=0, bytes_accessed=4 * len(places) * rows * feat, transcendentals=0),
        name=name,
    )(jnp.stack(places).astype(jnp.int32), *operands, *behind)


def lay_rows(one, two, own, over_one, over_two, far, dtype, behind=()):
    rows, feat = own.shape

    def body(step, refs, out_ref):
        start = 0
        for ref in refs[step : step + 1] if step < 3 else refs[3 : 3 + len(far)]:
            out_ref[:, start : start + ref.shape[1]] = ref[...].astype(dtype)
            start += ref.shape[1]

    places = [2 * one + two, 2 * (1 - one) + two, 2 * one + 1 - two, 2 * (1 - one) + 1 - two]
    return pieces_of(places, rows, feat, dtype, body, "lay_rows", [own, over_one, over_two] + list(far), behind)


def norm_first(places, pieces, gain, shift, behind=()):
    rows, feat = pieces[0].shape

    def body(step, refs, out_ref):
        values = refs[step][...].astype(F32)
        out_ref[...] = (centre(values)[0] * refs[4][...] + refs[5][...]).astype(LOW)

    return pieces_of(places, rows, feat, LOW, body, "norm_first", pieces + [gain, shift], behind).reshape(-1, feat)


def lay_pieces(places, pieces, behind=()):
    rows, feat = pieces[0].shape

    def body(step, refs, out_ref):
        out_ref[...] = refs[step][...]

    return pieces_of(places, rows, feat, LOW, body, "lay_pieces", pieces, behind).reshape(-1, feat)


def join(keep_first, came_first, keep_second, came_second, behind=()):
    _, rows, half = keep_first.shape

    def kernel(one, two, three, four, *refs):
        first_stays, first_goes, second_stays, second_goes = refs[-4:]
        first_stays[...] = one[0].astype(F32) + two[0].astype(F32)
        first_goes[...] = (one[1].astype(F32) + two[1].astype(F32)).astype(LOW)
        second_stays[...] = three[0].astype(F32) + four[0].astype(F32)
        second_goes[...] = (three[1].astype(F32) + four[1].astype(F32)).astype(LOW)

    tm = tiles(rows, 128)
    pair = pl.BlockSpec((2, tm, half), lambda i: (0, i, 0))
    flat = pl.BlockSpec((tm, half), lambda i: (i, 0))
    shape = lambda dtype: jax.ShapeDtypeStruct((rows, half), dtype)
    return pl.pallas_call(
        kernel,
        grid=(rows // tm,),
        in_specs=[pair] * 4 + [ANYWHERE] * len(behind),
        out_specs=[flat] * 4,
        out_shape=[shape(F32), shape(LOW)] * 2,
        cost_estimate=light(flops=4 * rows * half, bytes_accessed=28 * rows * half, transcendentals=0),
        compiler_params=pltpu.CompilerParams(vmem_limit_bytes=VMEM_BYTES),
        name="join",
    )(keep_first, came_first, keep_second, came_second, *behind)


def on_rows(kernel, shares, values, tables, outs, sums, name, behind=()):
    rows, half = shares[0].shape
    feat = 2 * half
    tm = tiles(rows, 128)
    count, tabled = len(values), len(tables)

    def body(*refs):
        total = jnp.concatenate(
            [refs[0][...] + refs[1][...].astype(F32), refs[2][...] + refs[3][...].astype(F32)], axis=1
        )
        rest = refs[4 + count + tabled + len(behind) :]
        kernel(total, refs[4 : 4 + count], refs[4 + count : 4 + count + tabled], rest[: len(outs)], rest[len(outs) :])

    block = lambda cols: pl.BlockSpec((tm, cols), lambda i: (i, 0))
    return pl.pallas_call(
        body,
        grid=(rows // tm,),
        in_specs=[block(half)] * 4
        + [block(feat)] * count
        + [pl.BlockSpec((1, feat), lambda i: (0, 0))] * tabled
        + [ANYWHERE] * len(behind),
        out_specs=[block(feat)] * len(outs) + [pl.BlockSpec((2, feat), lambda i: (0, 0))] * sums,
        out_shape=[jax.ShapeDtypeStruct((rows, feat), dtype) for dtype in outs]
        + [jax.ShapeDtypeStruct((2, feat), F32)] * sums,
        cost_estimate=light(flops=20 * rows * feat, bytes_accessed=20 * rows * feat, transcendentals=0),
        compiler_params=pltpu.CompilerParams(vmem_limit_bytes=VMEM_BYTES),
        name=name,
    )(*shares, *values, *tables, *behind)


def centre(values):
    centred = values - jnp.mean(values, axis=1, keepdims=True)
    inv_std = lax.rsqrt(jnp.mean(centred * centred, axis=1, keepdims=True) + EPSILON)
    return centred * inv_std, inv_std


def add_norm(shares, values, gain, shift, behind=()):
    def kernel(total, value_refs, table_refs, out_refs, _):
        middle = value_refs[0][...].astype(F32) + total
        out_refs[0][...] = middle
        out_refs[1][...] = (centre(middle)[0] * table_refs[0][...] + table_refs[1][...]).astype(LOW)

    return on_rows(kernel, shares, [values], [gain, shift], [F32, LOW], 0, "add_norm", behind)


def add_low(shares, values, behind=()):
    def kernel(total, value_refs, _, out_refs, __):
        out_refs[0][...] = (value_refs[0][...].astype(F32) + total).astype(LOW)

    return on_rows(kernel, shares, [values], [], [LOW], 0, "add_low", behind)[0]


def norm_back(shares, values, gain, grad, outs, behind=()):
    def kernel(total, value_refs, table_refs, out_refs, sum_refs):
        scaled, inv_std = centre(value_refs[0][...].astype(F32))
        part = total * table_refs[0][...]
        first = jnp.mean(part, axis=1, keepdims=True)
        second = jnp.mean(part * scaled, axis=1, keepdims=True)
        result = value_refs[1][...].astype(F32) + inv_std * (part - first - scaled * second)
        for ref in out_refs:
            ref[...] = result.astype(ref.dtype)
        sums = sum_refs[0]

        @pl.when(pl.program_id(0) == 0)
        def _():
            sums[...] = jnp.zeros_like(sums)

        sums[0:1, :] += jnp.sum(total * scaled, axis=0, keepdims=True)
        sums[1:2, :] += jnp.sum(total, axis=0, keepdims=True)

    return on_rows(kernel, shares, [values, grad], [gain], outs, 1, "norm_back", behind)


def qkv_back(mine, theirs, my_grad, their_grad, behind=()):
    rows, feat = mine.shape
    count, _, cols = my_grad.shape
    tm = tiles(feat, 512)

    def kernel(mine_ref, theirs_ref, my_ref, their_ref, *refs):
        one, two = mine_ref[...].T, theirs_ref[...].T
        for c in range(count):
            refs[-1][c] = (dot_nn(one, my_ref[c]) + dot_nn(two, their_ref[c])).astype(LOW)

    tall = pl.BlockSpec((rows, tm), lambda i: (0, i))
    whole = pl.BlockSpec((count, rows, cols), lambda i: (0, 0, 0))
    return pl.pallas_call(
        kernel,
        grid=(feat // tm,),
        in_specs=[tall, tall, whole, whole] + [ANYWHERE] * len(behind),
        out_specs=pl.BlockSpec((count, tm, cols), lambda i: (0, i, 0)),
        out_shape=jax.ShapeDtypeStruct((count, feat, cols), LOW),
        cost_estimate=light(
            flops=4 * count * rows * feat * cols,
            bytes_accessed=4 * rows * feat + 4 * count * rows * cols + 2 * count * feat * cols,
            transcendentals=0,
        ),
        compiler_params=pltpu.CompilerParams(vmem_limit_bytes=VMEM_BYTES),
        name="grad_qkv",
    )(mine, theirs, my_grad, their_grad, *behind)


class Place:
    def __init__(self):
        self.fsdp = lax.axis_size("fsdp")
        self.context = lax.axis_size("context")
        self.tensor = lax.axis_size("tensor")
        self.pairs = self.tensor // 2
        self.z = lax.axis_index("fsdp")
        self.x = lax.axis_index("context")
        self.t = lax.axis_index("tensor")
        self.y = self.t // 2
        self.core = self.t % 2

    def square(self, seqs):
        return self.context == 2 and self.pairs == 2 and seqs == 1

    def size(self, which):
        return self.context if which == "x" else self.pairs

    def at(self, which):
        return self.x if which == "x" else self.y

    def shift(self, value, which, step):
        if which == "z":
            n = self.fsdp
            return lax.ppermute(value, "fsdp", [(i, (i + step) % n) for i in range(n)])
        if which == "x":
            n = self.context
            return lax.ppermute(value, "context", [(i, (i + step) % n) for i in range(n)])
        n = self.tensor
        return lax.ppermute(value, "tensor", [(i, (i + 2 * step) % n) for i in range(n)])

    def swap(self, value):
        return lax.ppermute(value, "tensor", [(i, i ^ 1) for i in range(self.tensor)])


def pick(value, index, axis):
    return lax.dynamic_index_in_dim(value, index, axis, keepdims=False)


def scatter_stage(place, value, axis, which):
    n, at = place.size(which), place.at(which)
    total = pick(value, at, axis).astype(F32)
    for step in range(1, n):
        sent = pick(value, (at + step) % n, axis)
        total = total + place.shift(sent, which, step).astype(F32)
    return total


def gather_stage(place, value, axis, which):
    n, at = place.size(which), place.at(which)
    if n == 1:
        return value
    if n == 2:
        return ordered(at, value, place.shift(value, which, 1), axis)
    parts = [value] + [place.shift(value, which, step) for step in range(1, n)]
    order = (at - jnp.arange(n)) % n
    shape = list(value.shape)
    shape[axis] = n * shape[axis]
    return jnp.take(jnp.stack(parts, axis), order, axis=axis).reshape(shape)


class Gathered:
    def __init__(self, place, value, axis):
        self.place, self.value, self.axis = place, value, axis
        if place.context == 2:
            self.raw = place.shift(value, "x", 1)
        else:
            self.raw = gather_stage(place, value, axis, "x")

    def whole(self):
        if self.place.context != 2:
            return self.raw
        return ordered(self.place.x, self.value, self.raw, self.axis)


def ordered(at, mine, other, axis):
    first = jnp.where(at == 0, mine, other)
    second = jnp.where(at == 0, other, mine)
    return jnp.concatenate([first, second], axis=axis)


def after(value, *others):
    return lax.optimization_barrier((value,) + others)[0]


class RowSum:
    def __init__(self, place, kind, terms, seqs, name, behind=()):
        self.place = place
        self.square = place.square(seqs)
        if self.square:
            self.keep_first, self.sent, self.keep_second, self.second = products_apart(
                place, kind, terms, 512, name, behind
            )
            return
        value = self.sent = products(kind, terms, 1024, 512, name, behind=behind)
        feat = value.shape[1]
        value = value.reshape(seqs, place.context, place.pairs, -1, feat)
        first, second = value[..., : feat // 2], value[..., feat // 2 :]
        first = scatter_stage(place, first, 1, "x").astype(LOW)
        second = scatter_stage(place, second, 2, "y").astype(LOW)
        first = scatter_stage(place, first, 1, "y").reshape(-1, feat // 2)
        second = scatter_stage(place, second, 1, "x").reshape(-1, feat // 2)
        nothing = jnp.zeros(first.shape, LOW)
        self.shares = [first, nothing, second, nothing]

    def start(self, *others):
        if self.square:
            first, second = after((self.sent, self.second), *others) if others else (self.sent, self.second)
            self.came_first = self.place.shift(first, "x", 1)
            self.came_second = self.place.shift(second, "y", 1)
        return self

    def follow(self, behind=()):
        if not self.square:
            return self.shares[0]
        first, first_goes, second, second_goes = join(
            self.keep_first, self.came_first, self.keep_second, self.came_second, behind
        )
        self.shares = [first, self.place.shift(first_goes, "y", 1), second, self.place.shift(second_goes, "x", 1)]
        return first


def spread_rows(place, value, seqs, behind=()):
    feat = value.shape[-1]
    half = feat // 2
    if place.square(seqs):
        over_x = place.shift(value, "x", 1)
        over_y = place.shift(value, "y", 1)
        far_first = place.shift(over_y[:, :half], "x", 1)
        far_second = place.shift(over_x[:, half:], "y", 1)
        whole = lay_rows(place.x, place.y, value, over_x, over_y, [far_first, far_second], LOW, behind)
        return whole.reshape(-1, feat)
    value = value.reshape(seqs, -1, feat)
    rows = value.shape[1]
    first, second = value[..., :half], value[..., half:]
    first = gather_stage(place, first, 1, "y")
    second = gather_stage(place, second, 1, "x")
    first = gather_stage(place, first, 1, "x")
    second = second.reshape(seqs, place.context, rows, half)
    second = gather_stage(place, second, 2, "y").reshape(first.shape)
    return jnp.concatenate([first, second], axis=-1).reshape(-1, feat)


def whole_rows(place, value, seqs, dtype, behind=()):
    feat = value.shape[-1]
    if place.square(seqs):
        over_y, over_core = place.shift(value, "y", 1), place.swap(value)
        whole = lay_rows(place.core, place.y, value, over_core, over_y, [place.swap(over_y)], dtype, behind)
        return whole.reshape(2, -1, feat), over_y
    value = gather_stage(place, value.reshape(seqs, -1, feat), 1, "y")
    return ordered(place.core, value, place.swap(value), 0).astype(dtype), value


def other_rows(place, value):
    rows = value.shape[0] // 2
    straight = place.shift(lax.dynamic_slice_in_dim(value, place.y * rows, rows, 0), "x", 1)
    return [value[:rows], value[rows:], straight, place.shift(straight, "y", 1)]


def other_places(place):
    x, y = place.x, place.y
    return [2 * x, 2 * x + 1, 2 * (1 - x) + y, 2 * (1 - x) + 1 - y]


def empty_kernel(*refs):
    pass


def empty(shape, dtype, behind=()):
    return pl.pallas_call(
        empty_kernel,
        in_specs=[ANYWHERE] * len(behind),
        out_specs=ANYWHERE,
        out_shape=jax.ShapeDtypeStruct(shape, dtype),
        name="empty",
    )(*behind)


def lay_shards(place, shard, before, behind, low, high, ready):
    n, z = place.fsdp, place.z
    blocks, size, cols = shard.shape
    whole = empty((blocks, n * size, cols), shard.dtype, ready)
    for part, block, start in (
        (shard, 0, z),
        (before[:, :size], 0, (z + 3) % n),
        (behind[:, :size], 0, (z + 1) % n),
        (low[:, :size], 0, (z + 2) % n),
        (high, blocks // 2, (z + 2) % n),
    ):
        whole = lax.dynamic_update_slice(whole, part, (block, start * size, 0))
    return whole


class Shards:
    def __init__(self, place, grad, axis, half_axis, begin):
        self.place, self.grad, self.axis, self.half_axis = place, grad, axis, half_axis
        self.size = grad.shape[axis] // place.fsdp
        self.half = (self.size if axis == half_axis else grad.shape[half_axis]) // 2

        def pair(one, two):
            return after(jnp.stack([one, two]).astype(LOW), begin)

        self.left = place.shift(pair(self.part(2, 1), self.part(1, 0)), "z", 1)
        self.right = place.shift(pair(self.part(2, 0), self.part(3, 1)), "z", -1)

    def part(self, ahead, side):
        place, half = self.place, self.half
        start = (place.z + ahead) % place.fsdp * self.size
        shard = lax.dynamic_slice_in_dim(self.grad, start, self.size, self.axis)
        return lax.slice_in_dim(shard, side * half, (side + 1) * half, axis=self.half_axis).astype(F32)

    def follow(self, *ready):
        place = self.place
        self.left, self.right = after((self.left, self.right), *ready)
        high = (self.part(1, 1) + self.left[0].astype(F32)).astype(LOW)
        low = (self.part(3, 0) + self.right[0].astype(F32)).astype(LOW)
        self.high, self.low = place.shift(high, "z", 1), place.shift(low, "z", -1)
        return low

    def total(self, *ready):
        high, low = after((self.high, self.low), *ready) if ready else (self.high, self.low)
        low = self.part(0, 0) + self.left[1].astype(F32) + low.astype(F32)
        high = self.part(0, 1) + self.right[1].astype(F32) + high.astype(F32)
        return jnp.concatenate([low.astype(LOW), high.astype(LOW)], axis=self.half_axis)


def total_over(place, value, which):
    n = {"z": place.fsdp, "x": place.context, "y": place.pairs, "core": 2}[which]
    if n == 1:
        return value
    if which == "core":
        return value + place.swap(value)
    if n == 2:
        return value + place.shift(value, which, 1)
    at = {"z": place.z, "x": place.x, "y": place.y}[which]
    parts = jnp.zeros((n,) + value.shape, value.dtype)
    parts = lax.dynamic_update_index_in_dim(parts, value, at, 0)
    for step in range(1, n):
        sent = place.shift(value, which, step)
        parts = lax.dynamic_update_index_in_dim(parts, sent, (at - step) % n, 0)
    return jnp.sum(parts, axis=0)


def small_totals(place, sums, bias, bias_other):
    n, z = place.fsdp, place.z
    feat = sums.shape[1]
    pad = [(0, 1), (0, 0)]
    sent = place.swap(jnp.concatenate([sums, jnp.pad(bias_other, pad)], axis=1))
    sums, bias = sums + sent[:, :feat], jnp.pad(bias, pad) + sent[:, feat:]
    size = feat // n
    came = []
    for step in range(n):
        part = lax.dynamic_slice_in_dim(sums, (z + step) % n * size, size, 1)
        part = jnp.concatenate([part, bias], axis=1)
        came.append(place.shift(part, "z", step) if step else part)
    came = lax.optimization_barrier(tuple(came))
    parts = jnp.zeros((n,) + came[0].shape, F32)
    for step in range(n):
        parts = lax.dynamic_update_index_in_dim(parts, came[step], (z - step) % n, 0)
    return jnp.sum(parts, axis=0)


def last_totals(place, totals, size):
    if place.context == 2:
        sent = place.shift(totals, "x", 1)
        return totals[:, :size] + sent[:, :size], ordered(place.x, totals[:3, size:], sent[:3, size:], 1)
    return total_over(place, totals[:, :size], "x"), gather_stage(place, totals[:3, size:], 1, "x")


def local(
    hidden_in,
    norm_gains,
    norm_biases,
    qkv_weight,
    qkv_bias,
    out_weight,
    gate_up_weight,
    down_weight,
    cotangent,
):
    place = Place()
    all_seqs, part_rows, feat = hidden_in.shape
    seqs = all_seqs // 2
    length = part_rows * place.context
    own_rows = part_rows // place.pairs
    head_cols = qkv_bias.shape[1] // place.context
    hidden_cols = down_weight.shape[0] // place.context

    def columns(value, count, axis):
        return lax.dynamic_slice_in_dim(value, place.x * count, count, axis)

    def own_sequences(value):
        return lax.dynamic_slice_in_dim(value, place.core * seqs, seqs, 0)

    def own_piece(value):
        return lax.dynamic_slice_in_dim(value, place.y * own_rows, own_rows, 1)

    pack = jnp.concatenate(
        [columns(qkv_weight, head_cols, 2), columns(out_weight, head_cols, 0).T[None]]
    )
    norm_part = jnp.concatenate([norm_gains, norm_biases]).reshape(-1, head_cols)
    norm_rows = norm_part.shape[0]
    pad = -norm_rows % 16
    part_feat = pack.shape[1]
    norm_block = jnp.pad(norm_part, [(0, pad), (0, 0)])[None]
    extra = jnp.pad(norm_block, [(0, 3), (0, 0), (0, 0)])
    pack = jnp.concatenate([pack, extra], axis=1)
    pack_before, pack_behind = place.shift(pack, "z", 1), place.shift(pack, "z", -1)
    bias = columns(qkv_bias, head_cols, 1)
    bias_swapped = place.swap(bias)
    bias_other = bias_swapped.astype(F32)[None, :, None, :]
    bias = bias.astype(F32)[None, :, None, :]
    hidden_mine = own_sequences(hidden_in).reshape(-1, feat)
    top_mine = own_sequences(cotangent)
    if place.square(seqs):
        pieces = other_rows(place, hidden_mine)
        top_pieces = other_rows(place, top_mine.reshape(-1, feat))
        pack_before, pack_behind = after((pack_before, pack_behind), pieces[2], bias_swapped)
    else:
        whole = gather_stage(place, hidden_mine.reshape(seqs, -1, feat), 1, "x").reshape(-1, feat)
        pieces = top_pieces = [whole] * 4
    half = pack.shape[0] // 2
    pack_low = place.shift(pack_before[:half], "z", 1)
    pack_high = place.shift(pack_behind[half:, :part_feat], "z", -1)
    norms = jnp.zeros((2, 2, feat), F32)
    for step, piece in (
        (0, norm_block),
        (1, pack_before[:1, part_feat:]),
        (2, pack_low[:1, part_feat:]),
        (3, pack_behind[:1, part_feat:]),
    ):
        piece = piece[0, :norm_rows].reshape(2, 2, part_feat).astype(F32)
        norms = lax.dynamic_update_slice(norms, piece, (0, 0, (place.z - step) % place.fsdp * part_feat))
    gains, shifts = norms[0][:, None, :], norms[1][:, None, :]
    gate_up_part = columns(gate_up_weight, hidden_cols, 2).transpose(0, 2, 1)
    down_part = columns(down_weight, hidden_cols, 0)
    if place.square(seqs):
        normed = norm_first(other_places(place), pieces, gains[0], shifts[0])
        top_last = top_pieces[3]
    else:
        normed = (centre(whole.astype(F32))[0] * gains[0] + shifts[0]).astype(LOW)
        grad_top = top_last = gather_stage(place, top_mine, 1, "x").reshape(seqs * length, feat)
    w_attn = lay_shards(place, pack[:, :part_feat], pack_before, pack_behind, pack_low, after(pack_high, normed), [pieces[3], gate_up_part, down_part])
    gate_up_part, down_part = after((gate_up_part, down_part), pack_low, pack_high, top_pieces[2])
    w_gate_up = lax.all_gather(gate_up_part, "fsdp", axis=2, tiled=True)
    w_down = lax.all_gather(down_part, "fsdp", axis=1, tiled=True)
    tables = rotary_tables(length, min(head_cols, 128))
    w_attn_other = place.swap(w_attn)

    def attend(weight, bias, behind):
        mixed = jnp.einsum("rd,cde->cre", normed, weight[:3], preferred_element_type=F32)
        return attend_forward(mixed[None], bias, tables, seqs, length, behind)

    kept = attend(w_attn, bias, [])
    kept_other = attend(w_attn_other, bias_other, [kept[3], top_last])
    attended, attended_other = kept[3][0], kept_other[3][0]
    attn_sum = RowSum(
        place,
        "nt",
        [(attended, (), w_attn, (3,)), (attended_other, (), w_attn_other, (3,))],
        seqs,
        "out",
    ).start()
    if place.square(seqs):
        grad_top = lay_pieces(other_places(place), top_pieces, [attn_sum.sent])
    theirs_top, theirs_one, theirs_attended = place.swap(grad_top), place.swap(normed), place.swap(attended_other)
    attn_sum.follow([grad_top])
    inputs = own_piece(hidden_mine.reshape(seqs, -1, feat)).reshape(-1, feat)
    middle, normed_two = add_norm(
        attn_sum.shares, inputs, gains[1], shifts[1], behind=[theirs_attended]
    )
    normed_two = spread_rows(place, normed_two, seqs, [theirs_top, theirs_one])

    w_gate_up_other = place.swap(after(w_gate_up, middle))
    turned_other, slope_other, hidden_part = gate_up(normed_two, w_gate_up_other)
    theirs_turned, w_down_other = place.swap(turned_other), place.swap(after(w_down, turned_other))
    turned, slope, hidden = gate_up(normed_two, w_gate_up)
    grad_down = products(
        "nn",
        [(turned, (), grad_top, ()), (theirs_turned, (), theirs_top, ())],
        hidden_cols,
        512,
        "grad_down",
    )
    down_sum = lax.psum_scatter(grad_down, "fsdp", scatter_dimension=1, tiled=True)
    grad_gu_turned_other, grad_gu_other = hidden_back(grad_top, w_down_other, slope_other, [grad_down])
    theirs_gu, theirs_two = place.swap(grad_gu_turned_other), place.swap(normed_two)
    grad_gu_turned, grad_gu = hidden_back(grad_top, w_down, slope, [grad_gu_other])
    two_sum = RowSum(
        place,
        "nn",
        [(grad_gu, (c,), w_gate_up, (c,)) for c in range(2)]
        + [(grad_gu_other, (c,), w_gate_up_other, (c,)) for c in range(2)],
        seqs,
        "grad_two",
        behind=[theirs_two, theirs_gu],
    ).start()
    grad_gate_up = products(
        "nn",
        [(grad_gu_turned, (), normed_two, ()), (theirs_gu, (), theirs_two, ())],
        hidden_cols,
        512,
        "grad_gate_up",
        count=2,
        behind=[two_sum.sent],
    )
    two_next = two_sum.follow([grad_gate_up, down_sum])
    gate_up_sum = lax.psum_scatter(after(grad_gate_up, two_next), "fsdp", scatter_dimension=2, tiled=True)
    down_sums = RowSum(
        place,
        "nn",
        [(hidden, (), w_down, ()), (hidden_part, (), w_down_other, ())],
        seqs,
        "down",
        behind=[two_next],
    )
    top_rows = own_piece(top_mine).reshape(-1, feat)
    grad_middle, mid_low, sums_two = norm_back(
        two_sum.shares, middle, gains[1], top_rows, [F32, LOW], behind=[down_sums.sent]
    )
    grad_mid_low = spread_rows(place, mid_low, seqs)
    down_whole = lax.all_gather(after(down_sum, grad_mid_low), "context", axis=0, tiled=True)
    down_sums.start(grad_mid_low)

    def attend_grad(kept, weight, behind):
        grad_att = products("nn", [(grad_mid_low, (), weight, (3,))], 1024, head_cols, "grad_att", behind=behind)
        return attend_back(*kept, grad_att[None], tables, seqs, length)[0]

    theirs_mid = place.swap(grad_mid_low)
    grad_mixed_other = attend_grad(kept_other, w_attn_other, [])
    theirs_mixed = place.swap(grad_mixed_other)
    grad_out = products(
        "tn",
        [(grad_mid_low, (), attended, ()), (theirs_mid, (), theirs_attended, ())],
        512,
        head_cols,
        "grad_out",
        behind=[grad_mixed_other],
    )
    down_next = down_sums.follow([grad_out])
    grad_mixed = attend_grad(kept, w_attn, [down_next])
    final_out = add_low(down_sums.shares, middle, behind=[grad_mixed])
    out_sum = lax.psum_scatter(grad_out, "fsdp", scatter_dimension=0, tiled=True)
    one_sum = RowSum(
        place,
        "nt",
        [(grad_mixed, (c,), w_attn, (c,)) for c in range(3)]
        + [(grad_mixed_other, (c,), w_attn_other, (c,)) for c in range(3)],
        seqs,
        "grad_one",
        behind=[final_out],
    ).start()
    grad_qkv = qkv_back(
        normed, theirs_one, grad_mixed, theirs_mixed, behind=[one_sum.sent, gate_up_sum]
    )
    qkv_shards = Shards(place, grad_qkv, 1, 1, grad_mixed)
    one_next = one_sum.follow([grad_qkv])
    qkv_next = qkv_shards.follow(one_next)
    input_low, sums_one = norm_back(
        one_sum.shares,
        inputs,
        gains[0],
        grad_middle,
        [LOW],
        behind=[one_next, qkv_next],
    )
    gate_up_whole = lax.all_gather(gate_up_sum, "context", axis=1, tiled=True)
    sums = total_over(place, jnp.concatenate([sums_one, sums_two]), "y")
    input_grad, over_y = whole_rows(place, after(input_low, sums), seqs, F32)
    totals = small_totals(
        place,
        after(sums, qkv_shards.low, qkv_shards.high),
        jnp.sum(grad_mixed.astype(F32), axis=1),
        jnp.sum(grad_mixed_other.astype(F32), axis=1),
    )
    qkv_sum = qkv_shards.total()
    qkv_gathered = Gathered(place, qkv_sum, 2)
    out_gathered = Gathered(place, after(out_sum, qkv_sum), 1)
    layer_out, _ = whole_rows(place, after(final_out, over_y), seqs, LOW)
    sums, grad_bias = last_totals(place, after(totals, qkv_sum), norm_gains.shape[1])

    return (
        layer_out,
        input_grad,
        sums[0::2],
        sums[1::2],
        qkv_gathered.whole().astype(F32),
        grad_bias,
        out_gathered.whole().T.astype(F32),
        gate_up_whole.transpose(0, 2, 1).astype(F32),
        down_whole.astype(F32),
    )


def solution(mesh):
    placed = (
        P("fsdp", "context", None),
        P(None, "fsdp"),
        P(None, "fsdp"),
        P(None, "fsdp", "tensor"),
        P(None, "tensor"),
        P("tensor", "fsdp"),
        P(None, "fsdp", "tensor"),
        P("tensor", "fsdp"),
        P("fsdp", "context", None),
    )
    return jax.shard_map(
        local,
        mesh=mesh,
        in_specs=placed,
        out_specs=(
            P("fsdp", "context", None),
            P("fsdp", "context", None),
            P(None, "fsdp"),
            P(None, "fsdp"),
            P(None, "fsdp", "tensor"),
            P(None, "tensor"),
            P("tensor", "fsdp"),
            P(None, "fsdp", "tensor"),
            P("tensor", "fsdp"),
        ),
        check_vma=False,
    )
```

```python
import math

import jax
import jax.numpy as jnp
import numpy as np
from jax import lax
from jax.experimental import pallas as pl
from jax.experimental.pallas import tpu as pltpu
from jax.sharding import PartitionSpec as P

HEAD_DIM = 64
ROT = 16
EPSILON = 1e-05
F32 = jnp.float32
LOW = jnp.bfloat16


def rotary_tables(length, width):
    column = np.arange(width) % HEAD_DIM
    half = ROT // 2
    frequency = np.power(10000.0, -2.0 * (column % half) / ROT).astype(np.float32)
    angles = np.arange(length, dtype=np.float32)[:, None] * frequency[None, :]
    inside = column < ROT
    lower = column < half
    sine = np.sin(angles)
    cosine = np.where(inside, np.cos(angles), 1.0)
    minus = np.where(lower, -sine, 0.0)
    plus = np.where(inside & ~lower, sine, 0.0)
    return jnp.asarray(np.stack([cosine, minus, plus]).astype(np.float32))

def light(flops, bytes_accessed, transcendentals):
    return pl.CostEstimate(flops=flops // 100, bytes_accessed=bytes_accessed // 100, transcendentals=0)


def dot_nt(a,b): return lax.dot_general(a,b,(((1,),(1,)),((),())),preferred_element_type=F32)
def dot_nn(a,b): return lax.dot_general(a,b,(((1,),(0,)),((),())),preferred_element_type=F32)
def dot_tn(a,b): return lax.dot_general(a,b,(((0,),(0,)),((),())),preferred_element_type=F32)

def head_masks(width):
    lane=lax.broadcasted_iota(jnp.int32,(1,width),1)
    return [ (lane//HEAD_DIM)==h for h in range(width//HEAD_DIM)]

def fwd_kernel(block, mixed_ref, bias_ref, table_ref, *refs):
    q_ref, k_ref, v_ref, att_ref, lse_ref = refs[-5:]
    length, width = q_ref.shape
    half=ROT//2
    def rotated(c):
        v=mixed_ref[c]+bias_ref[c]
        return v*table_ref[0]+pltpu.roll(v,width-half,1)*table_ref[1]+pltpu.roll(v,half,1)*table_ref[2]
    q_ref[...]=(rotated(0)*(1.0/math.sqrt(HEAD_DIM))).astype(LOW)
    k_ref[...]=rotated(1).astype(LOW)
    v_ref[...]=(mixed_ref[2]+bias_ref[2]).astype(LOW)
    masks=head_masks(width)
    row=lax.broadcasted_iota(jnp.int32,(block,block),0)
    col=lax.broadcasted_iota(jnp.int32,(block,block),1)
    for i in range(length//block):
        rows=pl.ds(i*block,block)
        q=q_ref[rows,:]
        out=jnp.zeros((block,width),F32); lse=jnp.zeros((block,width),F32)
        for mask in masks:
            qh=jnp.where(mask,q,jnp.zeros_like(q))
            diag=jnp.where(row>=col,dot_nt(qh,k_ref[rows,:]),-1e30)
            top=jnp.max(diag,axis=1,keepdims=True)
            if i>0:
                rest=dot_nt(qh,k_ref[pl.ds(0,i*block),:])
                top=jnp.maximum(top,jnp.max(rest,axis=1,keepdims=True))
            diag=jnp.exp(diag-top)
            total=jnp.sum(diag,axis=1,keepdims=True)
            acc=dot_nn(diag.astype(LOW),v_ref[rows,:])
            if i>0:
                rest=jnp.exp(rest-top)
                total=total+jnp.sum(rest,axis=1,keepdims=True)
                acc=acc+dot_nn(rest.astype(LOW),v_ref[pl.ds(0,i*block),:])
            out=jnp.where(mask,acc/total,out)
            lse=jnp.where(mask,top+jnp.log(total),lse)
        att_ref[rows,:]=out.astype(LOW)
        lse_ref[rows,:]=lse

def attend_forward(mixed,bias,tables,seqs,length,behind=(),block=256):
    pair,_,rows,cols=mixed.shape
    width=min(cols,128); groups=cols//width
    tok=lambda o,s,g:(o,s,g)
    spec=pl.BlockSpec((None,length,width),tok)
    shape=lambda d:jax.ShapeDtypeStruct((pair,rows,cols),d)
    return pl.pallas_call(
        lambda *r: fwd_kernel(block,*r),
        grid=(pair,seqs,groups),
        in_specs=[pl.BlockSpec((None,3,length,width),lambda o,s,g:(o,0,s,g)),
                  pl.BlockSpec((None,3,1,width),lambda o,s,g:(o,0,0,g)),
                  pl.BlockSpec((3,length,width),lambda o,s,g:(0,0,0))]+[pl.BlockSpec(memory_space=pl.ANY)]*len(behind),
        out_specs=[spec]*5,
        out_shape=[shape(LOW)]*4+[shape(F32)],
        compiler_params=pltpu.CompilerParams(vmem_limit_bytes=48<<20),
        cost_estimate=light(flops=int(4*pair*rows*length*cols*0.6),bytes_accessed=pair*rows*cols*26,transcendentals=pair*rows*length*cols//128),
        name="attend_forward",
    )(mixed,bias,tables,*behind)

def bwd_kernel(block,q_ref,k_ref,v_ref,att_ref,lse_ref,do_ref,table_ref,out_ref,dk_acc,dv_acc,dq_acc):
    length,width=q_ref.shape
    half=ROT//2
    masks=head_masks(width)
    row=lax.broadcasted_iota(jnp.int32,(block,block),0)
    col=lax.broadcasted_iota(jnp.int32,(block,block),1)
    count=length//block
    for i in reversed(range(count)):
        rows=pl.ds(i*block,block)
        q=q_ref[rows,:]; do=do_ref[rows,:]; lse=lse_ref[rows,:]
        prod=do.astype(F32)*att_ref[rows,:].astype(F32)
        n=(i+1)*block
        keys=k_ref[pl.ds(0,n),:]; vals=v_ref[pl.ds(0,n),:]
        dq=jnp.zeros((block,width),F32)
        dk=None
        for h,mask in enumerate(masks):
            qh=jnp.where(mask,q,jnp.zeros_like(q)); dh=jnp.where(mask,do,jnp.zeros_like(do))
            delta=jnp.sum(jnp.where(mask,prod,0.0),axis=1,keepdims=True)
            lse_h=lse[:,h*HEAD_DIM:h*HEAD_DIM+1]
            s=dot_nt(qh,keys)
            p=jnp.exp(s-lse_h)
            if i==0:
                p=jnp.where(row>=col,p,0.0)
            else:
                p=jnp.concatenate([p[:,:n-block],jnp.where(row>=col,p[:,n-block:],0.0)],axis=1)
            dp=dot_nt(dh,vals)
            ds=(p*(dp-delta)).astype(LOW)
            pl_low=p.astype(LOW)
            dq=jnp.where(mask,dot_nn(ds,keys),dq)
            tk=dot_tn(ds,qh); tv=dot_tn(pl_low,dh)
            dk=tk if dk is None else dk+tk
            dv=tv if h==0 else dv+tv
        dq_acc[rows,:]=dq*(1.0/math.sqrt(HEAD_DIM))
        if i==count-1:
            dk_acc[...]=dk; dv_acc[...]=dv
        else:
            dk_acc[pl.ds(0,n),:]+=dk; dv_acc[pl.ds(0,n),:]+=dv
    def back(v):
        return v*table_ref[0]+pltpu.roll(v*table_ref[1],half,1)+pltpu.roll(v*table_ref[2],width-half,1)
    out_ref[0]=back(dq_acc[...]).astype(LOW)
    out_ref[1]=back(dk_acc[...]).astype(LOW)
    out_ref[2]=dv_acc[...].astype(LOW)

def attend_back(q,k,v,att,lse,grad,tables,seqs,length,block=256):
    pair,rows,cols=q.shape
    width=min(cols,128); groups=cols//width
    spec=pl.BlockSpec((None,length,width),lambda o,s,g:(o,s,g))
    return pl.pallas_call(
        lambda *r: bwd_kernel(block,*r),
        grid=(pair,seqs,groups),
        in_specs=[spec]*6+[pl.BlockSpec((3,length,width),lambda o,s,g:(0,0,0))],
        out_specs=pl.BlockSpec((None,3,length,width),lambda o,s,g:(o,0,s,g)),
        out_shape=jax.ShapeDtypeStruct((pair,3,rows,cols),LOW),
        scratch_shapes=[pltpu.VMEM((length,width),F32)]*3,
        compiler_params=pltpu.CompilerParams(vmem_limit_bytes=48<<20),
        cost_estimate=light(flops=int(10*pair*rows*length*cols*0.6),bytes_accessed=pair*rows*cols*20,transcendentals=pair*rows*length*cols//128),
        name="attend_back",
    )(q,k,v,att,lse,grad,tables)


VMEM_BYTES = 56 << 20
FORMS = {"nn": dot_nn, "nt": dot_nt, "tn": dot_tn}
ANYWHERE = pl.BlockSpec(memory_space=pl.ANY)


def tiles(size, most):
    while size > most and size % 2 == 0:
        size //= 2
    return size


def lead_spec(lead, block, where):
    return pl.BlockSpec((None,) * len(lead) + block, lambda *at: lead + where(*at))


def products(kind, terms, row_tile, col_tile, name, count=None, dtype=LOW, behind=()):
    one, _, two, _ = terms[0]
    deep = one.shape[-2] if kind == "tn" else one.shape[-1]
    rows = one.shape[-1] if kind == "tn" else one.shape[-2]
    cols = two.shape[-2] if kind == "nt" else two.shape[-1]
    tm, tn = tiles(rows, row_tile), tiles(cols, col_tile)
    one_block = ((deep, tm), lambda c, i, j: (0, i)) if kind == "tn" else ((tm, deep), lambda c, i, j: (i, 0))
    two_block = ((tn, deep), lambda c, i, j: (j, 0)) if kind == "nt" else ((deep, tn), lambda c, i, j: (0, j))
    number = len(terms)

    def kernel(*refs):
        total = sum(FORMS[kind](a[...], b[...]) for a, b in zip(refs[:number], refs[number : 2 * number]))
        refs[-1][...] = total.astype(dtype)

    if count is None:
        ones = [lead_spec(t[1], *one_block) for t in terms]
        out_spec = pl.BlockSpec((tm, tn), lambda c, i, j: (i, j))
        out_shape = (rows, cols)
    else:
        ones = [pl.BlockSpec((None,) + one_block[0], lambda c, i, j: (c,) + one_block[1](c, i, j)) for t in terms]
        out_spec = pl.BlockSpec((None, tm, tn), lambda c, i, j: (c, i, j))
        out_shape = (count, rows, cols)
    many = count or 1
    return pl.pallas_call(
        kernel,
        grid=(many, rows // tm, cols // tn),
        in_specs=ones + [lead_spec(t[3], *two_block) for t in terms] + [ANYWHERE] * len(behind),
        out_specs=out_spec,
        out_shape=jax.ShapeDtypeStruct(out_shape, dtype),
        compiler_params=pltpu.CompilerParams(vmem_limit_bytes=VMEM_BYTES),
        cost_estimate=light(
            flops=2 * rows * deep * cols * number * many,
            bytes_accessed=2 * (many * number * (rows * deep + deep * cols) + many * rows * cols),
            transcendentals=0,
        ),
        name=name,
    )(*[t[0] for t in terms], *[t[2] for t in terms], *behind)


def products_apart(place, kind, terms, col_tile, name, behind=()):
    one, _, two, _ = terms[0]
    deep = one.shape[-2] if kind == "tn" else one.shape[-1]
    rows = one.shape[-1] if kind == "tn" else one.shape[-2]
    cols = two.shape[-2] if kind == "nt" else two.shape[-1]
    tn = tiles(cols // 2, col_tile)
    half = cols // 2 // tn
    piece = rows // 4
    one_block = ((deep, rows), lambda j, at: (0, 0)) if kind == "tn" else ((rows, deep), lambda j, at: (0, 0))
    two_block = ((tn, deep), lambda j, at: (j, 0)) if kind == "nt" else ((deep, tn), lambda j, at: (0, j))
    number = len(terms)

    def kernel(at_ref, *refs):
        total = sum(FORMS[kind](a[...], b[...]) for a, b in zip(refs[:number], refs[number : 2 * number]))
        keep_first, send_first, keep_second, send_second, held = refs[-5:]
        held[...] = total.astype(LOW).reshape(held.shape)
        x, y = at_ref[0], at_ref[1]

        @pl.when(pl.program_id(0) < half)
        def _():
            for other in range(2):
                across = y if other == 0 else 1 - y
                keep_first[other] = held[2 * x + across]
                send_first[other] = held[2 * (1 - x) + across]

        @pl.when(pl.program_id(0) >= half)
        def _():
            for other in range(2):
                along = x if other == 0 else 1 - x
                keep_second[other] = held[2 * along + y]
                send_second[other] = held[2 * along + 1 - y]

    first = pl.BlockSpec((2, piece, tn), lambda j, at: (0, 0, jnp.minimum(j, half - 1)))
    second = pl.BlockSpec((2, piece, tn), lambda j, at: (0, 0, jnp.maximum(j - half, 0)))
    return pl.pallas_call(
        kernel,
        grid_spec=pltpu.PrefetchScalarGridSpec(
            num_scalar_prefetch=1,
            grid=(2 * half,),
            in_specs=[lead_spec(t[1], *one_block) for t in terms]
            + [lead_spec(t[3], *two_block) for t in terms]
            + [ANYWHERE] * len(behind),
            out_specs=[first, first, second, second],
            scratch_shapes=[pltpu.VMEM((4, piece, tn), LOW)],
        ),
        out_shape=[jax.ShapeDtypeStruct((2, piece, cols // 2), LOW)] * 4,
        compiler_params=pltpu.CompilerParams(vmem_limit_bytes=VMEM_BYTES),
        cost_estimate=light(
            flops=2 * rows * deep * cols * number,
            bytes_accessed=2 * (number * (rows * deep + deep * cols) + rows * cols),
            transcendentals=0,
        ),
        name=name,
    )(jnp.stack([place.x, place.y]).astype(jnp.int32), *[t[0] for t in terms], *[t[2] for t in terms], *behind)


def gate_kernel(weight_ref, rows_ref, turned_ref, slope_ref, hidden_ref):
    rows = rows_ref[...]
    gate = dot_nt(weight_ref[0], rows)
    up = dot_nt(weight_ref[1], rows)
    sig = 1.0 / (1.0 + jnp.exp(-gate))
    act = gate * sig
    hidden = (act * up).astype(LOW)
    turned_ref[...] = hidden
    hidden_ref[...] = hidden.T
    slope_ref[0] = (up * sig * (1.0 + gate * (1.0 - sig))).astype(LOW)
    slope_ref[1] = act.astype(LOW)


def gate_up(values, weight):
    rows, feat = values.shape
    units = weight.shape[1]
    tm = tiles(rows, 512)
    return pl.pallas_call(
        gate_kernel,
        grid=(rows // tm,),
        in_specs=[
            pl.BlockSpec((2, units, feat), lambda i: (0, 0, 0)),
            pl.BlockSpec((tm, feat), lambda i: (i, 0)),
        ],
        out_specs=[
            pl.BlockSpec((units, tm), lambda i: (0, i)),
            pl.BlockSpec((2, units, tm), lambda i: (0, 0, i)),
            pl.BlockSpec((tm, units), lambda i: (i, 0)),
        ],
        out_shape=[
            jax.ShapeDtypeStruct((units, rows), LOW),
            jax.ShapeDtypeStruct((2, units, rows), LOW),
            jax.ShapeDtypeStruct((rows, units), LOW),
        ],
        compiler_params=pltpu.CompilerParams(vmem_limit_bytes=VMEM_BYTES),
        cost_estimate=light(
            flops=4 * rows * feat * units,
            bytes_accessed=2 * (rows * feat + 2 * feat * units + 4 * rows * units),
            transcendentals=rows * units,
        ),
        name="gate_up",
    )(weight, values)


def hidden_back_kernel(weight_ref, grad_ref, slope_ref, *refs):
    turned_ref, out_ref = refs[-2:]
    grad = dot_nt(weight_ref[...], grad_ref[...])
    for c in range(2):
        part = (grad * slope_ref[c].astype(F32)).astype(LOW)
        turned_ref[c] = part
        out_ref[c] = part.T


def hidden_back(grad, weight, slope, behind=()):
    rows, feat = grad.shape
    units = weight.shape[0]
    tm = tiles(rows, 512)
    return pl.pallas_call(
        hidden_back_kernel,
        grid=(rows // tm,),
        in_specs=[
            pl.BlockSpec((units, feat), lambda i: (0, 0)),
            pl.BlockSpec((tm, feat), lambda i: (i, 0)),
            pl.BlockSpec((2, units, tm), lambda i: (0, 0, i)),
        ]
        + [ANYWHERE] * len(behind),
        out_specs=[
            pl.BlockSpec((2, units, tm), lambda i: (0, 0, i)),
            pl.BlockSpec((2, tm, units), lambda i: (0, i, 0)),
        ],
        out_shape=[
            jax.ShapeDtypeStruct((2, units, rows), LOW),
            jax.ShapeDtypeStruct((2, rows, units), LOW),
        ],
        compiler_params=pltpu.CompilerParams(vmem_limit_bytes=VMEM_BYTES),
        cost_estimate=light(
            flops=2 * rows * feat * units,
            bytes_accessed=2 * (rows * feat + feat * units + 6 * rows * units),
            transcendentals=0,
        ),
        name="hidden_back",
    )(weight, grad, slope, *behind)


def pieces_of(places, rows, feat, dtype, body, name, operands, behind=()):
    def kernel(at_ref, *refs):
        for step in range(len(places)):
            pl.when(pl.program_id(0) == step)(lambda step=step: body(step, refs, refs[-1]))

    specs = [pl.BlockSpec(v.shape, lambda i, at, n=v.ndim: (0,) * n) for v in operands]
    return pl.pallas_call(
        kernel,
        grid_spec=pltpu.PrefetchScalarGridSpec(
            num_scalar_prefetch=1,
            grid=(len(places),),
            in_specs=specs + [ANYWHERE] * len(behind),
            out_specs=pl.BlockSpec((None, rows, feat), lambda i, at: (at[i], 0, 0)),
        ),
        out_shape=jax.ShapeDtypeStruct((len(places), rows, feat), dtype),
        compiler_params=pltpu.CompilerParams(vmem_limit_bytes=VMEM_BYTES),
        cost_estimate=light(flops=0, bytes_accessed=4 * len(places) * rows * feat, transcendentals=0),
        name=name,
    )(jnp.stack(places).astype(jnp.int32), *operands, *behind)


def lay_rows(one, two, own, over_one, over_two, far, dtype, behind=()):
    rows, feat = own.shape

    def body(step, refs, out_ref):
        start = 0
        for ref in refs[step : step + 1] if step < 3 else refs[3 : 3 + len(far)]:
            out_ref[:, start : start + ref.shape[1]] = ref[...].astype(dtype)
            start += ref.shape[1]

    places = [2 * one + two, 2 * (1 - one) + two, 2 * one + 1 - two, 2 * (1 - one) + 1 - two]
    return pieces_of(places, rows, feat, dtype, body, "lay_rows", [own, over_one, over_two] + list(far), behind)


def norm_first(places, pieces, gain, shift, behind=()):
    rows, feat = pieces[0].shape

    def body(step, refs, out_ref):
        values = refs[step][...].astype(F32)
        out_ref[...] = (centre(values)[0] * refs[4][...] + refs[5][...]).astype(LOW)

    return pieces_of(places, rows, feat, LOW, body, "norm_first", pieces + [gain, shift], behind).reshape(-1, feat)


def lay_pieces(places, pieces, behind=()):
    rows, feat = pieces[0].shape

    def body(step, refs, out_ref):
        out_ref[...] = refs[step][...]

    return pieces_of(places, rows, feat, LOW, body, "lay_pieces", pieces, behind).reshape(-1, feat)


def join(keep_first, came_first, keep_second, came_second, behind=()):
    _, rows, half = keep_first.shape

    def kernel(one, two, three, four, *refs):
        first_stays, first_goes, second_stays, second_goes = refs[-4:]
        first_stays[...] = one[0].astype(F32) + two[0].astype(F32)
        first_goes[...] = (one[1].astype(F32) + two[1].astype(F32)).astype(LOW)
        second_stays[...] = three[0].astype(F32) + four[0].astype(F32)
        second_goes[...] = (three[1].astype(F32) + four[1].astype(F32)).astype(LOW)

    tm = tiles(rows, 128)
    pair = pl.BlockSpec((2, tm, half), lambda i: (0, i, 0))
    flat = pl.BlockSpec((tm, half), lambda i: (i, 0))
    shape = lambda dtype: jax.ShapeDtypeStruct((rows, half), dtype)
    return pl.pallas_call(
        kernel,
        grid=(rows // tm,),
        in_specs=[pair] * 4 + [ANYWHERE] * len(behind),
        out_specs=[flat] * 4,
        out_shape=[shape(F32), shape(LOW)] * 2,
        cost_estimate=light(flops=4 * rows * half, bytes_accessed=28 * rows * half, transcendentals=0),
        compiler_params=pltpu.CompilerParams(vmem_limit_bytes=VMEM_BYTES),
        name="join",
    )(keep_first, came_first, keep_second, came_second, *behind)


def on_rows(kernel, shares, values, tables, outs, sums, name, behind=()):
    rows, half = shares[0].shape
    feat = 2 * half
    tm = tiles(rows, 128)
    count, tabled = len(values), len(tables)

    def body(*refs):
        total = jnp.concatenate(
            [refs[0][...] + refs[1][...].astype(F32), refs[2][...] + refs[3][...].astype(F32)], axis=1
        )
        rest = refs[4 + count + tabled + len(behind) :]
        kernel(total, refs[4 : 4 + count], refs[4 + count : 4 + count + tabled], rest[: len(outs)], rest[len(outs) :])

    block = lambda cols: pl.BlockSpec((tm, cols), lambda i: (i, 0))
    return pl.pallas_call(
        body,
        grid=(rows // tm,),
        in_specs=[block(half)] * 4
        + [block(feat)] * count
        + [pl.BlockSpec((1, feat), lambda i: (0, 0))] * tabled
        + [ANYWHERE] * len(behind),
        out_specs=[block(feat)] * len(outs) + [pl.BlockSpec((2, feat), lambda i: (0, 0))] * sums,
        out_shape=[jax.ShapeDtypeStruct((rows, feat), dtype) for dtype in outs]
        + [jax.ShapeDtypeStruct((2, feat), F32)] * sums,
        cost_estimate=light(flops=20 * rows * feat, bytes_accessed=20 * rows * feat, transcendentals=0),
        compiler_params=pltpu.CompilerParams(vmem_limit_bytes=VMEM_BYTES),
        name=name,
    )(*shares, *values, *tables, *behind)


def centre(values):
    centred = values - jnp.mean(values, axis=1, keepdims=True)
    inv_std = lax.rsqrt(jnp.mean(centred * centred, axis=1, keepdims=True) + EPSILON)
    return centred * inv_std, inv_std


def add_norm(shares, values, gain, shift, behind=()):
    def kernel(total, value_refs, table_refs, out_refs, _):
        middle = value_refs[0][...].astype(F32) + total
        out_refs[0][...] = middle
        out_refs[1][...] = (centre(middle)[0] * table_refs[0][...] + table_refs[1][...]).astype(LOW)

    return on_rows(kernel, shares, [values], [gain, shift], [F32, LOW], 0, "add_norm", behind)


def add_low(shares, values, behind=()):
    def kernel(total, value_refs, _, out_refs, __):
        out_refs[0][...] = (value_refs[0][...].astype(F32) + total).astype(LOW)

    return on_rows(kernel, shares, [values], [], [LOW], 0, "add_low", behind)[0]


def norm_back(shares, values, gain, grad, outs, behind=()):
    def kernel(total, value_refs, table_refs, out_refs, sum_refs):
        scaled, inv_std = centre(value_refs[0][...].astype(F32))
        part = total * table_refs[0][...]
        first = jnp.mean(part, axis=1, keepdims=True)
        second = jnp.mean(part * scaled, axis=1, keepdims=True)
        result = value_refs[1][...].astype(F32) + inv_std * (part - first - scaled * second)
        for ref in out_refs:
            ref[...] = result.astype(ref.dtype)
        sums = sum_refs[0]

        @pl.when(pl.program_id(0) == 0)
        def _():
            sums[...] = jnp.zeros_like(sums)

        sums[0:1, :] += jnp.sum(total * scaled, axis=0, keepdims=True)
        sums[1:2, :] += jnp.sum(total, axis=0, keepdims=True)

    return on_rows(kernel, shares, [values, grad], [gain], outs, 1, "norm_back", behind)


def qkv_back(mine, theirs, my_grad, their_grad, behind=()):
    rows, feat = mine.shape
    count, _, cols = my_grad.shape
    tm = tiles(feat, 512)

    def kernel(mine_ref, theirs_ref, my_ref, their_ref, *refs):
        one, two = mine_ref[...].T, theirs_ref[...].T
        for c in range(count):
            refs[-1][c] = (dot_nn(one, my_ref[c]) + dot_nn(two, their_ref[c])).astype(LOW)

    tall = pl.BlockSpec((rows, tm), lambda i: (0, i))
    whole = pl.BlockSpec((count, rows, cols), lambda i: (0, 0, 0))
    return pl.pallas_call(
        kernel,
        grid=(feat // tm,),
        in_specs=[tall, tall, whole, whole] + [ANYWHERE] * len(behind),
        out_specs=pl.BlockSpec((count, tm, cols), lambda i: (0, i, 0)),
        out_shape=jax.ShapeDtypeStruct((count, feat, cols), LOW),
        cost_estimate=light(
            flops=4 * count * rows * feat * cols,
            bytes_accessed=4 * rows * feat + 4 * count * rows * cols + 2 * count * feat * cols,
            transcendentals=0,
        ),
        compiler_params=pltpu.CompilerParams(vmem_limit_bytes=VMEM_BYTES),
        name="grad_qkv",
    )(mine, theirs, my_grad, their_grad, *behind)


class Place:
    def __init__(self):
        self.fsdp = lax.axis_size("fsdp")
        self.context = lax.axis_size("context")
        self.tensor = lax.axis_size("tensor")
        self.pairs = self.tensor // 2
        self.z = lax.axis_index("fsdp")
        self.x = lax.axis_index("context")
        self.t = lax.axis_index("tensor")
        self.y = self.t // 2
        self.core = self.t % 2

    def square(self, seqs):
        return self.context == 2 and self.pairs == 2 and seqs == 1

    def size(self, which):
        return self.context if which == "x" else self.pairs

    def at(self, which):
        return self.x if which == "x" else self.y

    def shift(self, value, which, step):
        if which == "z":
            n = self.fsdp
            return lax.ppermute(value, "fsdp", [(i, (i + step) % n) for i in range(n)])
        if which == "x":
            n = self.context
            return lax.ppermute(value, "context", [(i, (i + step) % n) for i in range(n)])
        n = self.tensor
        return lax.ppermute(value, "tensor", [(i, (i + 2 * step) % n) for i in range(n)])

    def swap(self, value):
        return lax.ppermute(value, "tensor", [(i, i ^ 1) for i in range(self.tensor)])


def pick(value, index, axis):
    return lax.dynamic_index_in_dim(value, index, axis, keepdims=False)


def scatter_stage(place, value, axis, which):
    n, at = place.size(which), place.at(which)
    total = pick(value, at, axis).astype(F32)
    for step in range(1, n):
        sent = pick(value, (at + step) % n, axis)
        total = total + place.shift(sent, which, step).astype(F32)
    return total


def gather_stage(place, value, axis, which):
    n, at = place.size(which), place.at(which)
    if n == 1:
        return value
    if n == 2:
        return ordered(at, value, place.shift(value, which, 1), axis)
    parts = [value] + [place.shift(value, which, step) for step in range(1, n)]
    order = (at - jnp.arange(n)) % n
    shape = list(value.shape)
    shape[axis] = n * shape[axis]
    return jnp.take(jnp.stack(parts, axis), order, axis=axis).reshape(shape)


class Gathered:
    def __init__(self, place, value, axis):
        self.place, self.value, self.axis = place, value, axis
        if place.context == 2:
            self.raw = place.shift(value, "x", 1)
        else:
            self.raw = gather_stage(place, value, axis, "x")

    def whole(self):
        if self.place.context != 2:
            return self.raw
        return ordered(self.place.x, self.value, self.raw, self.axis)


def ordered(at, mine, other, axis):
    first = jnp.where(at == 0, mine, other)
    second = jnp.where(at == 0, other, mine)
    return jnp.concatenate([first, second], axis=axis)


def after(value, *others):
    return lax.optimization_barrier((value,) + others)[0]


class RowSum:
    def __init__(self, place, kind, terms, seqs, name, behind=()):
        self.place = place
        self.square = place.square(seqs)
        if self.square:
            self.keep_first, self.sent, self.keep_second, self.second = products_apart(
                place, kind, terms, 512, name, behind
            )
            return
        value = self.sent = products(kind, terms, 1024, 512, name, behind=behind)
        feat = value.shape[1]
        value = value.reshape(seqs, place.context, place.pairs, -1, feat)
        first, second = value[..., : feat // 2], value[..., feat // 2 :]
        first = scatter_stage(place, first, 1, "x").astype(LOW)
        second = scatter_stage(place, second, 2, "y").astype(LOW)
        first = scatter_stage(place, first, 1, "y").reshape(-1, feat // 2)
        second = scatter_stage(place, second, 1, "x").reshape(-1, feat // 2)
        nothing = jnp.zeros(first.shape, LOW)
        self.shares = [first, nothing, second, nothing]

    def start(self, *others):
        if self.square:
            first, second = after((self.sent, self.second), *others) if others else (self.sent, self.second)
            self.came_first = self.place.shift(first, "x", 1)
            self.came_second = self.place.shift(second, "y", 1)
        return self

    def follow(self, behind=()):
        if not self.square:
            return self.shares[0]
        first, first_goes, second, second_goes = join(
            self.keep_first, self.came_first, self.keep_second, self.came_second, behind
        )
        self.shares = [first, self.place.shift(first_goes, "y", 1), second, self.place.shift(second_goes, "x", 1)]
        return first


def spread_rows(place, value, seqs, behind=()):
    feat = value.shape[-1]
    half = feat // 2
    if place.square(seqs):
        over_x = place.shift(value, "x", 1)
        over_y = place.shift(value, "y", 1)
        far_first = place.shift(over_y[:, :half], "x", 1)
        far_second = place.shift(over_x[:, half:], "y", 1)
        whole = lay_rows(place.x, place.y, value, over_x, over_y, [far_first, far_second], LOW, behind)
        return whole.reshape(-1, feat)
    value = value.reshape(seqs, -1, feat)
    rows = value.shape[1]
    first, second = value[..., :half], value[..., half:]
    first = gather_stage(place, first, 1, "y")
    second = gather_stage(place, second, 1, "x")
    first = gather_stage(place, first, 1, "x")
    second = second.reshape(seqs, place.context, rows, half)
    second = gather_stage(place, second, 2, "y").reshape(first.shape)
    return jnp.concatenate([first, second], axis=-1).reshape(-1, feat)


class WholeRows:
    def __init__(self, place, value, seqs):
        self.place, self.value, self.seqs = place, value, seqs
        if place.square(seqs):
            self.over_y, self.over_core = place.shift(value, "y", 1), place.swap(value)
        else:
            self.over_y = gather_stage(place, value.reshape(seqs, -1, value.shape[-1]), 1, "y")
            self.over_core = place.swap(self.over_y)

    def whole(self, dtype, ready=(), behind=()):
        place, value = self.place, self.value
        if not place.square(self.seqs):
            return ordered(place.core, self.over_y, self.over_core, 0).astype(dtype)
        far = [place.swap(after(self.over_y, *ready) if ready else self.over_y)]
        whole = lay_rows(place.core, place.y, value, self.over_core, self.over_y, far, dtype, behind)
        return whole.reshape(2, -1, value.shape[-1])


def other_rows(place, value):
    rows = value.shape[0] // 2
    straight = place.shift(lax.dynamic_slice_in_dim(value, place.y * rows, rows, 0), "x", 1)
    return [value[:rows], value[rows:], straight, place.shift(straight, "y", 1)]


def other_places(place):
    x, y = place.x, place.y
    return [2 * x, 2 * x + 1, 2 * (1 - x) + y, 2 * (1 - x) + 1 - y]


def empty_kernel(*refs):
    pass


def empty(shape, dtype, behind=()):
    return pl.pallas_call(
        empty_kernel,
        in_specs=[ANYWHERE] * len(behind),
        out_specs=ANYWHERE,
        out_shape=jax.ShapeDtypeStruct(shape, dtype),
        name="empty",
    )(*behind)


def lay_shards(place, shard, before, behind, low, high, ready):
    n, z = place.fsdp, place.z
    blocks, size, cols = shard.shape
    whole = empty((blocks, n * size, cols), shard.dtype, ready)
    for part, block, start in (
        (shard, 0, z),
        (before[:, :size], 0, (z + 3) % n),
        (behind[:, :size], 0, (z + 1) % n),
        (low[:, :size], 0, (z + 2) % n),
        (high, blocks // 2, (z + 2) % n),
    ):
        whole = lax.dynamic_update_slice(whole, part, (block, start * size, 0))
    return whole


class Shards:
    def __init__(self, place, grad, axis, half_axis, begin):
        self.place, self.grad, self.axis, self.half_axis = place, grad, axis, half_axis
        self.size = grad.shape[axis] // place.fsdp
        self.half = (self.size if axis == half_axis else grad.shape[half_axis]) // 2

        def pair(one, two):
            return after(jnp.stack([one, two]).astype(LOW), begin)

        self.left = place.shift(pair(self.part(2, 1), self.part(1, 0)), "z", 1)
        self.right = place.shift(pair(self.part(2, 0), self.part(3, 1)), "z", -1)

    def part(self, ahead, side):
        place, half = self.place, self.half
        start = (place.z + ahead) % place.fsdp * self.size
        shard = lax.dynamic_slice_in_dim(self.grad, start, self.size, self.axis)
        return lax.slice_in_dim(shard, side * half, (side + 1) * half, axis=self.half_axis).astype(F32)

    def follow(self, *ready):
        place = self.place
        self.left, self.right = after((self.left, self.right), *ready)
        high = (self.part(1, 1) + self.left[0].astype(F32)).astype(LOW)
        low = (self.part(3, 0) + self.right[0].astype(F32)).astype(LOW)
        self.high, self.low = place.shift(high, "z", 1), place.shift(low, "z", -1)
        return low

    def total(self, *ready):
        high, low = after((self.high, self.low), *ready) if ready else (self.high, self.low)
        low = self.part(0, 0) + self.left[1].astype(F32) + low.astype(F32)
        high = self.part(0, 1) + self.right[1].astype(F32) + high.astype(F32)
        return jnp.concatenate([low.astype(LOW), high.astype(LOW)], axis=self.half_axis)


def total_over(place, value, which):
    n = {"z": place.fsdp, "x": place.context, "y": place.pairs, "core": 2}[which]
    if n == 1:
        return value
    if which == "core":
        return value + place.swap(value)
    if n == 2:
        return value + place.shift(value, which, 1)
    at = {"z": place.z, "x": place.x, "y": place.y}[which]
    parts = jnp.zeros((n,) + value.shape, value.dtype)
    parts = lax.dynamic_update_index_in_dim(parts, value, at, 0)
    for step in range(1, n):
        sent = place.shift(value, which, step)
        parts = lax.dynamic_update_index_in_dim(parts, sent, (at - step) % n, 0)
    return jnp.sum(parts, axis=0)


def small_totals(place, sums, bias, bias_other):
    n, z = place.fsdp, place.z
    feat = sums.shape[1]
    pad = [(0, 1), (0, 0)]
    sent = place.swap(jnp.concatenate([sums, jnp.pad(bias_other, pad)], axis=1))
    sums, bias = sums + sent[:, :feat], jnp.pad(bias, pad) + sent[:, feat:]
    size = feat // n
    came = []
    for step in range(n):
        part = lax.dynamic_slice_in_dim(sums, (z + step) % n * size, size, 1)
        part = jnp.concatenate([part, bias], axis=1)
        came.append(place.shift(part, "z", step) if step else part)
    came = lax.optimization_barrier(tuple(came))
    parts = jnp.zeros((n,) + came[0].shape, F32)
    for step in range(n):
        parts = lax.dynamic_update_index_in_dim(parts, came[step], (z - step) % n, 0)
    return jnp.sum(parts, axis=0)


def last_totals(place, totals, size):
    if place.context == 2:
        sent = place.shift(totals, "x", 1)
        return totals[:, :size] + sent[:, :size], ordered(place.x, totals[:3, size:], sent[:3, size:], 1)
    return total_over(place, totals[:, :size], "x"), gather_stage(place, totals[:3, size:], 1, "x")


def local(
    hidden_in,
    norm_gains,
    norm_biases,
    qkv_weight,
    qkv_bias,
    out_weight,
    gate_up_weight,
    down_weight,
    cotangent,
):
    place = Place()
    all_seqs, part_rows, feat = hidden_in.shape
    seqs = all_seqs // 2
    length = part_rows * place.context
    own_rows = part_rows // place.pairs
    head_cols = qkv_bias.shape[1] // place.context
    hidden_cols = down_weight.shape[0] // place.context

    def columns(value, count, axis):
        return lax.dynamic_slice_in_dim(value, place.x * count, count, axis)

    def own_sequences(value):
        return lax.dynamic_slice_in_dim(value, place.core * seqs, seqs, 0)

    def own_piece(value):
        return lax.dynamic_slice_in_dim(value, place.y * own_rows, own_rows, 1)

    pack = jnp.concatenate(
        [columns(qkv_weight, head_cols, 2), columns(out_weight, head_cols, 0).T[None]]
    )
    norm_part = jnp.concatenate([norm_gains, norm_biases]).reshape(-1, head_cols)
    norm_rows = norm_part.shape[0]
    pad = -norm_rows % 16
    part_feat = pack.shape[1]
    norm_block = jnp.pad(norm_part, [(0, pad), (0, 0)])[None]
    extra = jnp.pad(norm_block, [(0, 3), (0, 0), (0, 0)])
    pack = jnp.concatenate([pack, extra], axis=1)
    pack_before, pack_behind = place.shift(pack, "z", 1), place.shift(pack, "z", -1)
    bias = columns(qkv_bias, head_cols, 1)
    bias_swapped = place.swap(bias)
    bias_other = bias_swapped.astype(F32)[None, :, None, :]
    bias = bias.astype(F32)[None, :, None, :]
    hidden_mine = own_sequences(hidden_in).reshape(-1, feat)
    top_mine = own_sequences(cotangent)
    if place.square(seqs):
        pieces = other_rows(place, hidden_mine)
        top_pieces = other_rows(place, top_mine.reshape(-1, feat))
        pack_before, pack_behind = after((pack_before, pack_behind), pieces[2], bias_swapped)
    else:
        whole = gather_stage(place, hidden_mine.reshape(seqs, -1, feat), 1, "x").reshape(-1, feat)
        pieces = top_pieces = [whole] * 4
    half = pack.shape[0] // 2
    pack_low = place.shift(pack_before[:half], "z", 1)
    pack_high = place.shift(pack_behind[half:, :part_feat], "z", -1)
    norms = jnp.zeros((2, 2, feat), F32)
    for step, piece in (
        (0, norm_block),
        (1, pack_before[:1, part_feat:]),
        (2, pack_low[:1, part_feat:]),
        (3, pack_behind[:1, part_feat:]),
    ):
        piece = piece[0, :norm_rows].reshape(2, 2, part_feat).astype(F32)
        norms = lax.dynamic_update_slice(norms, piece, (0, 0, (place.z - step) % place.fsdp * part_feat))
    gains, shifts = norms[0][:, None, :], norms[1][:, None, :]
    gate_up_part = columns(gate_up_weight, hidden_cols, 2).transpose(0, 2, 1)
    down_part = columns(down_weight, hidden_cols, 0)
    if place.square(seqs):
        normed = norm_first(other_places(place), pieces, gains[0], shifts[0])
        top_last = top_pieces[3]
    else:
        normed = (centre(whole.astype(F32))[0] * gains[0] + shifts[0]).astype(LOW)
        grad_top = top_last = gather_stage(place, top_mine, 1, "x").reshape(seqs * length, feat)
    w_attn = lay_shards(place, pack[:, :part_feat], pack_before, pack_behind, pack_low, after(pack_high, normed), [pieces[3], gate_up_part, down_part])
    gate_up_part, down_part = after((gate_up_part, down_part), pack_low, pack_high, top_pieces[2])
    w_gate_up = lax.all_gather(gate_up_part, "fsdp", axis=2, tiled=True)
    w_down = lax.all_gather(down_part, "fsdp", axis=1, tiled=True)
    tables = rotary_tables(length, min(head_cols, 128))
    w_attn_other = place.swap(w_attn)

    def attend(weight, bias, behind):
        mixed = jnp.einsum("rd,cde->cre", normed, weight[:3], preferred_element_type=F32)
        return attend_forward(mixed[None], bias, tables, seqs, length, behind)

    kept = attend(w_attn, bias, [])
    kept_other = attend(w_attn_other, bias_other, [kept[3], top_last])
    attended, attended_other = kept[3][0], kept_other[3][0]
    attn_sum = RowSum(
        place,
        "nt",
        [(attended, (), w_attn, (3,)), (attended_other, (), w_attn_other, (3,))],
        seqs,
        "out",
    ).start()
    if place.square(seqs):
        grad_top = lay_pieces(other_places(place), top_pieces, [attn_sum.sent])
    theirs_top, theirs_one, theirs_attended = place.swap(grad_top), place.swap(normed), place.swap(attended_other)
    attn_sum.follow([grad_top])
    inputs = own_piece(hidden_mine.reshape(seqs, -1, feat)).reshape(-1, feat)
    middle, normed_two = add_norm(
        attn_sum.shares, inputs, gains[1], shifts[1], behind=[theirs_attended]
    )
    normed_two = spread_rows(place, normed_two, seqs, [theirs_top, theirs_one])

    w_gate_up_other = place.swap(after(w_gate_up, middle))
    turned_other, slope_other, hidden_part = gate_up(normed_two, w_gate_up_other)
    theirs_turned, w_down_other = place.swap(turned_other), place.swap(after(w_down, turned_other))
    turned, slope, hidden = gate_up(normed_two, w_gate_up)
    grad_down = products(
        "nn",
        [(turned, (), grad_top, ()), (theirs_turned, (), theirs_top, ())],
        hidden_cols,
        512,
        "grad_down",
    )
    down_sum = lax.psum_scatter(grad_down, "fsdp", scatter_dimension=1, tiled=True)
    grad_gu_turned_other, grad_gu_other = hidden_back(grad_top, w_down_other, slope_other, [grad_down])
    theirs_gu, theirs_two = place.swap(grad_gu_turned_other), place.swap(normed_two)
    grad_gu_turned, grad_gu = hidden_back(grad_top, w_down, slope, [grad_gu_other])
    two_sum = RowSum(
        place,
        "nn",
        [(grad_gu, (c,), w_gate_up, (c,)) for c in range(2)]
        + [(grad_gu_other, (c,), w_gate_up_other, (c,)) for c in range(2)],
        seqs,
        "grad_two",
        behind=[theirs_two, theirs_gu],
    ).start()
    grad_gate_up = products(
        "nn",
        [(grad_gu_turned, (), normed_two, ()), (theirs_gu, (), theirs_two, ())],
        hidden_cols,
        512,
        "grad_gate_up",
        count=2,
        behind=[two_sum.sent],
    )
    two_next = two_sum.follow([grad_gate_up, down_sum])
    gate_up_sum = lax.psum_scatter(after(grad_gate_up, two_next), "fsdp", scatter_dimension=2, tiled=True)
    down_sums = RowSum(
        place,
        "nn",
        [(hidden, (), w_down, ()), (hidden_part, (), w_down_other, ())],
        seqs,
        "down",
        behind=[two_next],
    )
    top_rows = own_piece(top_mine).reshape(-1, feat)
    grad_middle, mid_low, sums_two = norm_back(
        two_sum.shares, middle, gains[1], top_rows, [F32, LOW], behind=[down_sums.sent]
    )
    grad_mid_low = spread_rows(place, mid_low, seqs)
    down_gathered = Gathered(place, after(down_sum, grad_mid_low), 0)
    down_sums.start(grad_mid_low)

    def attend_grad(kept, weight, behind):
        grad_att = products("nn", [(grad_mid_low, (), weight, (3,))], 1024, head_cols, "grad_att", behind=behind)
        return attend_back(*kept, grad_att[None], tables, seqs, length)[0]

    theirs_mid = place.swap(grad_mid_low)
    grad_mixed_other = attend_grad(kept_other, w_attn_other, [])
    theirs_mixed = place.swap(grad_mixed_other)
    grad_out = products(
        "tn",
        [(grad_mid_low, (), attended, ()), (theirs_mid, (), theirs_attended, ())],
        512,
        head_cols,
        "grad_out",
        behind=[grad_mixed_other],
    )
    down_next = down_sums.follow([grad_out])
    grad_mixed = attend_grad(kept, w_attn, [down_next])
    final_out = add_low(down_sums.shares, middle, behind=[grad_mixed])
    out_sum = lax.psum_scatter(grad_out, "fsdp", scatter_dimension=0, tiled=True)
    one_sum = RowSum(
        place,
        "nt",
        [(grad_mixed, (c,), w_attn, (c,)) for c in range(3)]
        + [(grad_mixed_other, (c,), w_attn_other, (c,)) for c in range(3)],
        seqs,
        "grad_one",
        behind=[final_out, down_gathered.raw],
    ).start()
    grad_qkv = qkv_back(
        normed, theirs_one, grad_mixed, theirs_mixed, behind=[one_sum.sent, gate_up_sum]
    )
    qkv_shards = Shards(place, grad_qkv, 1, 1, grad_mixed)
    one_next = one_sum.follow([grad_qkv])
    qkv_next = qkv_shards.follow(one_next)
    layer_rows = WholeRows(place, after(final_out, one_sum.shares[1], one_sum.shares[3]), seqs)
    input_low, sums_one = norm_back(
        one_sum.shares, inputs, gains[0], grad_middle, [LOW], behind=[one_next, qkv_next]
    )
    gate_up_out = lax.all_gather(gate_up_sum, "context", axis=1, tiled=True)
    gate_up_out = gate_up_out.transpose(0, 2, 1).astype(F32)
    sums = after(jnp.concatenate([sums_one, sums_two]), layer_rows.over_y)
    sums = total_over(place, sums, "y")
    input_rows = WholeRows(place, after(input_low, sums), seqs)
    totals = small_totals(
        place,
        after(sums, qkv_shards.low, qkv_shards.high, gate_up_out),
        jnp.sum(grad_mixed.astype(F32), axis=1),
        jnp.sum(grad_mixed_other.astype(F32), axis=1),
    )
    qkv_sum = qkv_shards.total()
    qkv_gathered = Gathered(place, qkv_sum, 2)
    out_gathered = Gathered(place, after(out_sum, qkv_sum), 1)
    sums, grad_bias = last_totals(place, after(totals, qkv_sum), norm_gains.shape[1])
    layer_out = layer_rows.whole(LOW)
    input_grad = input_rows.whole(F32, [qkv_gathered.raw])

    return (
        layer_out,
        input_grad,
        sums[0::2],
        sums[1::2],
        qkv_gathered.whole().astype(F32),
        grad_bias,
        out_gathered.whole().T.astype(F32),
        gate_up_out,
        down_gathered.whole().astype(F32),
    )


def solution(mesh):
    placed = (
        P("fsdp", "context", None),
        P(None, "fsdp"),
        P(None, "fsdp"),
        P(None, "fsdp", "tensor"),
        P(None, "tensor"),
        P("tensor", "fsdp"),
        P(None, "fsdp", "tensor"),
        P("tensor", "fsdp"),
        P("fsdp", "context", None),
    )
    return jax.shard_map(
        local,
        mesh=mesh,
        in_specs=placed,
        out_specs=(
            P("fsdp", "context", None),
            P("fsdp", "context", None),
            P(None, "fsdp"),
            P(None, "fsdp"),
            P(None, "fsdp", "tensor"),
            P(None, "tensor"),
            P("tensor", "fsdp"),
            P(None, "fsdp", "tensor"),
            P("tensor", "fsdp"),
        ),
        check_vma=False,
    )
```

```python
import math

import jax
import jax.numpy as jnp
import numpy as np
from jax import lax
from jax.experimental import pallas as pl
from jax.experimental.pallas import tpu as pltpu
from jax.sharding import PartitionSpec as P

HEAD_DIM = 64
ROT = 16
EPSILON = 1e-05
F32 = jnp.float32
LOW = jnp.bfloat16


def rotary_tables(length, width):
    column = np.arange(width) % HEAD_DIM
    half = ROT // 2
    frequency = np.power(10000.0, -2.0 * (column % half) / ROT).astype(np.float32)
    angles = np.arange(length, dtype=np.float32)[:, None] * frequency[None, :]
    inside = column < ROT
    lower = column < half
    sine = np.sin(angles)
    cosine = np.where(inside, np.cos(angles), 1.0)
    minus = np.where(lower, -sine, 0.0)
    plus = np.where(inside & ~lower, sine, 0.0)
    return jnp.asarray(np.stack([cosine, minus, plus]).astype(np.float32))

def light(flops, bytes_accessed, transcendentals):
    return pl.CostEstimate(flops=flops // 100, bytes_accessed=bytes_accessed // 100, transcendentals=0)


def dot_nt(a,b): return lax.dot_general(a,b,(((1,),(1,)),((),())),preferred_element_type=F32)
def dot_nn(a,b): return lax.dot_general(a,b,(((1,),(0,)),((),())),preferred_element_type=F32)
def dot_tn(a,b): return lax.dot_general(a,b,(((0,),(0,)),((),())),preferred_element_type=F32)

def head_masks(width):
    lane=lax.broadcasted_iota(jnp.int32,(1,width),1)
    return [ (lane//HEAD_DIM)==h for h in range(width//HEAD_DIM)]

def fwd_kernel(block, mixed_ref, bias_ref, table_ref, *refs):
    q_ref, k_ref, v_ref, att_ref, lse_ref = refs[-5:]
    length, width = q_ref.shape
    half=ROT//2
    def rotated(c):
        v=mixed_ref[c]+bias_ref[c]
        return v*table_ref[0]+pltpu.roll(v,width-half,1)*table_ref[1]+pltpu.roll(v,half,1)*table_ref[2]
    q_ref[...]=(rotated(0)*(1.0/math.sqrt(HEAD_DIM))).astype(LOW)
    k_ref[...]=rotated(1).astype(LOW)
    v_ref[...]=(mixed_ref[2]+bias_ref[2]).astype(LOW)
    masks=head_masks(width)
    row=lax.broadcasted_iota(jnp.int32,(block,block),0)
    col=lax.broadcasted_iota(jnp.int32,(block,block),1)
    for i in range(length//block):
        rows=pl.ds(i*block,block)
        q=q_ref[rows,:]
        out=jnp.zeros((block,width),F32); lse=jnp.zeros((block,width),F32)
        for mask in masks:
            qh=jnp.where(mask,q,jnp.zeros_like(q))
            diag=jnp.where(row>=col,dot_nt(qh,k_ref[rows,:]),-1e30)
            top=jnp.max(diag,axis=1,keepdims=True)
            if i>0:
                rest=dot_nt(qh,k_ref[pl.ds(0,i*block),:])
                top=jnp.maximum(top,jnp.max(rest,axis=1,keepdims=True))
            diag=jnp.exp(diag-top)
            total=jnp.sum(diag,axis=1,keepdims=True)
            acc=dot_nn(diag.astype(LOW),v_ref[rows,:])
            if i>0:
                rest=jnp.exp(rest-top)
                total=total+jnp.sum(rest,axis=1,keepdims=True)
                acc=acc+dot_nn(rest.astype(LOW),v_ref[pl.ds(0,i*block),:])
            out=jnp.where(mask,acc/total,out)
            lse=jnp.where(mask,top+jnp.log(total),lse)
        att_ref[rows,:]=out.astype(LOW)
        lse_ref[rows,:]=lse

def attend_forward(mixed,bias,tables,seqs,length,behind=(),block=256):
    pair,_,rows,cols=mixed.shape
    width=min(cols,128); groups=cols//width
    tok=lambda o,s,g:(o,s,g)
    spec=pl.BlockSpec((None,length,width),tok)
    shape=lambda d:jax.ShapeDtypeStruct((pair,rows,cols),d)
    return pl.pallas_call(
        lambda *r: fwd_kernel(block,*r),
        grid=(pair,seqs,groups),
        in_specs=[pl.BlockSpec((None,3,length,width),lambda o,s,g:(o,0,s,g)),
                  pl.BlockSpec((None,3,1,width),lambda o,s,g:(o,0,0,g)),
                  pl.BlockSpec((3,length,width),lambda o,s,g:(0,0,0))]+[pl.BlockSpec(memory_space=pl.ANY)]*len(behind),
        out_specs=[spec]*5,
        out_shape=[shape(LOW)]*4+[shape(F32)],
        compiler_params=pltpu.CompilerParams(vmem_limit_bytes=48<<20),
        cost_estimate=light(flops=int(4*pair*rows*length*cols*0.6),bytes_accessed=pair*rows*cols*26,transcendentals=pair*rows*length*cols//128),
        name="attend_forward",
    )(mixed,bias,tables,*behind)

def bwd_kernel(block,q_ref,k_ref,v_ref,att_ref,lse_ref,do_ref,table_ref,out_ref,dk_acc,dv_acc,dq_acc):
    length,width=q_ref.shape
    half=ROT//2
    masks=head_masks(width)
    row=lax.broadcasted_iota(jnp.int32,(block,block),0)
    col=lax.broadcasted_iota(jnp.int32,(block,block),1)
    count=length//block
    for i in reversed(range(count)):
        rows=pl.ds(i*block,block)
        q=q_ref[rows,:]; do=do_ref[rows,:]; lse=lse_ref[rows,:]
        prod=do.astype(F32)*att_ref[rows,:].astype(F32)
        n=(i+1)*block
        keys=k_ref[pl.ds(0,n),:]; vals=v_ref[pl.ds(0,n),:]
        dq=jnp.zeros((block,width),F32)
        dk=None
        for h,mask in enumerate(masks):
            qh=jnp.where(mask,q,jnp.zeros_like(q)); dh=jnp.where(mask,do,jnp.zeros_like(do))
            delta=jnp.sum(jnp.where(mask,prod,0.0),axis=1,keepdims=True)
            lse_h=lse[:,h*HEAD_DIM:h*HEAD_DIM+1]
            s=dot_nt(qh,keys)
            p=jnp.exp(s-lse_h)
            if i==0:
                p=jnp.where(row>=col,p,0.0)
            else:
                p=jnp.concatenate([p[:,:n-block],jnp.where(row>=col,p[:,n-block:],0.0)],axis=1)
            dp=dot_nt(dh,vals)
            ds=(p*(dp-delta)).astype(LOW)
            pl_low=p.astype(LOW)
            dq=jnp.where(mask,dot_nn(ds,keys),dq)
            tk=dot_tn(ds,qh); tv=dot_tn(pl_low,dh)
            dk=tk if dk is None else dk+tk
            dv=tv if h==0 else dv+tv
        dq_acc[rows,:]=dq*(1.0/math.sqrt(HEAD_DIM))
        if i==count-1:
            dk_acc[...]=dk; dv_acc[...]=dv
        else:
            dk_acc[pl.ds(0,n),:]+=dk; dv_acc[pl.ds(0,n),:]+=dv
    def back(v):
        return v*table_ref[0]+pltpu.roll(v*table_ref[1],half,1)+pltpu.roll(v*table_ref[2],width-half,1)
    out_ref[0]=back(dq_acc[...]).astype(LOW)
    out_ref[1]=back(dk_acc[...]).astype(LOW)
    out_ref[2]=dv_acc[...].astype(LOW)

def attend_back(q,k,v,att,lse,grad,tables,seqs,length,block=256):
    pair,rows,cols=q.shape
    width=min(cols,128); groups=cols//width
    spec=pl.BlockSpec((None,length,width),lambda o,s,g:(o,s,g))
    return pl.pallas_call(
        lambda *r: bwd_kernel(block,*r),
        grid=(pair,seqs,groups),
        in_specs=[spec]*6+[pl.BlockSpec((3,length,width),lambda o,s,g:(0,0,0))],
        out_specs=pl.BlockSpec((None,3,length,width),lambda o,s,g:(o,0,s,g)),
        out_shape=jax.ShapeDtypeStruct((pair,3,rows,cols),LOW),
        scratch_shapes=[pltpu.VMEM((length,width),F32)]*3,
        compiler_params=pltpu.CompilerParams(vmem_limit_bytes=48<<20),
        cost_estimate=light(flops=int(10*pair*rows*length*cols*0.6),bytes_accessed=pair*rows*cols*20,transcendentals=pair*rows*length*cols//128),
        name="attend_back",
    )(q,k,v,att,lse,grad,tables)


VMEM_BYTES = 56 << 20
FORMS = {"nn": dot_nn, "nt": dot_nt, "tn": dot_tn}
ANYWHERE = pl.BlockSpec(memory_space=pl.ANY)


def tiles(size, most):
    while size > most and size % 2 == 0:
        size //= 2
    return size


def lead_spec(lead, block, where):
    return pl.BlockSpec((None,) * len(lead) + block, lambda *at: lead + where(*at))


def products(kind, terms, row_tile, col_tile, name, count=None, dtype=LOW, behind=()):
    one, _, two, _ = terms[0]
    deep = one.shape[-2] if kind == "tn" else one.shape[-1]
    rows = one.shape[-1] if kind == "tn" else one.shape[-2]
    cols = two.shape[-2] if kind == "nt" else two.shape[-1]
    tm, tn = tiles(rows, row_tile), tiles(cols, col_tile)
    one_block = ((deep, tm), lambda c, i, j: (0, i)) if kind == "tn" else ((tm, deep), lambda c, i, j: (i, 0))
    two_block = ((tn, deep), lambda c, i, j: (j, 0)) if kind == "nt" else ((deep, tn), lambda c, i, j: (0, j))
    number = len(terms)

    def kernel(*refs):
        total = sum(FORMS[kind](a[...], b[...]) for a, b in zip(refs[:number], refs[number : 2 * number]))
        refs[-1][...] = total.astype(dtype)

    if count is None:
        ones = [lead_spec(t[1], *one_block) for t in terms]
        out_spec = pl.BlockSpec((tm, tn), lambda c, i, j: (i, j))
        out_shape = (rows, cols)
    else:
        ones = [pl.BlockSpec((None,) + one_block[0], lambda c, i, j: (c,) + one_block[1](c, i, j)) for t in terms]
        out_spec = pl.BlockSpec((None, tm, tn), lambda c, i, j: (c, i, j))
        out_shape = (count, rows, cols)
    many = count or 1
    return pl.pallas_call(
        kernel,
        grid=(many, rows // tm, cols // tn),
        in_specs=ones + [lead_spec(t[3], *two_block) for t in terms] + [ANYWHERE] * len(behind),
        out_specs=out_spec,
        out_shape=jax.ShapeDtypeStruct(out_shape, dtype),
        compiler_params=pltpu.CompilerParams(vmem_limit_bytes=VMEM_BYTES),
        cost_estimate=light(
            flops=2 * rows * deep * cols * number * many,
            bytes_accessed=2 * (many * number * (rows * deep + deep * cols) + many * rows * cols),
            transcendentals=0,
        ),
        name=name,
    )(*[t[0] for t in terms], *[t[2] for t in terms], *behind)


def products_apart(place, kind, terms, col_tile, name, behind=()):
    one, _, two, _ = terms[0]
    deep = one.shape[-2] if kind == "tn" else one.shape[-1]
    rows = one.shape[-1] if kind == "tn" else one.shape[-2]
    cols = two.shape[-2] if kind == "nt" else two.shape[-1]
    tn = tiles(cols // 2, col_tile)
    half = cols // 2 // tn
    piece = rows // 4
    one_block = ((deep, rows), lambda j, at: (0, 0)) if kind == "tn" else ((rows, deep), lambda j, at: (0, 0))
    two_block = ((tn, deep), lambda j, at: (j, 0)) if kind == "nt" else ((deep, tn), lambda j, at: (0, j))
    number = len(terms)

    def kernel(at_ref, *refs):
        total = sum(FORMS[kind](a[...], b[...]) for a, b in zip(refs[:number], refs[number : 2 * number]))
        keep_first, send_first, keep_second, send_second, held = refs[-5:]
        held[...] = total.astype(LOW).reshape(held.shape)
        x, y = at_ref[0], at_ref[1]

        @pl.when(pl.program_id(0) < half)
        def _():
            for other in range(2):
                across = y if other == 0 else 1 - y
                keep_first[other] = held[2 * x + across]
                send_first[other] = held[2 * (1 - x) + across]

        @pl.when(pl.program_id(0) >= half)
        def _():
            for other in range(2):
                along = x if other == 0 else 1 - x
                keep_second[other] = held[2 * along + y]
                send_second[other] = held[2 * along + 1 - y]

    first = pl.BlockSpec((2, piece, tn), lambda j, at: (0, 0, jnp.minimum(j, half - 1)))
    second = pl.BlockSpec((2, piece, tn), lambda j, at: (0, 0, jnp.maximum(j - half, 0)))
    return pl.pallas_call(
        kernel,
        grid_spec=pltpu.PrefetchScalarGridSpec(
            num_scalar_prefetch=1,
            grid=(2 * half,),
            in_specs=[lead_spec(t[1], *one_block) for t in terms]
            + [lead_spec(t[3], *two_block) for t in terms]
            + [ANYWHERE] * len(behind),
            out_specs=[first, first, second, second],
            scratch_shapes=[pltpu.VMEM((4, piece, tn), LOW)],
        ),
        out_shape=[jax.ShapeDtypeStruct((2, piece, cols // 2), LOW)] * 4,
        compiler_params=pltpu.CompilerParams(vmem_limit_bytes=VMEM_BYTES),
        cost_estimate=light(
            flops=2 * rows * deep * cols * number,
            bytes_accessed=2 * (number * (rows * deep + deep * cols) + rows * cols),
            transcendentals=0,
        ),
        name=name,
    )(jnp.stack([place.x, place.y]).astype(jnp.int32), *[t[0] for t in terms], *[t[2] for t in terms], *behind)


def gate_kernel(weight_ref, rows_ref, turned_ref, slope_ref, hidden_ref):
    rows = rows_ref[...]
    gate = dot_nt(weight_ref[0], rows)
    up = dot_nt(weight_ref[1], rows)
    sig = 1.0 / (1.0 + jnp.exp(-gate))
    act = gate * sig
    hidden = (act * up).astype(LOW)
    turned_ref[...] = hidden
    hidden_ref[...] = hidden.T
    slope_ref[0] = (up * sig * (1.0 + gate * (1.0 - sig))).astype(LOW)
    slope_ref[1] = act.astype(LOW)


def gate_up(values, weight):
    rows, feat = values.shape
    units = weight.shape[1]
    tm = tiles(rows, 512)
    return pl.pallas_call(
        gate_kernel,
        grid=(rows // tm,),
        in_specs=[
            pl.BlockSpec((2, units, feat), lambda i: (0, 0, 0)),
            pl.BlockSpec((tm, feat), lambda i: (i, 0)),
        ],
        out_specs=[
            pl.BlockSpec((units, tm), lambda i: (0, i)),
            pl.BlockSpec((2, units, tm), lambda i: (0, 0, i)),
            pl.BlockSpec((tm, units), lambda i: (i, 0)),
        ],
        out_shape=[
            jax.ShapeDtypeStruct((units, rows), LOW),
            jax.ShapeDtypeStruct((2, units, rows), LOW),
            jax.ShapeDtypeStruct((rows, units), LOW),
        ],
        compiler_params=pltpu.CompilerParams(vmem_limit_bytes=VMEM_BYTES),
        cost_estimate=light(
            flops=4 * rows * feat * units,
            bytes_accessed=2 * (rows * feat + 2 * feat * units + 4 * rows * units),
            transcendentals=rows * units,
        ),
        name="gate_up",
    )(weight, values)


def hidden_back_kernel(weight_ref, grad_ref, slope_ref, *refs):
    turned_ref, out_ref = refs[-2:]
    grad = dot_nt(weight_ref[...], grad_ref[...])
    for c in range(2):
        part = (grad * slope_ref[c].astype(F32)).astype(LOW)
        turned_ref[c] = part
        out_ref[c] = part.T


def hidden_back(grad, weight, slope, behind=()):
    rows, feat = grad.shape
    units = weight.shape[0]
    tm = tiles(rows, 512)
    return pl.pallas_call(
        hidden_back_kernel,
        grid=(rows // tm,),
        in_specs=[
            pl.BlockSpec((units, feat), lambda i: (0, 0)),
            pl.BlockSpec((tm, feat), lambda i: (i, 0)),
            pl.BlockSpec((2, units, tm), lambda i: (0, 0, i)),
        ]
        + [ANYWHERE] * len(behind),
        out_specs=[
            pl.BlockSpec((2, units, tm), lambda i: (0, 0, i)),
            pl.BlockSpec((2, tm, units), lambda i: (0, i, 0)),
        ],
        out_shape=[
            jax.ShapeDtypeStruct((2, units, rows), LOW),
            jax.ShapeDtypeStruct((2, rows, units), LOW),
        ],
        compiler_params=pltpu.CompilerParams(vmem_limit_bytes=VMEM_BYTES),
        cost_estimate=light(
            flops=2 * rows * feat * units,
            bytes_accessed=2 * (rows * feat + feat * units + 6 * rows * units),
            transcendentals=0,
        ),
        name="hidden_back",
    )(weight, grad, slope, *behind)


def pieces_of(places, rows, feat, dtype, body, name, operands, behind=()):
    def kernel(at_ref, *refs):
        for step in range(len(places)):
            pl.when(pl.program_id(0) == step)(lambda step=step: body(step, refs, refs[-1]))

    specs = [pl.BlockSpec(v.shape, lambda i, at, n=v.ndim: (0,) * n) for v in operands]
    return pl.pallas_call(
        kernel,
        grid_spec=pltpu.PrefetchScalarGridSpec(
            num_scalar_prefetch=1,
            grid=(len(places),),
            in_specs=specs + [ANYWHERE] * len(behind),
            out_specs=pl.BlockSpec((None, rows, feat), lambda i, at: (at[i], 0, 0)),
        ),
        out_shape=jax.ShapeDtypeStruct((len(places), rows, feat), dtype),
        compiler_params=pltpu.CompilerParams(vmem_limit_bytes=VMEM_BYTES),
        cost_estimate=light(flops=0, bytes_accessed=4 * len(places) * rows * feat, transcendentals=0),
        name=name,
    )(jnp.stack(places).astype(jnp.int32), *operands, *behind)


def lay_rows(one, two, own, over_one, over_two, far, dtype, behind=()):
    rows, feat = own.shape

    def body(step, refs, out_ref):
        start = 0
        for ref in refs[step : step + 1] if step < 3 else refs[3 : 3 + len(far)]:
            out_ref[:, start : start + ref.shape[1]] = ref[...].astype(dtype)
            start += ref.shape[1]

    places = [2 * one + two, 2 * (1 - one) + two, 2 * one + 1 - two, 2 * (1 - one) + 1 - two]
    return pieces_of(places, rows, feat, dtype, body, "lay_rows", [own, over_one, over_two] + list(far), behind)


def norm_first(places, pieces, gain, shift, behind=()):
    rows, feat = pieces[0].shape

    def body(step, refs, out_ref):
        values = refs[step][...].astype(F32)
        out_ref[...] = (centre(values)[0] * refs[4][...] + refs[5][...]).astype(LOW)

    return pieces_of(places, rows, feat, LOW, body, "norm_first", pieces + [gain, shift], behind).reshape(-1, feat)


def lay_pieces(places, pieces, behind=()):
    rows, feat = pieces[0].shape

    def body(step, refs, out_ref):
        out_ref[...] = refs[step][...]

    return pieces_of(places, rows, feat, LOW, body, "lay_pieces", pieces, behind).reshape(-1, feat)


def join(keep_first, came_first, keep_second, came_second, behind=()):
    _, rows, half = keep_first.shape

    def kernel(one, two, three, four, *refs):
        first_stays, first_goes, second_stays, second_goes = refs[-4:]
        first_stays[...] = one[0].astype(F32) + two[0].astype(F32)
        first_goes[...] = (one[1].astype(F32) + two[1].astype(F32)).astype(LOW)
        second_stays[...] = three[0].astype(F32) + four[0].astype(F32)
        second_goes[...] = (three[1].astype(F32) + four[1].astype(F32)).astype(LOW)

    tm = tiles(rows, 128)
    pair = pl.BlockSpec((2, tm, half), lambda i: (0, i, 0))
    flat = pl.BlockSpec((tm, half), lambda i: (i, 0))
    shape = lambda dtype: jax.ShapeDtypeStruct((rows, half), dtype)
    return pl.pallas_call(
        kernel,
        grid=(rows // tm,),
        in_specs=[pair] * 4 + [ANYWHERE] * len(behind),
        out_specs=[flat] * 4,
        out_shape=[shape(F32), shape(LOW)] * 2,
        cost_estimate=light(flops=4 * rows * half, bytes_accessed=28 * rows * half, transcendentals=0),
        compiler_params=pltpu.CompilerParams(vmem_limit_bytes=VMEM_BYTES),
        name="join",
    )(keep_first, came_first, keep_second, came_second, *behind)


def on_rows(kernel, shares, values, tables, outs, sums, name, behind=()):
    rows, half = shares[0].shape
    feat = 2 * half
    tm = tiles(rows, 128)
    count, tabled = len(values), len(tables)

    def body(*refs):
        total = jnp.concatenate(
            [refs[0][...] + refs[1][...].astype(F32), refs[2][...] + refs[3][...].astype(F32)], axis=1
        )
        rest = refs[4 + count + tabled + len(behind) :]
        kernel(total, refs[4 : 4 + count], refs[4 + count : 4 + count + tabled], rest[: len(outs)], rest[len(outs) :])

    block = lambda cols: pl.BlockSpec((tm, cols), lambda i: (i, 0))
    return pl.pallas_call(
        body,
        grid=(rows // tm,),
        in_specs=[block(half)] * 4
        + [block(feat)] * count
        + [pl.BlockSpec((1, feat), lambda i: (0, 0))] * tabled
        + [ANYWHERE] * len(behind),
        out_specs=[block(feat)] * len(outs) + [pl.BlockSpec((2, feat), lambda i: (0, 0))] * sums,
        out_shape=[jax.ShapeDtypeStruct((rows, feat), dtype) for dtype in outs]
        + [jax.ShapeDtypeStruct((2, feat), F32)] * sums,
        cost_estimate=light(flops=20 * rows * feat, bytes_accessed=20 * rows * feat, transcendentals=0),
        compiler_params=pltpu.CompilerParams(vmem_limit_bytes=VMEM_BYTES),
        name=name,
    )(*shares, *values, *tables, *behind)


def centre(values):
    centred = values - jnp.mean(values, axis=1, keepdims=True)
    inv_std = lax.rsqrt(jnp.mean(centred * centred, axis=1, keepdims=True) + EPSILON)
    return centred * inv_std, inv_std


def add_norm(shares, values, gain, shift, behind=()):
    def kernel(total, value_refs, table_refs, out_refs, _):
        middle = value_refs[0][...].astype(F32) + total
        out_refs[0][...] = middle
        out_refs[1][...] = (centre(middle)[0] * table_refs[0][...] + table_refs[1][...]).astype(LOW)

    return on_rows(kernel, shares, [values], [gain, shift], [F32, LOW], 0, "add_norm", behind)


def add_low(shares, values, behind=()):
    def kernel(total, value_refs, _, out_refs, __):
        out_refs[0][...] = (value_refs[0][...].astype(F32) + total).astype(LOW)

    return on_rows(kernel, shares, [values], [], [LOW], 0, "add_low", behind)[0]


def norm_back(shares, values, gain, grad, outs, behind=()):
    def kernel(total, value_refs, table_refs, out_refs, sum_refs):
        scaled, inv_std = centre(value_refs[0][...].astype(F32))
        part = total * table_refs[0][...]
        first = jnp.mean(part, axis=1, keepdims=True)
        second = jnp.mean(part * scaled, axis=1, keepdims=True)
        result = value_refs[1][...].astype(F32) + inv_std * (part - first - scaled * second)
        for ref in out_refs:
            ref[...] = result.astype(ref.dtype)
        sums = sum_refs[0]

        @pl.when(pl.program_id(0) == 0)
        def _():
            sums[...] = jnp.zeros_like(sums)

        sums[0:1, :] += jnp.sum(total * scaled, axis=0, keepdims=True)
        sums[1:2, :] += jnp.sum(total, axis=0, keepdims=True)

    return on_rows(kernel, shares, [values, grad], [gain], outs, 1, "norm_back", behind)


def qkv_back(mine, theirs, my_grad, their_grad, behind=()):
    rows, feat = mine.shape
    count, _, cols = my_grad.shape
    tm = tiles(feat, 512)

    def kernel(mine_ref, theirs_ref, my_ref, their_ref, *refs):
        one, two = mine_ref[...].T, theirs_ref[...].T
        for c in range(count):
            refs[-1][c] = (dot_nn(one, my_ref[c]) + dot_nn(two, their_ref[c])).astype(LOW)

    tall = pl.BlockSpec((rows, tm), lambda i: (0, i))
    whole = pl.BlockSpec((count, rows, cols), lambda i: (0, 0, 0))
    return pl.pallas_call(
        kernel,
        grid=(feat // tm,),
        in_specs=[tall, tall, whole, whole] + [ANYWHERE] * len(behind),
        out_specs=pl.BlockSpec((count, tm, cols), lambda i: (0, i, 0)),
        out_shape=jax.ShapeDtypeStruct((count, feat, cols), LOW),
        cost_estimate=light(
            flops=4 * count * rows * feat * cols,
            bytes_accessed=4 * rows * feat + 4 * count * rows * cols + 2 * count * feat * cols,
            transcendentals=0,
        ),
        compiler_params=pltpu.CompilerParams(vmem_limit_bytes=VMEM_BYTES),
        name="grad_qkv",
    )(mine, theirs, my_grad, their_grad, *behind)


def turn(value, behind=()):
    count, rows, cols = value.shape
    tn = tiles(cols, 128)

    def kernel(value_ref, *refs):
        refs[-1][...] = value_ref[...].astype(F32).T

    return pl.pallas_call(
        kernel,
        grid=(count, cols // tn),
        in_specs=[pl.BlockSpec((None, rows, tn), lambda c, j: (c, 0, j))] + [ANYWHERE] * len(behind),
        out_specs=pl.BlockSpec((None, tn, rows), lambda c, j: (c, j, 0)),
        out_shape=jax.ShapeDtypeStruct((count, cols, rows), F32),
        cost_estimate=light(flops=count * rows * cols, bytes_accessed=6 * count * rows * cols, transcendentals=0),
        compiler_params=pltpu.CompilerParams(vmem_limit_bytes=VMEM_BYTES),
        name="turn",
    )(value, *behind)


class Place:
    def __init__(self):
        self.fsdp = lax.axis_size("fsdp")
        self.context = lax.axis_size("context")
        self.tensor = lax.axis_size("tensor")
        self.pairs = self.tensor // 2
        self.z = lax.axis_index("fsdp")
        self.x = lax.axis_index("context")
        self.t = lax.axis_index("tensor")
        self.y = self.t // 2
        self.core = self.t % 2

    def square(self, seqs):
        return self.context == 2 and self.pairs == 2 and seqs == 1

    def size(self, which):
        return self.context if which == "x" else self.pairs

    def at(self, which):
        return self.x if which == "x" else self.y

    def shift(self, value, which, step):
        if which == "z":
            n = self.fsdp
            return lax.ppermute(value, "fsdp", [(i, (i + step) % n) for i in range(n)])
        if which == "x":
            n = self.context
            return lax.ppermute(value, "context", [(i, (i + step) % n) for i in range(n)])
        n = self.tensor
        return lax.ppermute(value, "tensor", [(i, (i + 2 * step) % n) for i in range(n)])

    def swap(self, value):
        return lax.ppermute(value, "tensor", [(i, i ^ 1) for i in range(self.tensor)])


def pick(value, index, axis):
    return lax.dynamic_index_in_dim(value, index, axis, keepdims=False)


def scatter_stage(place, value, axis, which):
    n, at = place.size(which), place.at(which)
    total = pick(value, at, axis).astype(F32)
    for step in range(1, n):
        sent = pick(value, (at + step) % n, axis)
        total = total + place.shift(sent, which, step).astype(F32)
    return total


def gather_stage(place, value, axis, which):
    n, at = place.size(which), place.at(which)
    if n == 1:
        return value
    if n == 2:
        return ordered(at, value, place.shift(value, which, 1), axis)
    parts = [value] + [place.shift(value, which, step) for step in range(1, n)]
    order = (at - jnp.arange(n)) % n
    shape = list(value.shape)
    shape[axis] = n * shape[axis]
    return jnp.take(jnp.stack(parts, axis), order, axis=axis).reshape(shape)


class Gathered:
    def __init__(self, place, value, axis):
        self.place, self.value, self.axis = place, value, axis
        if place.context == 2:
            self.raw = place.shift(value, "x", 1)
        else:
            self.raw = gather_stage(place, value, axis, "x")

    def whole(self):
        if self.place.context != 2:
            return self.raw
        return ordered(self.place.x, self.value, self.raw, self.axis)


def ordered(at, mine, other, axis):
    first = jnp.where(at == 0, mine, other)
    second = jnp.where(at == 0, other, mine)
    return jnp.concatenate([first, second], axis=axis)


def after(value, *others):
    return lax.optimization_barrier((value,) + others)[0]


class RowSum:
    def __init__(self, place, kind, terms, seqs, name, behind=()):
        self.place = place
        self.square = place.square(seqs)
        if self.square:
            self.keep_first, self.sent, self.keep_second, self.second = products_apart(
                place, kind, terms, 512, name, behind
            )
            return
        value = self.sent = products(kind, terms, 1024, 512, name, behind=behind)
        feat = value.shape[1]
        value = value.reshape(seqs, place.context, place.pairs, -1, feat)
        first, second = value[..., : feat // 2], value[..., feat // 2 :]
        first = scatter_stage(place, first, 1, "x").astype(LOW)
        second = scatter_stage(place, second, 2, "y").astype(LOW)
        first = scatter_stage(place, first, 1, "y").reshape(-1, feat // 2)
        second = scatter_stage(place, second, 1, "x").reshape(-1, feat // 2)
        nothing = jnp.zeros(first.shape, LOW)
        self.shares = [first, nothing, second, nothing]

    def start(self, *others):
        if self.square:
            first, second = after((self.sent, self.second), *others) if others else (self.sent, self.second)
            self.came_first = self.place.shift(first, "x", 1)
            self.came_second = self.place.shift(second, "y", 1)
        return self

    def follow(self, behind=()):
        if not self.square:
            return self.shares[0]
        first, first_goes, second, second_goes = join(
            self.keep_first, self.came_first, self.keep_second, self.came_second, behind
        )
        self.shares = [first, self.place.shift(first_goes, "y", 1), second, self.place.shift(second_goes, "x", 1)]
        return first


def spread_rows(place, value, seqs, behind=()):
    feat = value.shape[-1]
    half = feat // 2
    if place.square(seqs):
        over_x = place.shift(value, "x", 1)
        over_y = place.shift(value, "y", 1)
        far_first = place.shift(over_y[:, :half], "x", 1)
        far_second = place.shift(over_x[:, half:], "y", 1)
        whole = lay_rows(place.x, place.y, value, over_x, over_y, [far_first, far_second], LOW, behind)
        return whole.reshape(-1, feat)
    value = value.reshape(seqs, -1, feat)
    rows = value.shape[1]
    first, second = value[..., :half], value[..., half:]
    first = gather_stage(place, first, 1, "y")
    second = gather_stage(place, second, 1, "x")
    first = gather_stage(place, first, 1, "x")
    second = second.reshape(seqs, place.context, rows, half)
    second = gather_stage(place, second, 2, "y").reshape(first.shape)
    return jnp.concatenate([first, second], axis=-1).reshape(-1, feat)


class WholeRows:
    def __init__(self, place, value, seqs):
        self.place, self.value, self.seqs = place, value, seqs
        if place.square(seqs):
            self.over_y, self.over_core = place.shift(value, "y", 1), place.swap(value)
        else:
            self.over_y = gather_stage(place, value.reshape(seqs, -1, value.shape[-1]), 1, "y")
            self.over_core = place.swap(self.over_y)

    def whole(self, dtype, ready=(), behind=()):
        place, value = self.place, self.value
        if not place.square(self.seqs):
            return ordered(place.core, self.over_y, self.over_core, 0).astype(dtype)
        far = [place.swap(after(self.over_y, *ready) if ready else self.over_y)]
        whole = lay_rows(place.core, place.y, value, self.over_core, self.over_y, far, dtype, behind)
        return whole.reshape(2, -1, value.shape[-1])


def other_rows(place, value):
    rows = value.shape[0] // 2
    straight = place.shift(lax.dynamic_slice_in_dim(value, place.y * rows, rows, 0), "x", 1)
    return [value[:rows], value[rows:], straight, place.shift(straight, "y", 1)]


def other_places(place):
    x, y = place.x, place.y
    return [2 * x, 2 * x + 1, 2 * (1 - x) + y, 2 * (1 - x) + 1 - y]


def empty_kernel(*refs):
    pass


def empty(shape, dtype, behind=()):
    return pl.pallas_call(
        empty_kernel,
        in_specs=[ANYWHERE] * len(behind),
        out_specs=ANYWHERE,
        out_shape=jax.ShapeDtypeStruct(shape, dtype),
        name="empty",
    )(*behind)


def lay_shards(place, shard, before, behind, low, high, ready):
    n, z = place.fsdp, place.z
    blocks, size, cols = shard.shape
    whole = empty((blocks, n * size, cols), shard.dtype, ready)
    for part, block, start in (
        (shard, 0, z),
        (before[:, :size], 0, (z + 3) % n),
        (behind[:, :size], 0, (z + 1) % n),
        (low[:, :size], 0, (z + 2) % n),
        (high, blocks // 2, (z + 2) % n),
    ):
        whole = lax.dynamic_update_slice(whole, part, (block, start * size, 0))
    return whole


class Shards:
    def __init__(self, place, grad, axis, half_axis, begin):
        self.place, self.grad, self.axis, self.half_axis = place, grad, axis, half_axis
        self.size = grad.shape[axis] // place.fsdp
        self.half = (self.size if axis == half_axis else grad.shape[half_axis]) // 2

        def pair(one, two):
            return after(jnp.stack([one, two]).astype(LOW), begin)

        self.left = place.shift(pair(self.part(2, 1), self.part(1, 0)), "z", 1)
        self.right = place.shift(pair(self.part(2, 0), self.part(3, 1)), "z", -1)

    def part(self, ahead, side):
        place, half = self.place, self.half
        start = (place.z + ahead) % place.fsdp * self.size
        shard = lax.dynamic_slice_in_dim(self.grad, start, self.size, self.axis)
        return lax.slice_in_dim(shard, side * half, (side + 1) * half, axis=self.half_axis).astype(F32)

    def follow(self, *ready):
        place = self.place
        self.left, self.right = after((self.left, self.right), *ready)
        high = (self.part(1, 1) + self.left[0].astype(F32)).astype(LOW)
        low = (self.part(3, 0) + self.right[0].astype(F32)).astype(LOW)
        self.high, self.low = place.shift(high, "z", 1), place.shift(low, "z", -1)
        return low

    def total(self, *ready):
        high, low = after((self.high, self.low), *ready) if ready else (self.high, self.low)
        low = self.part(0, 0) + self.left[1].astype(F32) + low.astype(F32)
        high = self.part(0, 1) + self.right[1].astype(F32) + high.astype(F32)
        return jnp.concatenate([low.astype(LOW), high.astype(LOW)], axis=self.half_axis)


def total_over(place, value, which):
    n = {"z": place.fsdp, "x": place.context, "y": place.pairs, "core": 2}[which]
    if n == 1:
        return value
    if which == "core":
        return value + place.swap(value)
    if n == 2:
        return value + place.shift(value, which, 1)
    at = {"z": place.z, "x": place.x, "y": place.y}[which]
    parts = jnp.zeros((n,) + value.shape, value.dtype)
    parts = lax.dynamic_update_index_in_dim(parts, value, at, 0)
    for step in range(1, n):
        sent = place.shift(value, which, step)
        parts = lax.dynamic_update_index_in_dim(parts, sent, (at - step) % n, 0)
    return jnp.sum(parts, axis=0)


def small_totals(place, sums, bias, bias_other):
    n, z = place.fsdp, place.z
    feat = sums.shape[1]
    pad = [(0, 1), (0, 0)]
    sent = place.swap(jnp.concatenate([sums, jnp.pad(bias_other, pad)], axis=1))
    sums, bias = sums + sent[:, :feat], jnp.pad(bias, pad) + sent[:, feat:]
    size = feat // n
    came = []
    for step in range(n):
        part = lax.dynamic_slice_in_dim(sums, (z + step) % n * size, size, 1)
        part = jnp.concatenate([part, bias], axis=1)
        came.append(place.shift(part, "z", step) if step else part)
    came = lax.optimization_barrier(tuple(came))
    parts = jnp.zeros((n,) + came[0].shape, F32)
    for step in range(n):
        parts = lax.dynamic_update_index_in_dim(parts, came[step], (z - step) % n, 0)
    return jnp.sum(parts, axis=0)


def last_totals(place, totals, size):
    if place.context == 2:
        sent = place.shift(totals, "x", 1)
        return totals[:, :size] + sent[:, :size], ordered(place.x, totals[:3, size:], sent[:3, size:], 1)
    return total_over(place, totals[:, :size], "x"), gather_stage(place, totals[:3, size:], 1, "x")


def local(
    hidden_in,
    norm_gains,
    norm_biases,
    qkv_weight,
    qkv_bias,
    out_weight,
    gate_up_weight,
    down_weight,
    cotangent,
):
    place = Place()
    all_seqs, part_rows, feat = hidden_in.shape
    seqs = all_seqs // 2
    length = part_rows * place.context
    own_rows = part_rows // place.pairs
    head_cols = qkv_bias.shape[1] // place.context
    hidden_cols = down_weight.shape[0] // place.context

    def columns(value, count, axis):
        return lax.dynamic_slice_in_dim(value, place.x * count, count, axis)

    def own_sequences(value):
        return lax.dynamic_slice_in_dim(value, place.core * seqs, seqs, 0)

    def own_piece(value):
        return lax.dynamic_slice_in_dim(value, place.y * own_rows, own_rows, 1)

    pack = jnp.concatenate(
        [columns(qkv_weight, head_cols, 2), columns(out_weight, head_cols, 0).T[None]]
    )
    norm_part = jnp.concatenate([norm_gains, norm_biases]).reshape(-1, head_cols)
    norm_rows = norm_part.shape[0]
    pad = -norm_rows % 16
    part_feat = pack.shape[1]
    norm_block = jnp.pad(norm_part, [(0, pad), (0, 0)])[None]
    extra = jnp.pad(norm_block, [(0, 3), (0, 0), (0, 0)])
    pack = jnp.concatenate([pack, extra], axis=1)
    pack_before, pack_behind = place.shift(pack, "z", 1), place.shift(pack, "z", -1)
    bias = columns(qkv_bias, head_cols, 1)
    bias_swapped = place.swap(bias)
    bias_other = bias_swapped.astype(F32)[None, :, None, :]
    bias = bias.astype(F32)[None, :, None, :]
    hidden_mine = own_sequences(hidden_in).reshape(-1, feat)
    top_mine = own_sequences(cotangent)
    if place.square(seqs):
        pieces = other_rows(place, hidden_mine)
        top_pieces = other_rows(place, top_mine.reshape(-1, feat))
        pack_before, pack_behind = after((pack_before, pack_behind), pieces[2], bias_swapped)
    else:
        whole = gather_stage(place, hidden_mine.reshape(seqs, -1, feat), 1, "x").reshape(-1, feat)
        pieces = top_pieces = [whole] * 4
    half = pack.shape[0] // 2
    pack_low = place.shift(pack_before[:half], "z", 1)
    pack_high = place.shift(pack_behind[half:, :part_feat], "z", -1)
    norms = jnp.zeros((2, 2, feat), F32)
    for step, piece in (
        (0, norm_block),
        (1, pack_before[:1, part_feat:]),
        (2, pack_low[:1, part_feat:]),
        (3, pack_behind[:1, part_feat:]),
    ):
        piece = piece[0, :norm_rows].reshape(2, 2, part_feat).astype(F32)
        norms = lax.dynamic_update_slice(norms, piece, (0, 0, (place.z - step) % place.fsdp * part_feat))
    gains, shifts = norms[0][:, None, :], norms[1][:, None, :]
    gate_up_part = columns(gate_up_weight, hidden_cols, 2).transpose(0, 2, 1)
    down_part = columns(down_weight, hidden_cols, 0)
    if place.square(seqs):
        normed = norm_first(other_places(place), pieces, gains[0], shifts[0])
        top_last = top_pieces[3]
    else:
        normed = (centre(whole.astype(F32))[0] * gains[0] + shifts[0]).astype(LOW)
        grad_top = top_last = gather_stage(place, top_mine, 1, "x").reshape(seqs * length, feat)
    w_attn = lay_shards(place, pack[:, :part_feat], pack_before, pack_behind, pack_low, after(pack_high, normed), [pieces[3], gate_up_part, down_part])
    gate_up_part, down_part = after((gate_up_part, down_part), pack_low, pack_high, top_pieces[2])
    w_gate_up = lax.all_gather(gate_up_part, "fsdp", axis=2, tiled=True)
    w_down = lax.all_gather(down_part, "fsdp", axis=1, tiled=True)
    tables = rotary_tables(length, min(head_cols, 128))
    w_attn_other = place.swap(w_attn)

    def attend(weight, bias, behind):
        mixed = jnp.einsum("rd,cde->cre", normed, weight[:3], preferred_element_type=F32)
        return attend_forward(mixed[None], bias, tables, seqs, length, behind)

    kept = attend(w_attn, bias, [])
    kept_other = attend(w_attn_other, bias_other, [kept[3], top_last])
    attended, attended_other = kept[3][0], kept_other[3][0]
    attn_sum = RowSum(
        place,
        "nt",
        [(attended, (), w_attn, (3,)), (attended_other, (), w_attn_other, (3,))],
        seqs,
        "out",
    ).start()
    if place.square(seqs):
        grad_top = lay_pieces(other_places(place), top_pieces, [attn_sum.sent])
    theirs_top, theirs_one, theirs_attended = place.swap(grad_top), place.swap(normed), place.swap(attended_other)
    attn_sum.follow([grad_top])
    inputs = own_piece(hidden_mine.reshape(seqs, -1, feat)).reshape(-1, feat)
    middle, normed_two = add_norm(
        attn_sum.shares, inputs, gains[1], shifts[1], behind=[theirs_attended]
    )
    normed_two = spread_rows(place, normed_two, seqs, [theirs_top, theirs_one])

    w_gate_up_other = place.swap(after(w_gate_up, middle))
    turned_other, slope_other, hidden_part = gate_up(normed_two, w_gate_up_other)
    theirs_turned, w_down_other = place.swap(turned_other), place.swap(after(w_down, turned_other))
    turned, slope, hidden = gate_up(normed_two, w_gate_up)
    grad_down = products(
        "nn",
        [(turned, (), grad_top, ()), (theirs_turned, (), theirs_top, ())],
        hidden_cols,
        512,
        "grad_down",
    )
    down_sum = lax.psum_scatter(grad_down, "fsdp", scatter_dimension=1, tiled=True)
    grad_gu_turned_other, grad_gu_other = hidden_back(grad_top, w_down_other, slope_other, [grad_down])
    theirs_gu, theirs_two = place.swap(grad_gu_turned_other), place.swap(normed_two)
    grad_gu_turned, grad_gu = hidden_back(grad_top, w_down, slope, [grad_gu_other])
    two_sum = RowSum(
        place,
        "nn",
        [(grad_gu, (c,), w_gate_up, (c,)) for c in range(2)]
        + [(grad_gu_other, (c,), w_gate_up_other, (c,)) for c in range(2)],
        seqs,
        "grad_two",
        behind=[theirs_two, theirs_gu],
    ).start()
    grad_gate_up = products(
        "nn",
        [(grad_gu_turned, (), normed_two, ()), (theirs_gu, (), theirs_two, ())],
        hidden_cols,
        512,
        "grad_gate_up",
        count=2,
        behind=[two_sum.sent],
    )
    two_next = two_sum.follow([grad_gate_up, down_sum])
    gate_up_sum = lax.psum_scatter(after(grad_gate_up, two_next), "fsdp", scatter_dimension=2, tiled=True)
    down_sums = RowSum(
        place,
        "nn",
        [(hidden, (), w_down, ()), (hidden_part, (), w_down_other, ())],
        seqs,
        "down",
        behind=[two_next],
    )
    top_rows = own_piece(top_mine).reshape(-1, feat)
    grad_middle, mid_low, sums_two = norm_back(
        two_sum.shares, middle, gains[1], top_rows, [F32, LOW], behind=[down_sums.sent]
    )
    grad_mid_low = spread_rows(place, mid_low, seqs)
    down_gathered = Gathered(place, after(down_sum, grad_mid_low), 0)
    down_sums.start(grad_mid_low)

    def attend_grad(kept, weight, behind):
        grad_att = products("nn", [(grad_mid_low, (), weight, (3,))], 1024, head_cols, "grad_att", behind=behind)
        return attend_back(*kept, grad_att[None], tables, seqs, length)[0]

    theirs_mid = place.swap(grad_mid_low)
    grad_mixed_other = attend_grad(kept_other, w_attn_other, [])
    theirs_mixed = place.swap(grad_mixed_other)
    grad_out = products(
        "tn",
        [(grad_mid_low, (), attended, ()), (theirs_mid, (), theirs_attended, ())],
        512,
        head_cols,
        "grad_out",
        behind=[grad_mixed_other],
    )
    down_next = down_sums.follow([grad_out])
    grad_mixed = attend_grad(kept, w_attn, [down_next])
    final_out = add_low(down_sums.shares, middle, behind=[grad_mixed])
    out_sum = lax.psum_scatter(grad_out, "fsdp", scatter_dimension=0, tiled=True)
    one_sum = RowSum(
        place,
        "nt",
        [(grad_mixed, (c,), w_attn, (c,)) for c in range(3)]
        + [(grad_mixed_other, (c,), w_attn_other, (c,)) for c in range(3)],
        seqs,
        "grad_one",
        behind=[final_out, down_gathered.raw],
    ).start()
    grad_qkv = qkv_back(
        normed, theirs_one, grad_mixed, theirs_mixed, behind=[one_sum.sent, gate_up_sum]
    )
    qkv_shards = Shards(place, grad_qkv, 1, 1, grad_mixed)
    one_next = one_sum.follow([grad_qkv])
    qkv_next = qkv_shards.follow(one_next)
    layer_rows = WholeRows(place, after(final_out, one_sum.shares[1], one_sum.shares[3]), seqs)
    input_low, sums_one = norm_back(
        one_sum.shares, inputs, gains[0], grad_middle, [LOW], behind=[one_next, qkv_next]
    )
    gate_up_out = lax.all_gather(gate_up_sum, "context", axis=1, tiled=True)
    gate_up_out = turn(gate_up_out)
    sums = after(jnp.concatenate([sums_one, sums_two]), layer_rows.over_y)
    sums = total_over(place, sums, "y")
    input_rows = WholeRows(place, after(input_low, sums), seqs)
    layer_out = layer_rows.whole(LOW)
    totals = small_totals(
        place,
        after(sums, qkv_shards.low, qkv_shards.high, gate_up_out, input_rows.over_y, layer_out),
        jnp.sum(grad_mixed.astype(F32), axis=1),
        jnp.sum(grad_mixed_other.astype(F32), axis=1),
    )
    qkv_sum = qkv_shards.total()
    qkv_gathered = Gathered(place, qkv_sum, 2)
    out_gathered = Gathered(place, after(out_sum, qkv_sum), 1)
    sums, grad_bias = last_totals(place, after(totals, qkv_sum), norm_gains.shape[1])
    input_grad = input_rows.whole(F32, [qkv_gathered.raw])

    return (
        layer_out,
        input_grad,
        sums[0::2],
        sums[1::2],
        qkv_gathered.whole().astype(F32),
        grad_bias,
        out_gathered.whole().T.astype(F32),
        gate_up_out,
        down_gathered.whole().astype(F32),
    )


def solution(mesh):
    placed = (
        P("fsdp", "context", None),
        P(None, "fsdp"),
        P(None, "fsdp"),
        P(None, "fsdp", "tensor"),
        P(None, "tensor"),
        P("tensor", "fsdp"),
        P(None, "fsdp", "tensor"),
        P("tensor", "fsdp"),
        P("fsdp", "context", None),
    )
    return jax.shard_map(
        local,
        mesh=mesh,
        in_specs=placed,
        out_specs=(
            P("fsdp", "context", None),
            P("fsdp", "context", None),
            P(None, "fsdp"),
            P(None, "fsdp"),
            P(None, "fsdp", "tensor"),
            P(None, "tensor"),
            P("tensor", "fsdp"),
            P(None, "fsdp", "tensor"),
            P("tensor", "fsdp"),
        ),
        check_vma=False,
    )
```

```python
import math

import jax
import jax.numpy as jnp
import numpy as np
from jax import lax
from jax.experimental import pallas as pl
from jax.experimental.pallas import tpu as pltpu
from jax.sharding import PartitionSpec as P

HEAD_DIM = 64
ROT = 16
EPSILON = 1e-05
F32 = jnp.float32
LOW = jnp.bfloat16


def rotary_tables(length, width):
    column = np.arange(width) % HEAD_DIM
    half = ROT // 2
    frequency = np.power(10000.0, -2.0 * (column % half) / ROT).astype(np.float32)
    angles = np.arange(length, dtype=np.float32)[:, None] * frequency[None, :]
    inside = column < ROT
    lower = column < half
    sine = np.sin(angles)
    cosine = np.where(inside, np.cos(angles), 1.0)
    minus = np.where(lower, -sine, 0.0)
    plus = np.where(inside & ~lower, sine, 0.0)
    return jnp.asarray(np.stack([cosine, minus, plus]).astype(np.float32))

def light(flops, bytes_accessed, transcendentals):
    return pl.CostEstimate(flops=flops // 100, bytes_accessed=bytes_accessed // 100, transcendentals=0)


def dot_nt(a,b): return lax.dot_general(a,b,(((1,),(1,)),((),())),preferred_element_type=F32)
def dot_nn(a,b): return lax.dot_general(a,b,(((1,),(0,)),((),())),preferred_element_type=F32)
def dot_tn(a,b): return lax.dot_general(a,b,(((0,),(0,)),((),())),preferred_element_type=F32)

def head_masks(width):
    lane=lax.broadcasted_iota(jnp.int32,(1,width),1)
    return [ (lane//HEAD_DIM)==h for h in range(width//HEAD_DIM)]

def fwd_kernel(block, mixed_ref, bias_ref, table_ref, *refs):
    q_ref, k_ref, v_ref, att_ref, lse_ref = refs[-5:]
    length, width = q_ref.shape
    half=ROT//2
    def rotated(c):
        v=mixed_ref[c]+bias_ref[c]
        return v*table_ref[0]+pltpu.roll(v,width-half,1)*table_ref[1]+pltpu.roll(v,half,1)*table_ref[2]
    q_ref[...]=(rotated(0)*(1.0/math.sqrt(HEAD_DIM))).astype(LOW)
    k_ref[...]=rotated(1).astype(LOW)
    v_ref[...]=(mixed_ref[2]+bias_ref[2]).astype(LOW)
    masks=head_masks(width)
    row=lax.broadcasted_iota(jnp.int32,(block,block),0)
    col=lax.broadcasted_iota(jnp.int32,(block,block),1)
    for i in range(length//block):
        rows=pl.ds(i*block,block)
        q=q_ref[rows,:]
        out=jnp.zeros((block,width),F32); lse=jnp.zeros((block,width),F32)
        for mask in masks:
            qh=jnp.where(mask,q,jnp.zeros_like(q))
            diag=jnp.where(row>=col,dot_nt(qh,k_ref[rows,:]),-1e30)
            top=jnp.max(diag,axis=1,keepdims=True)
            if i>0:
                rest=dot_nt(qh,k_ref[pl.ds(0,i*block),:])
                top=jnp.maximum(top,jnp.max(rest,axis=1,keepdims=True))
            diag=jnp.exp(diag-top)
            total=jnp.sum(diag,axis=1,keepdims=True)
            acc=dot_nn(diag.astype(LOW),v_ref[rows,:])
            if i>0:
                rest=jnp.exp(rest-top)
                total=total+jnp.sum(rest,axis=1,keepdims=True)
                acc=acc+dot_nn(rest.astype(LOW),v_ref[pl.ds(0,i*block),:])
            out=jnp.where(mask,acc/total,out)
            lse=jnp.where(mask,top+jnp.log(total),lse)
        att_ref[rows,:]=out.astype(LOW)
        lse_ref[rows,:]=lse

def attend_forward(mixed,bias,tables,seqs,length,behind=(),block=256):
    pair,_,rows,cols=mixed.shape
    width=min(cols,128); groups=cols//width
    tok=lambda o,s,g:(o,s,g)
    spec=pl.BlockSpec((None,length,width),tok)
    shape=lambda d:jax.ShapeDtypeStruct((pair,rows,cols),d)
    return pl.pallas_call(
        lambda *r: fwd_kernel(block,*r),
        grid=(pair,seqs,groups),
        in_specs=[pl.BlockSpec((None,3,length,width),lambda o,s,g:(o,0,s,g)),
                  pl.BlockSpec((None,3,1,width),lambda o,s,g:(o,0,0,g)),
                  pl.BlockSpec((3,length,width),lambda o,s,g:(0,0,0))]+[pl.BlockSpec(memory_space=pl.ANY)]*len(behind),
        out_specs=[spec]*5,
        out_shape=[shape(LOW)]*4+[shape(F32)],
        compiler_params=pltpu.CompilerParams(vmem_limit_bytes=48<<20),
        cost_estimate=light(flops=int(4*pair*rows*length*cols*0.6),bytes_accessed=pair*rows*cols*26,transcendentals=pair*rows*length*cols//128),
        name="attend_forward",
    )(mixed,bias,tables,*behind)

def bwd_kernel(block,q_ref,k_ref,v_ref,att_ref,lse_ref,do_ref,table_ref,out_ref,dk_acc,dv_acc,dq_acc):
    length,width=q_ref.shape
    half=ROT//2
    masks=head_masks(width)
    row=lax.broadcasted_iota(jnp.int32,(block,block),0)
    col=lax.broadcasted_iota(jnp.int32,(block,block),1)
    count=length//block
    for i in reversed(range(count)):
        rows=pl.ds(i*block,block)
        q=q_ref[rows,:]; do=do_ref[rows,:]; lse=lse_ref[rows,:]
        prod=do.astype(F32)*att_ref[rows,:].astype(F32)
        n=(i+1)*block
        keys=k_ref[pl.ds(0,n),:]; vals=v_ref[pl.ds(0,n),:]
        dq=jnp.zeros((block,width),F32)
        dk=None
        for h,mask in enumerate(masks):
            qh=jnp.where(mask,q,jnp.zeros_like(q)); dh=jnp.where(mask,do,jnp.zeros_like(do))
            delta=jnp.sum(jnp.where(mask,prod,0.0),axis=1,keepdims=True)
            lse_h=lse[:,h*HEAD_DIM:h*HEAD_DIM+1]
            s=dot_nt(qh,keys)
            p=jnp.exp(s-lse_h)
            if i==0:
                p=jnp.where(row>=col,p,0.0)
            else:
                p=jnp.concatenate([p[:,:n-block],jnp.where(row>=col,p[:,n-block:],0.0)],axis=1)
            dp=dot_nt(dh,vals)
            ds=(p*(dp-delta)).astype(LOW)
            pl_low=p.astype(LOW)
            dq=jnp.where(mask,dot_nn(ds,keys),dq)
            tk=dot_tn(ds,qh); tv=dot_tn(pl_low,dh)
            dk=tk if dk is None else dk+tk
            dv=tv if h==0 else dv+tv
        dq_acc[rows,:]=dq*(1.0/math.sqrt(HEAD_DIM))
        if i==count-1:
            dk_acc[...]=dk; dv_acc[...]=dv
        else:
            dk_acc[pl.ds(0,n),:]+=dk; dv_acc[pl.ds(0,n),:]+=dv
    def back(v):
        return v*table_ref[0]+pltpu.roll(v*table_ref[1],half,1)+pltpu.roll(v*table_ref[2],width-half,1)
    out_ref[0]=back(dq_acc[...]).astype(LOW)
    out_ref[1]=back(dk_acc[...]).astype(LOW)
    out_ref[2]=dv_acc[...].astype(LOW)

def attend_back(q,k,v,att,lse,grad,tables,seqs,length,block=256):
    pair,rows,cols=q.shape
    width=min(cols,128); groups=cols//width
    spec=pl.BlockSpec((None,length,width),lambda o,s,g:(o,s,g))
    return pl.pallas_call(
        lambda *r: bwd_kernel(block,*r),
        grid=(pair,seqs,groups),
        in_specs=[spec]*6+[pl.BlockSpec((3,length,width),lambda o,s,g:(0,0,0))],
        out_specs=pl.BlockSpec((None,3,length,width),lambda o,s,g:(o,0,s,g)),
        out_shape=jax.ShapeDtypeStruct((pair,3,rows,cols),LOW),
        scratch_shapes=[pltpu.VMEM((length,width),F32)]*3,
        compiler_params=pltpu.CompilerParams(vmem_limit_bytes=48<<20),
        cost_estimate=light(flops=int(10*pair*rows*length*cols*0.6),bytes_accessed=pair*rows*cols*20,transcendentals=pair*rows*length*cols//128),
        name="attend_back",
    )(q,k,v,att,lse,grad,tables)


VMEM_BYTES = 56 << 20
FORMS = {"nn": dot_nn, "nt": dot_nt, "tn": dot_tn}
ANYWHERE = pl.BlockSpec(memory_space=pl.ANY)


def tiles(size, most):
    while size > most and size % 2 == 0:
        size //= 2
    return size


def lead_spec(lead, block, where):
    return pl.BlockSpec((None,) * len(lead) + block, lambda *at: lead + where(*at))


def products(kind, terms, row_tile, col_tile, name, count=None, dtype=LOW, behind=()):
    one, _, two, _ = terms[0]
    deep = one.shape[-2] if kind == "tn" else one.shape[-1]
    rows = one.shape[-1] if kind == "tn" else one.shape[-2]
    cols = two.shape[-2] if kind == "nt" else two.shape[-1]
    tm, tn = tiles(rows, row_tile), tiles(cols, col_tile)
    one_block = ((deep, tm), lambda c, i, j: (0, i)) if kind == "tn" else ((tm, deep), lambda c, i, j: (i, 0))
    two_block = ((tn, deep), lambda c, i, j: (j, 0)) if kind == "nt" else ((deep, tn), lambda c, i, j: (0, j))
    number = len(terms)

    def kernel(*refs):
        total = sum(FORMS[kind](a[...], b[...]) for a, b in zip(refs[:number], refs[number : 2 * number]))
        refs[-1][...] = total.astype(dtype)

    if count is None:
        ones = [lead_spec(t[1], *one_block) for t in terms]
        out_spec = pl.BlockSpec((tm, tn), lambda c, i, j: (i, j))
        out_shape = (rows, cols)
    else:
        ones = [pl.BlockSpec((None,) + one_block[0], lambda c, i, j: (c,) + one_block[1](c, i, j)) for t in terms]
        out_spec = pl.BlockSpec((None, tm, tn), lambda c, i, j: (c, i, j))
        out_shape = (count, rows, cols)
    many = count or 1
    return pl.pallas_call(
        kernel,
        grid=(many, rows // tm, cols // tn),
        in_specs=ones + [lead_spec(t[3], *two_block) for t in terms] + [ANYWHERE] * len(behind),
        out_specs=out_spec,
        out_shape=jax.ShapeDtypeStruct(out_shape, dtype),
        compiler_params=pltpu.CompilerParams(vmem_limit_bytes=VMEM_BYTES),
        cost_estimate=light(
            flops=2 * rows * deep * cols * number * many,
            bytes_accessed=2 * (many * number * (rows * deep + deep * cols) + many * rows * cols),
            transcendentals=0,
        ),
        name=name,
    )(*[t[0] for t in terms], *[t[2] for t in terms], *behind)


def products_apart(place, kind, terms, col_tile, name, behind=()):
    one, _, two, _ = terms[0]
    deep = one.shape[-2] if kind == "tn" else one.shape[-1]
    rows = one.shape[-1] if kind == "tn" else one.shape[-2]
    cols = two.shape[-2] if kind == "nt" else two.shape[-1]
    tn = tiles(cols // 2, col_tile)
    half = cols // 2 // tn
    piece = rows // 4
    one_block = ((deep, rows), lambda j, at: (0, 0)) if kind == "tn" else ((rows, deep), lambda j, at: (0, 0))
    two_block = ((tn, deep), lambda j, at: (j, 0)) if kind == "nt" else ((deep, tn), lambda j, at: (0, j))
    number = len(terms)

    def kernel(at_ref, *refs):
        total = sum(FORMS[kind](a[...], b[...]) for a, b in zip(refs[:number], refs[number : 2 * number]))
        keep_first, send_first, keep_second, send_second, held = refs[-5:]
        held[...] = total.astype(LOW).reshape(held.shape)
        x, y = at_ref[0], at_ref[1]

        @pl.when(pl.program_id(0) < half)
        def _():
            for other in range(2):
                across = y if other == 0 else 1 - y
                keep_first[other] = held[2 * x + across]
                send_first[other] = held[2 * (1 - x) + across]

        @pl.when(pl.program_id(0) >= half)
        def _():
            for other in range(2):
                along = x if other == 0 else 1 - x
                keep_second[other] = held[2 * along + y]
                send_second[other] = held[2 * along + 1 - y]

    first = pl.BlockSpec((2, piece, tn), lambda j, at: (0, 0, jnp.minimum(j, half - 1)))
    second = pl.BlockSpec((2, piece, tn), lambda j, at: (0, 0, jnp.maximum(j - half, 0)))
    return pl.pallas_call(
        kernel,
        grid_spec=pltpu.PrefetchScalarGridSpec(
            num_scalar_prefetch=1,
            grid=(2 * half,),
            in_specs=[lead_spec(t[1], *one_block) for t in terms]
            + [lead_spec(t[3], *two_block) for t in terms]
            + [ANYWHERE] * len(behind),
            out_specs=[first, first, second, second],
            scratch_shapes=[pltpu.VMEM((4, piece, tn), LOW)],
        ),
        out_shape=[jax.ShapeDtypeStruct((2, piece, cols // 2), LOW)] * 4,
        compiler_params=pltpu.CompilerParams(vmem_limit_bytes=VMEM_BYTES),
        cost_estimate=light(
            flops=2 * rows * deep * cols * number,
            bytes_accessed=2 * (number * (rows * deep + deep * cols) + rows * cols),
            transcendentals=0,
        ),
        name=name,
    )(jnp.stack([place.x, place.y]).astype(jnp.int32), *[t[0] for t in terms], *[t[2] for t in terms], *behind)


def gate_kernel(weight_ref, rows_ref, turned_ref, slope_ref, hidden_ref):
    rows = rows_ref[...]
    gate = dot_nt(weight_ref[0], rows)
    up = dot_nt(weight_ref[1], rows)
    sig = 1.0 / (1.0 + jnp.exp(-gate))
    act = gate * sig
    hidden = (act * up).astype(LOW)
    turned_ref[...] = hidden
    hidden_ref[...] = hidden.T
    slope_ref[0] = (up * sig * (1.0 + gate * (1.0 - sig))).astype(LOW)
    slope_ref[1] = act.astype(LOW)


def gate_up(values, weight):
    rows, feat = values.shape
    units = weight.shape[1]
    tm = tiles(rows, 512)
    return pl.pallas_call(
        gate_kernel,
        grid=(rows // tm,),
        in_specs=[
            pl.BlockSpec((2, units, feat), lambda i: (0, 0, 0)),
            pl.BlockSpec((tm, feat), lambda i: (i, 0)),
        ],
        out_specs=[
            pl.BlockSpec((units, tm), lambda i: (0, i)),
            pl.BlockSpec((2, units, tm), lambda i: (0, 0, i)),
            pl.BlockSpec((tm, units), lambda i: (i, 0)),
        ],
        out_shape=[
            jax.ShapeDtypeStruct((units, rows), LOW),
            jax.ShapeDtypeStruct((2, units, rows), LOW),
            jax.ShapeDtypeStruct((rows, units), LOW),
        ],
        compiler_params=pltpu.CompilerParams(vmem_limit_bytes=VMEM_BYTES),
        cost_estimate=light(
            flops=4 * rows * feat * units,
            bytes_accessed=2 * (rows * feat + 2 * feat * units + 4 * rows * units),
            transcendentals=rows * units,
        ),
        name="gate_up",
    )(weight, values)


def hidden_back_kernel(weight_ref, grad_ref, slope_ref, *refs):
    turned_ref, out_ref = refs[-2:]
    grad = dot_nt(weight_ref[...], grad_ref[...])
    for c in range(2):
        part = (grad * slope_ref[c].astype(F32)).astype(LOW)
        turned_ref[c] = part
        out_ref[c] = part.T


def hidden_back(grad, weight, slope, behind=()):
    rows, feat = grad.shape
    units = weight.shape[0]
    tm = tiles(rows, 512)
    return pl.pallas_call(
        hidden_back_kernel,
        grid=(rows // tm,),
        in_specs=[
            pl.BlockSpec((units, feat), lambda i: (0, 0)),
            pl.BlockSpec((tm, feat), lambda i: (i, 0)),
            pl.BlockSpec((2, units, tm), lambda i: (0, 0, i)),
        ]
        + [ANYWHERE] * len(behind),
        out_specs=[
            pl.BlockSpec((2, units, tm), lambda i: (0, 0, i)),
            pl.BlockSpec((2, tm, units), lambda i: (0, i, 0)),
        ],
        out_shape=[
            jax.ShapeDtypeStruct((2, units, rows), LOW),
            jax.ShapeDtypeStruct((2, rows, units), LOW),
        ],
        compiler_params=pltpu.CompilerParams(vmem_limit_bytes=VMEM_BYTES),
        cost_estimate=light(
            flops=2 * rows * feat * units,
            bytes_accessed=2 * (rows * feat + feat * units + 6 * rows * units),
            transcendentals=0,
        ),
        name="hidden_back",
    )(weight, grad, slope, *behind)


def pieces_of(places, rows, feat, dtype, body, name, operands, behind=()):
    def kernel(at_ref, *refs):
        for step in range(len(places)):
            pl.when(pl.program_id(0) == step)(lambda step=step: body(step, refs, refs[-1]))

    specs = [pl.BlockSpec(v.shape, lambda i, at, n=v.ndim: (0,) * n) for v in operands]
    return pl.pallas_call(
        kernel,
        grid_spec=pltpu.PrefetchScalarGridSpec(
            num_scalar_prefetch=1,
            grid=(len(places),),
            in_specs=specs + [ANYWHERE] * len(behind),
            out_specs=pl.BlockSpec((None, rows, feat), lambda i, at: (at[i], 0, 0)),
        ),
        out_shape=jax.ShapeDtypeStruct((len(places), rows, feat), dtype),
        compiler_params=pltpu.CompilerParams(vmem_limit_bytes=VMEM_BYTES),
        cost_estimate=light(flops=0, bytes_accessed=4 * len(places) * rows * feat, transcendentals=0),
        name=name,
    )(jnp.stack(places).astype(jnp.int32), *operands, *behind)


def lay_rows(one, two, own, over_one, over_two, far, dtype, behind=()):
    rows, feat = own.shape

    def body(step, refs, out_ref):
        start = 0
        for ref in refs[step : step + 1] if step < 3 else refs[3 : 3 + len(far)]:
            out_ref[:, start : start + ref.shape[1]] = ref[...].astype(dtype)
            start += ref.shape[1]

    places = [2 * one + two, 2 * (1 - one) + two, 2 * one + 1 - two, 2 * (1 - one) + 1 - two]
    return pieces_of(places, rows, feat, dtype, body, "lay_rows", [own, over_one, over_two] + list(far), behind)


def norm_first(places, pieces, gain, shift, behind=()):
    rows, feat = pieces[0].shape

    def body(step, refs, out_ref):
        values = refs[step][...].astype(F32)
        out_ref[...] = (centre(values)[0] * refs[4][...] + refs[5][...]).astype(LOW)

    return pieces_of(places, rows, feat, LOW, body, "norm_first", pieces + [gain, shift], behind).reshape(-1, feat)


def lay_pieces(places, pieces, behind=()):
    rows, feat = pieces[0].shape

    def body(step, refs, out_ref):
        out_ref[...] = refs[step][...]

    return pieces_of(places, rows, feat, LOW, body, "lay_pieces", pieces, behind).reshape(-1, feat)


def join(keep_first, came_first, keep_second, came_second, behind=()):
    _, rows, half = keep_first.shape

    def kernel(one, two, three, four, *refs):
        first_stays, first_goes, second_stays, second_goes = refs[-4:]
        first_stays[...] = one[0].astype(F32) + two[0].astype(F32)
        first_goes[...] = (one[1].astype(F32) + two[1].astype(F32)).astype(LOW)
        second_stays[...] = three[0].astype(F32) + four[0].astype(F32)
        second_goes[...] = (three[1].astype(F32) + four[1].astype(F32)).astype(LOW)

    tm = tiles(rows, 128)
    pair = pl.BlockSpec((2, tm, half), lambda i: (0, i, 0))
    flat = pl.BlockSpec((tm, half), lambda i: (i, 0))
    shape = lambda dtype: jax.ShapeDtypeStruct((rows, half), dtype)
    return pl.pallas_call(
        kernel,
        grid=(rows // tm,),
        in_specs=[pair] * 4 + [ANYWHERE] * len(behind),
        out_specs=[flat] * 4,
        out_shape=[shape(F32), shape(LOW)] * 2,
        cost_estimate=light(flops=4 * rows * half, bytes_accessed=28 * rows * half, transcendentals=0),
        compiler_params=pltpu.CompilerParams(vmem_limit_bytes=VMEM_BYTES),
        name="join",
    )(keep_first, came_first, keep_second, came_second, *behind)


def on_rows(kernel, shares, values, tables, outs, sums, name, behind=()):
    rows, half = shares[0].shape
    feat = 2 * half
    tm = tiles(rows, 128)
    count, tabled = len(values), len(tables)

    def body(*refs):
        total = jnp.concatenate(
            [refs[0][...] + refs[1][...].astype(F32), refs[2][...] + refs[3][...].astype(F32)], axis=1
        )
        rest = refs[4 + count + tabled + len(behind) :]
        kernel(total, refs[4 : 4 + count], refs[4 + count : 4 + count + tabled], rest[: len(outs)], rest[len(outs) :])

    block = lambda cols: pl.BlockSpec((tm, cols), lambda i: (i, 0))
    return pl.pallas_call(
        body,
        grid=(rows // tm,),
        in_specs=[block(half)] * 4
        + [block(feat)] * count
        + [pl.BlockSpec((1, feat), lambda i: (0, 0))] * tabled
        + [ANYWHERE] * len(behind),
        out_specs=[block(feat)] * len(outs) + [pl.BlockSpec((2, feat), lambda i: (0, 0))] * sums,
        out_shape=[jax.ShapeDtypeStruct((rows, feat), dtype) for dtype in outs]
        + [jax.ShapeDtypeStruct((2, feat), F32)] * sums,
        cost_estimate=light(flops=20 * rows * feat, bytes_accessed=20 * rows * feat, transcendentals=0),
        compiler_params=pltpu.CompilerParams(vmem_limit_bytes=VMEM_BYTES),
        name=name,
    )(*shares, *values, *tables, *behind)


def centre(values):
    centred = values - jnp.mean(values, axis=1, keepdims=True)
    inv_std = lax.rsqrt(jnp.mean(centred * centred, axis=1, keepdims=True) + EPSILON)
    return centred * inv_std, inv_std


def add_norm(shares, values, gain, shift, behind=()):
    def kernel(total, value_refs, table_refs, out_refs, _):
        middle = value_refs[0][...].astype(F32) + total
        out_refs[0][...] = middle
        out_refs[1][...] = (centre(middle)[0] * table_refs[0][...] + table_refs[1][...]).astype(LOW)

    return on_rows(kernel, shares, [values], [gain, shift], [F32, LOW], 0, "add_norm", behind)


def add_low(shares, values, behind=()):
    def kernel(total, value_refs, _, out_refs, __):
        out_refs[0][...] = (value_refs[0][...].astype(F32) + total).astype(LOW)

    return on_rows(kernel, shares, [values], [], [LOW], 0, "add_low", behind)[0]


def norm_back(shares, values, gain, grad, outs, behind=()):
    def kernel(total, value_refs, table_refs, out_refs, sum_refs):
        scaled, inv_std = centre(value_refs[0][...].astype(F32))
        part = total * table_refs[0][...]
        first = jnp.mean(part, axis=1, keepdims=True)
        second = jnp.mean(part * scaled, axis=1, keepdims=True)
        result = value_refs[1][...].astype(F32) + inv_std * (part - first - scaled * second)
        for ref in out_refs:
            ref[...] = result.astype(ref.dtype)
        sums = sum_refs[0]

        @pl.when(pl.program_id(0) == 0)
        def _():
            sums[...] = jnp.zeros_like(sums)

        sums[0:1, :] += jnp.sum(total * scaled, axis=0, keepdims=True)
        sums[1:2, :] += jnp.sum(total, axis=0, keepdims=True)

    return on_rows(kernel, shares, [values, grad], [gain], outs, 1, "norm_back", behind)


def qkv_back(mine, theirs, my_grad, their_grad, behind=()):
    rows, feat = mine.shape
    count, _, cols = my_grad.shape
    tm = tiles(feat, 512)

    def kernel(mine_ref, theirs_ref, my_ref, their_ref, *refs):
        one, two = mine_ref[...].T, theirs_ref[...].T
        for c in range(count):
            refs[-1][c] = (dot_nn(one, my_ref[c]) + dot_nn(two, their_ref[c])).astype(LOW)

    tall = pl.BlockSpec((rows, tm), lambda i: (0, i))
    whole = pl.BlockSpec((count, rows, cols), lambda i: (0, 0, 0))
    return pl.pallas_call(
        kernel,
        grid=(feat // tm,),
        in_specs=[tall, tall, whole, whole] + [ANYWHERE] * len(behind),
        out_specs=pl.BlockSpec((count, tm, cols), lambda i: (0, i, 0)),
        out_shape=jax.ShapeDtypeStruct((count, feat, cols), LOW),
        cost_estimate=light(
            flops=4 * count * rows * feat * cols,
            bytes_accessed=4 * rows * feat + 4 * count * rows * cols + 2 * count * feat * cols,
            transcendentals=0,
        ),
        compiler_params=pltpu.CompilerParams(vmem_limit_bytes=VMEM_BYTES),
        name="grad_qkv",
    )(mine, theirs, my_grad, their_grad, *behind)


def turn(value, behind=()):
    count, rows, cols = value.shape
    tn = tiles(cols, 256)

    def kernel(value_ref, *refs):
        refs[-1][...] = value_ref[...].astype(F32).T

    return pl.pallas_call(
        kernel,
        grid=(count, cols // tn),
        in_specs=[pl.BlockSpec((None, rows, tn), lambda c, j: (c, 0, j))] + [ANYWHERE] * len(behind),
        out_specs=pl.BlockSpec((None, tn, rows), lambda c, j: (c, j, 0)),
        out_shape=jax.ShapeDtypeStruct((count, cols, rows), F32),
        cost_estimate=light(flops=count * rows * cols, bytes_accessed=6 * count * rows * cols, transcendentals=0),
        compiler_params=pltpu.CompilerParams(vmem_limit_bytes=VMEM_BYTES),
        name="turn",
    )(value, *behind)


class Place:
    def __init__(self):
        self.fsdp = lax.axis_size("fsdp")
        self.context = lax.axis_size("context")
        self.tensor = lax.axis_size("tensor")
        self.pairs = self.tensor // 2
        self.z = lax.axis_index("fsdp")
        self.x = lax.axis_index("context")
        self.t = lax.axis_index("tensor")
        self.y = self.t // 2
        self.core = self.t % 2

    def square(self, seqs):
        return self.context == 2 and self.pairs == 2 and seqs == 1

    def size(self, which):
        return self.context if which == "x" else self.pairs

    def at(self, which):
        return self.x if which == "x" else self.y

    def shift(self, value, which, step):
        if which == "z":
            n = self.fsdp
            return lax.ppermute(value, "fsdp", [(i, (i + step) % n) for i in range(n)])
        if which == "x":
            n = self.context
            return lax.ppermute(value, "context", [(i, (i + step) % n) for i in range(n)])
        n = self.tensor
        return lax.ppermute(value, "tensor", [(i, (i + 2 * step) % n) for i in range(n)])

    def swap(self, value):
        return lax.ppermute(value, "tensor", [(i, i ^ 1) for i in range(self.tensor)])


def pick(value, index, axis):
    return lax.dynamic_index_in_dim(value, index, axis, keepdims=False)


def scatter_stage(place, value, axis, which):
    n, at = place.size(which), place.at(which)
    total = pick(value, at, axis).astype(F32)
    for step in range(1, n):
        sent = pick(value, (at + step) % n, axis)
        total = total + place.shift(sent, which, step).astype(F32)
    return total


def gather_stage(place, value, axis, which):
    n, at = place.size(which), place.at(which)
    if n == 1:
        return value
    if n == 2:
        return ordered(at, value, place.shift(value, which, 1), axis)
    parts = [value] + [place.shift(value, which, step) for step in range(1, n)]
    order = (at - jnp.arange(n)) % n
    shape = list(value.shape)
    shape[axis] = n * shape[axis]
    return jnp.take(jnp.stack(parts, axis), order, axis=axis).reshape(shape)


class Gathered:
    def __init__(self, place, value, axis):
        self.place, self.value, self.axis = place, value, axis
        if place.context == 2:
            self.raw = place.shift(value, "x", 1)
        else:
            self.raw = gather_stage(place, value, axis, "x")

    def whole(self):
        if self.place.context != 2:
            return self.raw
        return ordered(self.place.x, self.value, self.raw, self.axis)


def ordered(at, mine, other, axis):
    first = jnp.where(at == 0, mine, other)
    second = jnp.where(at == 0, other, mine)
    return jnp.concatenate([first, second], axis=axis)


def after(value, *others):
    return lax.optimization_barrier((value,) + others)[0]


class RowSum:
    def __init__(self, place, kind, terms, seqs, name, behind=()):
        self.place = place
        self.square = place.square(seqs)
        if self.square:
            self.keep_first, self.sent, self.keep_second, self.second = products_apart(
                place, kind, terms, 512, name, behind
            )
            return
        value = self.sent = products(kind, terms, 1024, 512, name, behind=behind)
        feat = value.shape[1]
        value = value.reshape(seqs, place.context, place.pairs, -1, feat)
        first, second = value[..., : feat // 2], value[..., feat // 2 :]
        first = scatter_stage(place, first, 1, "x").astype(LOW)
        second = scatter_stage(place, second, 2, "y").astype(LOW)
        first = scatter_stage(place, first, 1, "y").reshape(-1, feat // 2)
        second = scatter_stage(place, second, 1, "x").reshape(-1, feat // 2)
        nothing = jnp.zeros(first.shape, LOW)
        self.shares = [first, nothing, second, nothing]

    def start(self, *others):
        if self.square:
            first, second = after((self.sent, self.second), *others) if others else (self.sent, self.second)
            self.came_first = self.place.shift(first, "x", 1)
            self.came_second = self.place.shift(second, "y", 1)
        return self

    def follow(self, behind=()):
        if not self.square:
            return self.shares[0]
        first, first_goes, second, second_goes = join(
            self.keep_first, self.came_first, self.keep_second, self.came_second, behind
        )
        self.shares = [first, self.place.shift(first_goes, "y", 1), second, self.place.shift(second_goes, "x", 1)]
        return first


def spread_rows(place, value, seqs, behind=()):
    feat = value.shape[-1]
    half = feat // 2
    if place.square(seqs):
        over_x = place.shift(value, "x", 1)
        over_y = place.shift(value, "y", 1)
        far_first = place.shift(over_y[:, :half], "x", 1)
        far_second = place.shift(over_x[:, half:], "y", 1)
        whole = lay_rows(place.x, place.y, value, over_x, over_y, [far_first, far_second], LOW, behind)
        return whole.reshape(-1, feat)
    value = value.reshape(seqs, -1, feat)
    rows = value.shape[1]
    first, second = value[..., :half], value[..., half:]
    first = gather_stage(place, first, 1, "y")
    second = gather_stage(place, second, 1, "x")
    first = gather_stage(place, first, 1, "x")
    second = second.reshape(seqs, place.context, rows, half)
    second = gather_stage(place, second, 2, "y").reshape(first.shape)
    return jnp.concatenate([first, second], axis=-1).reshape(-1, feat)


class WholeRows:
    def __init__(self, place, value, seqs):
        self.place, self.value, self.seqs = place, value, seqs
        if place.square(seqs):
            self.over_y, self.over_core = place.shift(value, "y", 1), place.swap(value)
        else:
            self.over_y = gather_stage(place, value.reshape(seqs, -1, value.shape[-1]), 1, "y")
            self.over_core = place.swap(self.over_y)

    def whole(self, dtype, ready=(), behind=()):
        place, value = self.place, self.value
        if not place.square(self.seqs):
            return ordered(place.core, self.over_y, self.over_core, 0).astype(dtype)
        far = [place.swap(after(self.over_y, *ready) if ready else self.over_y)]
        whole = lay_rows(place.core, place.y, value, self.over_core, self.over_y, far, dtype, behind)
        return whole.reshape(2, -1, value.shape[-1])


def other_rows(place, value):
    rows = value.shape[0] // 2
    straight = place.shift(lax.dynamic_slice_in_dim(value, place.y * rows, rows, 0), "x", 1)
    return [value[:rows], value[rows:], straight, place.shift(straight, "y", 1)]


def other_places(place):
    x, y = place.x, place.y
    return [2 * x, 2 * x + 1, 2 * (1 - x) + y, 2 * (1 - x) + 1 - y]


def empty_kernel(*refs):
    pass


def empty(shape, dtype, behind=()):
    return pl.pallas_call(
        empty_kernel,
        in_specs=[ANYWHERE] * len(behind),
        out_specs=ANYWHERE,
        out_shape=jax.ShapeDtypeStruct(shape, dtype),
        name="empty",
    )(*behind)


def lay_shards(place, shard, before, behind, low, high, ready):
    n, z = place.fsdp, place.z
    blocks, size, cols = shard.shape
    whole = empty((blocks, n * size, cols), shard.dtype, ready)
    for part, block, start in (
        (shard, 0, z),
        (before[:, :size], 0, (z + 3) % n),
        (behind[:, :size], 0, (z + 1) % n),
        (low[:, :size], 0, (z + 2) % n),
        (high, blocks // 2, (z + 2) % n),
    ):
        whole = lax.dynamic_update_slice(whole, part, (block, start * size, 0))
    return whole


class Shards:
    def __init__(self, place, grad, axis, half_axis, begin):
        self.place, self.grad, self.axis, self.half_axis = place, grad, axis, half_axis
        self.size = grad.shape[axis] // place.fsdp
        self.half = (self.size if axis == half_axis else grad.shape[half_axis]) // 2

        def pair(one, two):
            return after(jnp.stack([one, two]).astype(LOW), begin)

        self.left = place.shift(pair(self.part(2, 1), self.part(1, 0)), "z", 1)
        self.right = place.shift(pair(self.part(2, 0), self.part(3, 1)), "z", -1)

    def part(self, ahead, side):
        place, half = self.place, self.half
        start = (place.z + ahead) % place.fsdp * self.size
        shard = lax.dynamic_slice_in_dim(self.grad, start, self.size, self.axis)
        return lax.slice_in_dim(shard, side * half, (side + 1) * half, axis=self.half_axis).astype(F32)

    def follow(self, *ready):
        place = self.place
        self.left, self.right = after((self.left, self.right), *ready)
        high = (self.part(1, 1) + self.left[0].astype(F32)).astype(LOW)
        low = (self.part(3, 0) + self.right[0].astype(F32)).astype(LOW)
        self.high, self.low = place.shift(high, "z", 1), place.shift(low, "z", -1)
        return low

    def total(self, *ready):
        high, low = after((self.high, self.low), *ready) if ready else (self.high, self.low)
        low = self.part(0, 0) + self.left[1].astype(F32) + low.astype(F32)
        high = self.part(0, 1) + self.right[1].astype(F32) + high.astype(F32)
        return jnp.concatenate([low.astype(LOW), high.astype(LOW)], axis=self.half_axis)


def total_over(place, value, which):
    n = {"z": place.fsdp, "x": place.context, "y": place.pairs, "core": 2}[which]
    if n == 1:
        return value
    if which == "core":
        return value + place.swap(value)
    if n == 2:
        return value + place.shift(value, which, 1)
    at = {"z": place.z, "x": place.x, "y": place.y}[which]
    parts = jnp.zeros((n,) + value.shape, value.dtype)
    parts = lax.dynamic_update_index_in_dim(parts, value, at, 0)
    for step in range(1, n):
        sent = place.shift(value, which, step)
        parts = lax.dynamic_update_index_in_dim(parts, sent, (at - step) % n, 0)
    return jnp.sum(parts, axis=0)


def small_totals(place, sums, bias, bias_other):
    n, z = place.fsdp, place.z
    feat = sums.shape[1]
    pad = [(0, 1), (0, 0)]
    sent = place.swap(jnp.concatenate([sums, jnp.pad(bias_other, pad)], axis=1))
    sums, bias = sums + sent[:, :feat], jnp.pad(bias, pad) + sent[:, feat:]
    size = feat // n
    came = []
    for step in range(n):
        part = lax.dynamic_slice_in_dim(sums, (z + step) % n * size, size, 1)
        part = jnp.concatenate([part, bias], axis=1)
        came.append(place.shift(part, "z", step) if step else part)
    came = lax.optimization_barrier(tuple(came))
    parts = jnp.zeros((n,) + came[0].shape, F32)
    for step in range(n):
        parts = lax.dynamic_update_index_in_dim(parts, came[step], (z - step) % n, 0)
    return jnp.sum(parts, axis=0)


def last_totals(place, totals, size):
    if place.context == 2:
        sent = place.shift(totals, "x", 1)
        return totals[:, :size] + sent[:, :size], ordered(place.x, totals[:3, size:], sent[:3, size:], 1)
    return total_over(place, totals[:, :size], "x"), gather_stage(place, totals[:3, size:], 1, "x")


def local(
    hidden_in,
    norm_gains,
    norm_biases,
    qkv_weight,
    qkv_bias,
    out_weight,
    gate_up_weight,
    down_weight,
    cotangent,
):
    place = Place()
    all_seqs, part_rows, feat = hidden_in.shape
    seqs = all_seqs // 2
    length = part_rows * place.context
    own_rows = part_rows // place.pairs
    head_cols = qkv_bias.shape[1] // place.context
    hidden_cols = down_weight.shape[0] // place.context

    def columns(value, count, axis):
        return lax.dynamic_slice_in_dim(value, place.x * count, count, axis)

    def own_sequences(value):
        return lax.dynamic_slice_in_dim(value, place.core * seqs, seqs, 0)

    def own_piece(value):
        return lax.dynamic_slice_in_dim(value, place.y * own_rows, own_rows, 1)

    pack = jnp.concatenate(
        [columns(qkv_weight, head_cols, 2), columns(out_weight, head_cols, 0).T[None]]
    )
    norm_part = jnp.concatenate([norm_gains, norm_biases]).reshape(-1, head_cols)
    norm_rows = norm_part.shape[0]
    pad = -norm_rows % 16
    part_feat = pack.shape[1]
    norm_block = jnp.pad(norm_part, [(0, pad), (0, 0)])[None]
    extra = jnp.pad(norm_block, [(0, 3), (0, 0), (0, 0)])
    pack = jnp.concatenate([pack, extra], axis=1)
    pack_before, pack_behind = place.shift(pack, "z", 1), place.shift(pack, "z", -1)
    bias = columns(qkv_bias, head_cols, 1)
    bias_swapped = place.swap(bias)
    bias_other = bias_swapped.astype(F32)[None, :, None, :]
    bias = bias.astype(F32)[None, :, None, :]
    hidden_mine = own_sequences(hidden_in).reshape(-1, feat)
    top_mine = own_sequences(cotangent)
    if place.square(seqs):
        pieces = other_rows(place, hidden_mine)
        top_pieces = other_rows(place, top_mine.reshape(-1, feat))
        pack_before, pack_behind = after((pack_before, pack_behind), pieces[2], bias_swapped)
    else:
        whole = gather_stage(place, hidden_mine.reshape(seqs, -1, feat), 1, "x").reshape(-1, feat)
        pieces = top_pieces = [whole] * 4
    half = pack.shape[0] // 2
    pack_low = place.shift(pack_before[:half], "z", 1)
    pack_high = place.shift(pack_behind[half:, :part_feat], "z", -1)
    norms = jnp.zeros((2, 2, feat), F32)
    for step, piece in (
        (0, norm_block),
        (1, pack_before[:1, part_feat:]),
        (2, pack_low[:1, part_feat:]),
        (3, pack_behind[:1, part_feat:]),
    ):
        piece = piece[0, :norm_rows].reshape(2, 2, part_feat).astype(F32)
        norms = lax.dynamic_update_slice(norms, piece, (0, 0, (place.z - step) % place.fsdp * part_feat))
    gains, shifts = norms[0][:, None, :], norms[1][:, None, :]
    gate_up_part = columns(gate_up_weight, hidden_cols, 2).transpose(0, 2, 1)
    down_part = columns(down_weight, hidden_cols, 0)
    if place.square(seqs):
        normed = norm_first(other_places(place), pieces, gains[0], shifts[0])
        top_last = top_pieces[3]
    else:
        normed = (centre(whole.astype(F32))[0] * gains[0] + shifts[0]).astype(LOW)
        grad_top = top_last = gather_stage(place, top_mine, 1, "x").reshape(seqs * length, feat)
    w_attn = lay_shards(place, pack[:, :part_feat], pack_before, pack_behind, pack_low, after(pack_high, normed), [pieces[3], gate_up_part, down_part])
    gate_up_part, down_part = after((gate_up_part, down_part), pack_low, pack_high, top_pieces[2])
    w_gate_up = lax.all_gather(gate_up_part, "fsdp", axis=2, tiled=True)
    w_down = lax.all_gather(down_part, "fsdp", axis=1, tiled=True)
    tables = rotary_tables(length, min(head_cols, 128))
    w_attn_other = place.swap(w_attn)

    def attend(weight, bias, behind):
        mixed = jnp.einsum("rd,cde->cre", normed, weight[:3], preferred_element_type=F32)
        return attend_forward(mixed[None], bias, tables, seqs, length, behind)

    kept = attend(w_attn, bias, [])
    kept_other = attend(w_attn_other, bias_other, [kept[3], top_last])
    attended, attended_other = kept[3][0], kept_other[3][0]
    attn_sum = RowSum(
        place,
        "nt",
        [(attended, (), w_attn, (3,)), (attended_other, (), w_attn_other, (3,))],
        seqs,
        "out",
    ).start()
    if place.square(seqs):
        grad_top = lay_pieces(other_places(place), top_pieces, [attn_sum.sent])
    theirs_top, theirs_one, theirs_attended = place.swap(grad_top), place.swap(normed), place.swap(attended_other)
    attn_sum.follow([grad_top])
    inputs = own_piece(hidden_mine.reshape(seqs, -1, feat)).reshape(-1, feat)
    middle, normed_two = add_norm(
        attn_sum.shares, inputs, gains[1], shifts[1], behind=[theirs_attended]
    )
    normed_two = spread_rows(place, normed_two, seqs, [theirs_top, theirs_one])

    w_gate_up_other = place.swap(after(w_gate_up, middle))
    turned_other, slope_other, hidden_part = gate_up(normed_two, w_gate_up_other)
    theirs_turned, w_down_other = place.swap(turned_other), place.swap(after(w_down, turned_other))
    turned, slope, hidden = gate_up(normed_two, w_gate_up)
    grad_down = products(
        "nn",
        [(turned, (), grad_top, ()), (theirs_turned, (), theirs_top, ())],
        hidden_cols,
        512,
        "grad_down",
    )
    down_sum = lax.psum_scatter(grad_down, "fsdp", scatter_dimension=1, tiled=True)
    grad_gu_turned_other, grad_gu_other = hidden_back(grad_top, w_down_other, slope_other, [grad_down])
    theirs_gu, theirs_two = place.swap(grad_gu_turned_other), place.swap(normed_two)
    grad_gu_turned, grad_gu = hidden_back(grad_top, w_down, slope, [grad_gu_other])
    two_sum = RowSum(
        place,
        "nn",
        [(grad_gu, (c,), w_gate_up, (c,)) for c in range(2)]
        + [(grad_gu_other, (c,), w_gate_up_other, (c,)) for c in range(2)],
        seqs,
        "grad_two",
        behind=[theirs_two, theirs_gu],
    ).start()
    grad_gate_up = products(
        "nn",
        [(grad_gu_turned, (), normed_two, ()), (theirs_gu, (), theirs_two, ())],
        hidden_cols,
        512,
        "grad_gate_up",
        count=2,
        behind=[two_sum.sent],
    )
    two_next = two_sum.follow([grad_gate_up, down_sum])
    gate_up_sum = lax.psum_scatter(after(grad_gate_up, two_next), "fsdp", scatter_dimension=2, tiled=True)
    down_sums = RowSum(
        place,
        "nn",
        [(hidden, (), w_down, ()), (hidden_part, (), w_down_other, ())],
        seqs,
        "down",
        behind=[two_next],
    )
    top_rows = own_piece(top_mine).reshape(-1, feat)
    grad_middle, mid_low, sums_two = norm_back(
        two_sum.shares, middle, gains[1], top_rows, [F32, LOW], behind=[down_sums.sent]
    )
    grad_mid_low = spread_rows(place, mid_low, seqs)
    down_gathered = Gathered(place, after(down_sum, grad_mid_low), 0)
    down_sums.start(grad_mid_low)

    def attend_grad(kept, weight, behind):
        grad_att = products("nn", [(grad_mid_low, (), weight, (3,))], 1024, head_cols, "grad_att", behind=behind)
        return attend_back(*kept, grad_att[None], tables, seqs, length)[0]

    theirs_mid = place.swap(grad_mid_low)
    grad_mixed_other = attend_grad(kept_other, w_attn_other, [])
    theirs_mixed = place.swap(grad_mixed_other)
    grad_out = products(
        "tn",
        [(grad_mid_low, (), attended, ()), (theirs_mid, (), theirs_attended, ())],
        512,
        head_cols,
        "grad_out",
        behind=[grad_mixed_other],
    )
    down_next = down_sums.follow([grad_out])
    grad_mixed = attend_grad(kept, w_attn, [down_next])
    final_out = add_low(down_sums.shares, middle, behind=[grad_mixed])
    out_sum = lax.psum_scatter(grad_out, "fsdp", scatter_dimension=0, tiled=True)
    one_sum = RowSum(
        place,
        "nt",
        [(grad_mixed, (c,), w_attn, (c,)) for c in range(3)]
        + [(grad_mixed_other, (c,), w_attn_other, (c,)) for c in range(3)],
        seqs,
        "grad_one",
        behind=[final_out, down_gathered.raw],
    ).start()
    grad_qkv = qkv_back(
        normed, theirs_one, grad_mixed, theirs_mixed, behind=[one_sum.sent, gate_up_sum]
    )
    qkv_shards = Shards(place, grad_qkv, 1, 1, grad_mixed)
    one_next = one_sum.follow([grad_qkv])
    qkv_next = qkv_shards.follow(one_next)
    layer_rows = WholeRows(place, after(final_out, one_sum.shares[1], one_sum.shares[3]), seqs)
    input_low, sums_one = norm_back(
        one_sum.shares, inputs, gains[0], grad_middle, [LOW], behind=[one_next, qkv_next]
    )
    gate_up_out = lax.all_gather(gate_up_sum, "context", axis=1, tiled=True)
    gate_up_out = turn(gate_up_out)
    sums = after(jnp.concatenate([sums_one, sums_two]), layer_rows.over_y)
    sums = total_over(place, sums, "y")
    input_rows = WholeRows(place, after(input_low, sums), seqs)
    layer_out = layer_rows.whole(LOW)
    totals = small_totals(
        place,
        after(sums, qkv_shards.low, qkv_shards.high, gate_up_out, input_rows.over_y, layer_out),
        jnp.sum(grad_mixed.astype(F32), axis=1),
        jnp.sum(grad_mixed_other.astype(F32), axis=1),
    )
    qkv_sum = qkv_shards.total()
    qkv_gathered = Gathered(place, qkv_sum, 2)
    out_gathered = Gathered(place, after(out_sum, qkv_sum), 1)
    sums, grad_bias = last_totals(place, after(totals, qkv_sum), norm_gains.shape[1])
    input_grad = input_rows.whole(F32, [qkv_gathered.raw])

    return (
        layer_out,
        input_grad,
        sums[0::2],
        sums[1::2],
        qkv_gathered.whole().astype(F32),
        grad_bias,
        out_gathered.whole().T.astype(F32),
        gate_up_out,
        down_gathered.whole().astype(F32),
    )


def solution(mesh):
    placed = (
        P("fsdp", "context", None),
        P(None, "fsdp"),
        P(None, "fsdp"),
        P(None, "fsdp", "tensor"),
        P(None, "tensor"),
        P("tensor", "fsdp"),
        P(None, "fsdp", "tensor"),
        P("tensor", "fsdp"),
        P("fsdp", "context", None),
    )
    return jax.shard_map(
        local,
        mesh=mesh,
        in_specs=placed,
        out_specs=(
            P("fsdp", "context", None),
            P("fsdp", "context", None),
            P(None, "fsdp"),
            P(None, "fsdp"),
            P(None, "fsdp", "tensor"),
            P(None, "tensor"),
            P("tensor", "fsdp"),
            P(None, "fsdp", "tensor"),
            P("tensor", "fsdp"),
        ),
        check_vma=False,
    )
```
